32 devices in a mesh: groups: 2 (over y), tensor: 4 (over z), seq: 2 (over x), pipe: 2 (over core).
Axes of the slice: x: 2, y: 2, z: 4, core: 2. Of those that a mesh axis runs over, the one named last changes fastest.
Arguments:
- queries: bfloat16 [2048, 4096], P(('groups', 'seq', 'pipe'), 'tensor'), parts along dimension 0, may hold values from -20 to 20
- new_keys: bfloat16 [2048, 512], P(('groups', 'seq', 'pipe')), parts along dimension 0, may hold values from -6 to 6
- new_values: bfloat16 [2048, 512], P(('groups', 'seq', 'pipe')), parts along dimension 0, may hold values from -6 to 6
- key_cache: bfloat16 [4, 8192, 128], P(None, ('groups', 'seq', 'pipe')), parts along dimension 1, may hold values from -20 to 20
- value_cache: bfloat16 [4, 8192, 128], P(None, ('groups', 'seq', 'pipe')), parts along dimension 1, may hold values from -6 to 6
- prefix_len: int32 [8], P(('groups', 'seq', 'pipe')), parts along dimension 0, may hold values from 256 to 1024, as said below
- stretch_start: int32 [2], P('groups'), parts along dimension 0, may hold values from 4096 to 8191
- out_weight: bfloat16 [4096, 8192], P('tensor'), may hold values from -2 to 2
Outputs:
- out_values: bfloat16 [2048, 8192], P(('groups', 'seq', 'pipe'), 'tensor'), parts along dimension 0
- out_scales: float32 [2048, 64], P(('groups', 'seq', 'pipe'), 'tensor'), parts along dimension 0
The draws below stay inside these ranges and needn't reach their ends.
There are 2 independent parts, one for each index of `groups`. The reference program is written for one: setup_inputs(seed, part) draws one part's arguments, and reference() takes and returns one part's arrays. A program takes and returns all parts, laid end to end along the dimension named above; an argument that names none is the same for every part. Nothing has to cross between parts.
Inputs may be any that keep to these rules, and one draw needn't show every extreme that they name: `prefix_len`: each shard's count is at least 256; some shard is full in every draw.
All inputs are finite; a program needn't handle non-finite values. Where the reference program divides by a largest or mean magnitude, that divisor is 1e-20 or more.
Results may differ from the reference program's by a relative error of at most 0.029.
Values may be sent and summed in bfloat16 or wider, within the bound.
No kernel may reach another device: no remote copies, remote signals or barrier semaphores. Data moves between devices by JAX's collectives and lax.ppermute only.
A program may use at most 192 MiB of HBM per device.

```python
import math
import jax
import jax.numpy as jnp
from jax import lax

D = 8192
HD = 128
HQ = 32
KVH = 4
BLOCK = 128
CACHE = 1024
SHARDS = 4
STRETCH = 1024
PREFIX = 4096
N_TENSOR = 4


def draw_queries(key, part):
    key = jax.random.fold_in(key, 11)
    values = jnp.clip(jax.random.normal(key, (STRETCH, HQ * HD), jnp.float32), -6.0, 6.0)
    return values.astype(jnp.bfloat16)


def draw_key_cache(key, part):
    key = jax.random.fold_in(key, 23)
    values = jnp.clip(jax.random.normal(key, (KVH, PREFIX, HD), jnp.float32), -6.0, 6.0)
    return values.astype(jnp.bfloat16)


def draw_prefix_len(key, part):
    key = jax.random.fold_in(key, 37)
    length_key, full_key = jax.random.split(key)
    lengths = jax.random.randint(length_key, (SHARDS,), CACHE // 4, CACHE + 1)
    full_shard = jax.random.randint(full_key, (), 0, SHARDS)
    return jnp.where(jnp.arange(SHARDS) == full_shard, CACHE, lengths).astype(jnp.int32)


def raised(values, stream_key, source, target, blocks, factor):
    owner, partner = [(jnp.arange(values.shape[axis_at]) // (values.shape[axis_at] // blocks)).reshape([-1 if axis == axis_at else 1 for axis in range(values.ndim)]) for axis_at in (source, target)]
    chosen = jax.random.permutation(stream_key, blocks)[partner]
    strong = (owner == chosen) | (owner == (partner + blocks // 2) % blocks)
    return jnp.where(strong, factor * values, values)


def shard_levels(rng, dims, cuts, low, top_value):
    def one(axis_at, parts):
        steps = jax.random.uniform(jax.random.fold_in(jax.random.fold_in(rng, 6), axis_at), (parts,), jnp.float32, low / len(cuts), top_value / len(cuts))
        return jnp.repeat(jnp.exp(steps), dims[axis_at] // parts).reshape((-1,) + (1,) * (len(dims) - axis_at - 1))

    loudness = one(*cuts[0])
    for cut in cuts[1:]:
        loudness = loudness * one(*cut)
    return loudness


def scatter_about(key, dims, scale, most, cuts=(), kind=jnp.bfloat16):
    level = shard_levels(key, dims, cuts, -0.22, 0.18) if cuts else 1.0
    array = jax.random.normal(key, dims, jnp.float32) * scale * level
    return jnp.minimum(jnp.maximum(array, -most), most).astype(kind)


def bell_draw_with(stream_key, extent, spread, bound, cuts, heavy, held_as=jnp.bfloat16):
    drawn = spread * jax.random.normal(stream_key, extent, jnp.float32)
    if cuts:
        drawn = drawn * shard_levels(stream_key, extent, cuts, -0.22, 0.18)
    return jnp.clip(raised(drawn, jax.random.fold_in(stream_key, 3), *heavy), -bound, bound).astype(held_as)


def setup_inputs(seed: int = 0, part: int = 0) -> dict:
    key_list = jax.random.split(jax.random.key(seed), 9)
    part_keys = jax.random.split(jax.random.fold_in(key_list[8], part), 9)
    return {
        "queries": draw_queries(jax.random.fold_in(jax.random.fold_in(key_list[8], part), 71), part),
        "new_keys": scatter_about(part_keys[1], (STRETCH, KVH * HD), 1.0, 6.0, ((0, 4),)),
        "new_values": scatter_about(part_keys[2], (STRETCH, KVH * HD), 1.0, 6.0, ((0, 4),)),
        "key_cache": draw_key_cache(jax.random.fold_in(jax.random.fold_in(key_list[8], part), 71), part),
        "value_cache": scatter_about(part_keys[4], (KVH, PREFIX, HD), 1.0, 6.0, ((1, 4),)),
        "prefix_len": draw_prefix_len(jax.random.fold_in(jax.random.fold_in(key_list[8], part), 71), part),
        "stretch_start": jax.random.randint(part_keys[6], (1,), PREFIX, 2 * PREFIX).astype(jnp.int32),
        "out_weight": bell_draw_with(key_list[7], (HQ * HD, D), (HD // 8) ** -0.5, 2.0, ((0, 4),), (0, 1, 4, 2.0)),
    }


def rotate(values, positions):
    half = values.shape[-1] // 2
    freq = 500000.0 ** (-(jnp.arange(half, dtype=jnp.float32) * 2.0 / values.shape[-1]))
    angle = positions.astype(jnp.float32)[:, None] * freq[None, :]
    cosine = jnp.cos(angle)[:, None, :]
    sine = jnp.sin(angle)[:, None, :]
    first = values[..., :half]
    second = values[..., half:]
    return jnp.concatenate([first * cosine - second * sine, second * cosine + first * sine], axis=-1)

def reference(queries, new_keys, new_values, key_cache, value_cache, prefix_len, stretch_start, out_weight):
    row_count = queries.shape[0]
    positions = stretch_start[0] + jnp.arange(row_count, dtype=jnp.int32)
    rot_q = rotate(queries.reshape(row_count, HQ, HD).astype(jnp.float32), positions).astype(jnp.bfloat16)
    rot_k = rotate(new_keys.reshape(row_count, KVH, HD).astype(jnp.float32), positions).astype(jnp.bfloat16)
    fresh_values = new_values.reshape(row_count, KVH, HD)
    slot_index = jnp.arange(PREFIX, dtype=jnp.int32)
    cache_live = slot_index % CACHE < prefix_len[slot_index // CACHE]
    causal = jnp.arange(row_count)[None, :] <= jnp.arange(row_count)[:, None]
    factor = 1.0 / math.sqrt(HD)
    group = HQ // KVH

    def one_head(head):
        kv_head = head // group
        query = rot_q[:, head]
        cached = jnp.dot(query, key_cache[kv_head].T, preferred_element_type=jnp.float32) * factor
        recent = jnp.dot(query, rot_k[:, kv_head].T, preferred_element_type=jnp.float32) * factor
        cached = jnp.where(cache_live[None, :], cached, -1e+30)
        recent = jnp.where(causal, recent, -1e+30)
        peak = jnp.maximum(lax.optimization_barrier(jnp.max(cached, axis=1)), lax.optimization_barrier(jnp.max(recent, axis=1)))
        cached_w = jnp.where(cache_live[None, :], jnp.exp(cached - peak[:, None]), 0.0)
        recent_w = jnp.where(causal, jnp.exp(recent - peak[:, None]), 0.0)
        denominators = lax.optimization_barrier(jnp.sum(cached_w, axis=1)) + lax.optimization_barrier(jnp.sum(recent_w, axis=1))
        mixed = jnp.dot(cached_w.astype(jnp.bfloat16), value_cache[kv_head], preferred_element_type=jnp.float32)
        mixed = mixed + jnp.dot(recent_w.astype(jnp.bfloat16), fresh_values[:, kv_head], preferred_element_type=jnp.float32)
        return (mixed / denominators[:, None]).astype(jnp.bfloat16)
    heads_out = lax.map(one_head, jnp.arange(HQ, dtype=jnp.int32))
    attended = jnp.transpose(heads_out, (1, 0, 2)).reshape(row_count, HQ * HD)
    width = HQ * HD // N_TENSOR

    def add_term(total, index):
        columns = lax.dynamic_slice_in_dim(attended, index * width, width, 1)
        weights = lax.dynamic_slice_in_dim(out_weight, index * width, width, 0)
        partial_value = jnp.dot(columns, weights, preferred_element_type=jnp.float32)
        blocks = partial_value.reshape(row_count, D // BLOCK, BLOCK)
        scale = lax.optimization_barrier(jnp.max(jnp.abs(blocks), axis=2, keepdims=True)) + 1e-06
        coded = lax.optimization_barrier((blocks / scale).astype(jnp.bfloat16))
        return (total + coded.astype(jnp.float32) * scale, None)
    start_total = jnp.zeros((row_count, D // BLOCK, BLOCK), jnp.float32)
    total = lax.scan(add_term, start_total, jnp.arange(N_TENSOR, dtype=jnp.int32))[0]
    out_scales = lax.optimization_barrier(jnp.max(jnp.abs(total), axis=2)) + 1e-06
    out_values = (total / out_scales[:, :, None]).astype(jnp.bfloat16).reshape(row_count, D)
    return (out_values, out_scales)
```

```python
import functools
import math

import jax
import jax.numpy as jnp
from jax import lax
from jax.experimental import pallas as pl
from jax.experimental.pallas import tpu as pltpu
from jax.sharding import PartitionSpec as P

D = 8192
HD = 128
HQ = 32
KVH = 4
BLOCK = 128
LEN_ROWS = 16
LOW = 32
NEG = -1e30
VMEM_LIMIT = 48 * 1024 * 1024
F32 = jnp.float32
BF16 = jnp.bfloat16
NT = (((1,), (1,)), ((), ()))


def params(steps=1):
    return pltpu.CompilerParams(
        dimension_semantics=("arbitrary",) * steps, vmem_limit_bytes=VMEM_LIMIT
    )


def cost(flops, nbytes, transcendentals=0):
    return pl.CostEstimate(
        flops=int(flops), bytes_accessed=int(nbytes), transcendentals=int(transcendentals)
    )


def rotated(x, cosine, sine):
    return x * cosine + pltpu.roll(x, HD // 2, 1) * sine


def pack_first_kernel(info_ref, k_ref, v_ref, out_ref):
    half = k_ref.shape[1]
    out_ref[0, :half] = k_ref[0]
    out_ref[1, :half] = v_ref[0]
    live = info_ref[1]
    high = (live // LOW).astype(F32)
    low = (live % LOW).astype(F32)
    out_ref[0, half:] = jnp.full((LEN_ROWS, HD), high, F32).astype(BF16)
    out_ref[1, half:] = jnp.full((LEN_ROWS, HD), low, F32).astype(BF16)


def pack_first(info, key_cache, value_cache):
    half = key_cache.shape[1] // 2
    spec = pl.BlockSpec((1, half, HD), lambda i, info: (info[0], 0, 0))
    return pl.pallas_call(
        pack_first_kernel,
        out_shape=jax.ShapeDtypeStruct((2, half + LEN_ROWS, HD), BF16),
        grid_spec=pltpu.PrefetchScalarGridSpec(
            num_scalar_prefetch=1,
            grid=(1,),
            in_specs=[spec, spec],
            out_specs=pl.BlockSpec((2, half + LEN_ROWS, HD), lambda i, info: (0, 0, 0)),
        ),
        compiler_params=params(),
        cost_estimate=cost(0, 4 * half * HD * 2),
        name="pack_first",
    )(info, key_cache, value_cache)


def pack_second_kernel(info_ref, k_ref, v_ref, nk_ref, nv_ref, cos_ref, sin_ref, out_ref):
    half = k_ref.shape[1]
    out_ref[0, :half] = k_ref[0]
    out_ref[1, :half] = v_ref[0]
    out_ref[0, half:] = rotated(nk_ref[...].astype(F32), cos_ref[...], sin_ref[...]).astype(BF16)
    out_ref[1, half:] = nv_ref[...]


def pack_second(info, key_cache, value_cache, new_keys, new_values, cosine, sine):
    half = key_cache.shape[1] // 2
    rows = new_keys.shape[0]
    cache_spec = pl.BlockSpec((1, half, HD), lambda i, info: (info[0], 1, 0))
    new_spec = pl.BlockSpec((rows, HD), lambda i, info: (0, info[0]))
    table_spec = pl.BlockSpec((rows, HD), lambda i, info: (0, 0))
    return pl.pallas_call(
        pack_second_kernel,
        out_shape=jax.ShapeDtypeStruct((2, half + rows, HD), BF16),
        grid_spec=pltpu.PrefetchScalarGridSpec(
            num_scalar_prefetch=1,
            grid=(1,),
            in_specs=[cache_spec, cache_spec, new_spec, new_spec, table_spec, table_spec],
            out_specs=pl.BlockSpec((2, half + rows, HD), lambda i, info: (0, 0, 0)),
        ),
        compiler_params=params(),
        cost_estimate=cost(0, 4 * (half + rows) * HD * 2),
        name="pack_second",
    )(info, key_cache, value_cache, new_keys, new_values, cosine, sine)


def rope_kernel(q_ref, cos_ref, sin_ref, out_ref):
    factor = math.log2(math.e) / math.sqrt(HD)
    cosine = cos_ref[...] * factor
    sine = sin_ref[...] * factor
    for head in range(q_ref.shape[1] // HD):
        at = slice(head * HD, (head + 1) * HD)
        out_ref[:, at] = rotated(q_ref[:, at].astype(F32), cosine, sine).astype(BF16)


def rope_queries(queries, cosine, sine):
    return pl.pallas_call(
        rope_kernel,
        out_shape=jax.ShapeDtypeStruct(queries.shape, BF16),
        compiler_params=pltpu.CompilerParams(vmem_limit_bytes=VMEM_LIMIT),
        cost_estimate=cost(queries.size * 4, queries.size * 4),
        name="rope_queries",
    )(queries, cosine, sine)


def lane_max(x):
    parts = [x[:, i : i + HD] for i in range(0, x.shape[1], HD)]
    return functools.reduce(jnp.maximum, parts)


def lane_sum(x):
    parts = [x[:, i : i + HD] for i in range(0, x.shape[1], HD)]
    return functools.reduce(jnp.add, parts)


def attend_kernel(plan, lens, first, last, heads_per_step, n_kv, offs_ref, *refs):
    q_ref = refs[0]
    kv_refs = refs[1 : 1 + n_kv]
    refs = refs[1 + n_kv :]
    if not first:
        acc_in, top_in, sum_in = refs[:3]
        refs = refs[3:]
    rows = q_ref.shape[0]
    masks = []
    for array, begin, count, kind, argument in plan:
        if kind == "live":
            ref = kv_refs[lens[array]]
            at = ref.shape[1] - LEN_ROWS
            live = ref[0, at : at + 8, :].astype(F32) * LOW + ref[1, at : at + 8, :].astype(F32)
            live = live[:1, :]
            slot = lax.broadcasted_iota(jnp.int32, (1, HD), 1).astype(F32)
            pieces = [
                jnp.where(slot + float(argument + i) < live, 0.0, NEG)
                for i in range(0, count, HD)
            ]
            masks.append(jnp.concatenate(pieces, axis=1))
        else:
            row = lax.broadcasted_iota(jnp.int32, (rows, count), 0)
            column = lax.broadcasted_iota(jnp.int32, (rows, count), 1)
            masks.append(jnp.where(column <= row + offs_ref[argument], 0.0, NEG))
    for head in range(heads_per_step):
        at = slice(head * HD, (head + 1) * HD)
        query = q_ref[:, at]
        scores = []
        for (array, begin, count, kind, argument), mask in zip(plan, masks):
            keys = kv_refs[array][0, begin : begin + count, :]
            scores.append(lax.dot_general(query, keys, NT, preferred_element_type=F32) + mask)
        peak = functools.reduce(jnp.maximum, [lane_max(x) for x in scores])
        peak = jnp.max(peak, axis=1, keepdims=True)
        if not first:
            before = top_in[:, at]
            peak = jnp.maximum(before, peak)
            shrink = jnp.exp2(before - peak)
        else:
            peak = jnp.broadcast_to(peak, (rows, HD))
        total = None
        out = None
        for (array, begin, count, kind, argument), score in zip(plan, scores):
            weights = jnp.exp2(score - peak[:, :1])
            part = lane_sum(weights)
            total = part if total is None else total + part
            values = kv_refs[array][1, begin : begin + count, :]
            update = jnp.dot(weights.astype(BF16), values, preferred_element_type=F32)
            out = update if out is None else out + update
        if not first:
            total = total + sum_in[:, at] * shrink
            out = out + acc_in[:, at] * shrink
        if last:
            denominator = jnp.sum(total, axis=1, keepdims=True)
            refs[0][:, at] = (out / denominator).astype(BF16)
        else:
            refs[0][:, at] = out
            refs[1][:, at] = peak
            refs[2][:, at] = total


def attend(name, query, arrays, plan, lens, offs, state, last, heads_per_step=2):
    rows, width = query.shape
    heads_per_step = min(heads_per_step, width // HD)
    first = state is None
    block = pl.BlockSpec((rows, heads_per_step * HD), lambda i, offs: (0, i))
    in_specs = [block]
    for array in arrays:
        in_specs.append(pl.BlockSpec(array.shape, lambda i, offs: (0, 0, 0)))
    state = () if first else state
    in_specs += [block] * len(state)
    if last:
        out_shape = jax.ShapeDtypeStruct((rows, width), BF16)
        out_specs = block
    else:
        out_shape = (jax.ShapeDtypeStruct((rows, width), F32),) * 3
        out_specs = (block,) * 3
    keys = sum(p[2] for p in plan)
    return pl.pallas_call(
        functools.partial(
            attend_kernel, plan, lens, first, last, heads_per_step, len(arrays)
        ),
        out_shape=out_shape,
        grid_spec=pltpu.PrefetchScalarGridSpec(
            num_scalar_prefetch=1,
            grid=(width // (heads_per_step * HD),),
            in_specs=in_specs,
            out_specs=out_specs,
        ),
        compiler_params=params(),
        cost_estimate=cost(
            8 * rows * width * keys, rows * width * 14 + keys * HD * 4, rows * (width // HD) * keys
        ),
        name=name,
    )(offs, query, *arrays, *state)


def project_kernel(order_ref, x_ref, w_ref, out_ref):
    out_ref[0] = jnp.dot(x_ref[...], w_ref[...], preferred_element_type=F32).astype(BF16)


def project(name, order, begin, count, attended, out_weight, chunk, tile=1024):
    rows, depth = attended.shape
    tile = min(tile, chunk)
    per = chunk // tile
    return pl.pallas_call(
        project_kernel,
        out_shape=jax.ShapeDtypeStruct((count, rows, chunk), BF16),
        grid_spec=pltpu.PrefetchScalarGridSpec(
            num_scalar_prefetch=1,
            grid=(count, per),
            in_specs=[
                pl.BlockSpec((rows, depth), lambda i, j, order: (0, 0)),
                pl.BlockSpec((depth, tile), lambda i, j, order: (0, order[begin + i] * per + j)),
            ],
            out_specs=pl.BlockSpec((1, rows, tile), lambda i, j, order: (i, 0, j)),
        ),
        compiler_params=params(2),
        cost_estimate=cost(2 * rows * depth * chunk * count, depth * chunk * count * 2),
        name=name,
    )(order, attended, out_weight)


def finish_kernel(parts, out_ref, scale_ref):
    rows, columns = out_ref.shape
    blocks = columns // BLOCK
    lane = lax.broadcasted_iota(jnp.int32, (rows, blocks), 1)
    scales = jnp.zeros((rows, blocks), F32)
    for block in range(blocks):
        at = slice(block * BLOCK, (block + 1) * BLOCK)
        total = functools.reduce(jnp.add, [part[:, at].astype(F32) for part in parts])
        scale = jnp.max(jnp.abs(total), axis=1, keepdims=True) + 1e-06
        out_ref[:, at] = (total / scale).astype(BF16)
        scales = jnp.where(lane == block, scale, scales)
    scale_ref[...] = scales


def finish(parts, tile=64):
    rows, columns = parts[0].shape
    tile = min(tile, rows)
    spec = pl.BlockSpec((tile, columns), lambda i: (i, 0))

    def kernel(*refs):
        finish_kernel(refs[: len(parts)], refs[-2], refs[-1])

    return pl.pallas_call(
        kernel,
        out_shape=(
            jax.ShapeDtypeStruct((rows, columns), BF16),
            jax.ShapeDtypeStruct((rows, columns // BLOCK), F32),
        ),
        grid=(rows // tile,),
        in_specs=[spec] * len(parts),
        out_specs=(spec, pl.BlockSpec((tile, columns // BLOCK), lambda i: (i, 0))),
        compiler_params=params(),
        cost_estimate=cost(rows * columns * 6, rows * columns * 2 * (len(parts) + 1)),
        name="finish",
    )(*parts)


def after(value, *others):
    return lax.optimization_barrier((value, *others))[0]


def added(a, b):
    return (a.astype(F32) + b.astype(F32)).astype(BF16)


def local(
    queries, new_keys, new_values, key_cache, value_cache, prefix_len, stretch_start, out_weight
):
    rows = queries.shape[0]
    heads_here = queries.shape[1] // HD
    group = HQ // KVH
    tensor_pos = lax.axis_index("tensor")
    lanes = lax.axis_size("tensor")
    n_seq, n_pipe = lax.axis_size("seq"), lax.axis_size("pipe")
    shards = n_seq * n_pipe
    assert heads_here <= group
    half = key_cache.shape[1] // 2
    kv_head = tensor_pos * heads_here // group
    me = lax.axis_index("seq") * n_pipe + lax.axis_index("pipe")
    info = jnp.stack([kv_head.astype(jnp.int32), prefix_len[0]])

    positions = stretch_start[0] + me * rows + jnp.arange(rows, dtype=jnp.int32)
    lane = jnp.arange(HD)
    freq = 500000.0 ** (-((lane % (HD // 2)).astype(F32) * 2.0 / HD))
    angle = positions.astype(F32)[:, None] * freq[None, :]
    cosine = jnp.cos(angle)
    sine = jnp.sin(angle) * jnp.where(lane < HD // 2, -1.0, 1.0)[None, :]

    own_a = pack_first(info, key_cache, value_cache)
    own_b = pack_second(info, key_cache, value_cache, new_keys, new_values, cosine, sine)
    query = rope_queries(queries, cosine, sine)

    def whole_plan(a, b, off):
        return [
            (a, 0, half, "live", 0),
            (b, 0, half, "live", half),
            (b, half, rows, "rows", off),
        ]

    if n_seq == 2 and n_pipe == 2:
        swap = [(0, 1), (1, 0)]
        far_a = lax.ppermute(own_a, "seq", swap)
        near_a = lax.ppermute(own_a, "pipe", swap)
        far_b = lax.ppermute(own_b, "seq", swap)
        near_b = lax.ppermute(own_b, "pipe", swap)
        cross_a = lax.ppermute(far_a, "pipe", swap)
        cross_b = lax.ppermute(far_b, "pipe", swap)
        offs = (me - jnp.stack([me, me ^ 1, me ^ 2, me ^ 3])).astype(jnp.int32) * rows
        state = attend(
            "attend_own", query, [own_a, own_b], whole_plan(0, 1, 0), {0: 0, 1: 0}, offs, None, False
        )
        state = attend(
            "attend_near", query, [near_a, near_b], whole_plan(0, 1, 1), {0: 0, 1: 0}, offs, state, False
        )
        state = attend(
            "attend_far_a",
            query,
            [far_a, cross_a],
            [(0, 0, half, "live", 0), (1, 0, half, "live", 0)],
            {0: 0, 1: 1},
            offs,
            state,
            False,
        )
        tail_a, tail_c = far_a[:, half:], cross_a[:, half:]
        attended = attend(
            "attend_far_b",
            query,
            [far_b, cross_b, tail_a, tail_c],
            [
                (0, 0, half, "live", half),
                (0, half, rows, "rows", 2),
                (1, 0, half, "live", half),
                (1, half, rows, "rows", 3),
            ],
            {0: 2, 1: 3},
            offs,
            state,
            True,
        )
    else:
        all_a = lax.all_gather(own_a, ("seq", "pipe"), axis=0)
        all_b = lax.all_gather(own_b, ("seq", "pipe"), axis=0)
        offs = (me - jnp.arange(shards)).astype(jnp.int32) * rows
        state = None
        for shard in range(shards):
            state = attend(
                "attend",
                query,
                [all_a[shard], all_b[shard]],
                whole_plan(0, 1, shard),
                {0: 0, 1: 0},
                offs,
                state,
                shard == shards - 1,
            )
        attended = state

    columns = D // lanes
    if lanes == 4:
        step = jnp.arange(4, dtype=jnp.int32)
        order = jnp.where(tensor_pos < 2, 3 - step, step)
        inward = [(0, 1), (3, 2)]
        middle = [(1, 2), (2, 1)]
        outward = [(1, 0), (2, 3)]
        p0 = project("project_0", order, 0, 1, attended, out_weight, columns)[0]
        rest = project("project_rest", order, 1, 3, attended, out_weight, columns)
        p1, p2, p3 = rest[0], rest[1], rest[2]
        cut = rows // 2
        halves = [slice(0, cut), slice(cut, rows)]
        e1 = [lax.ppermute(p0[h], "tensor", inward) for h in halves]
        e2, o1, e3, o2, f = [], [], [], [], []
        for i, h in enumerate(halves):
            e2.append(lax.ppermute(after(p1[h], e1[i]), "tensor", inward))
            o1.append(lax.ppermute(added(p0[h], e1[i]), "tensor", middle))
        for i, h in enumerate(halves):
            e3.append(lax.ppermute(after(p2[h], e2[i]), "tensor", inward))
            o2.append(lax.ppermute(added(p1[h], e2[i]), "tensor", middle))
            f.append(lax.ppermute(added(p3[h], o1[i]), "tensor", outward))
        outer = (tensor_pos == 0) | (tensor_pos == 3)
        values, scales = [], []
        for i, h in enumerate(halves):
            zero = jnp.zeros_like(e3[i])
            parts = [
                jnp.where(outer, p3[h], p2[h]),
                jnp.where(outer, f[i], e3[i]),
                jnp.where(outer, zero, o2[i]),
            ]
            v, s = finish(parts)
            values.append(v)
            scales.append(s)
        return jnp.concatenate(values, axis=0), jnp.concatenate(scales, axis=0)
    order = jnp.arange(lanes, dtype=jnp.int32)
    partial = project("project_all", order, 0, lanes, attended, out_weight, columns)
    total = lax.psum_scatter(partial, "tensor", scatter_dimension=0, tiled=True)[0]
    return tuple(finish([total]))


def solution(mesh):
    return jax.shard_map(
        local,
        mesh=mesh,
        in_specs=(
            P(("groups", "seq", "pipe"), "tensor"),
            P(("groups", "seq", "pipe"), None),
            P(("groups", "seq", "pipe"), None),
            P(None, ("groups", "seq", "pipe"), None),
            P(None, ("groups", "seq", "pipe"), None),
            P(("groups", "seq", "pipe")),
            P("groups"),
            P("tensor", None),
        ),
        out_specs=(P(("groups", "seq", "pipe"), "tensor"), P(("groups", "seq", "pipe"), "tensor")),
        check_vma=False,
    )
```

```python
import functools
import math

import jax
import jax.numpy as jnp
from jax import lax
from jax.experimental import pallas as pl
from jax.experimental.pallas import tpu as pltpu
from jax.sharding import PartitionSpec as P

D = 8192
HD = 128
HQ = 32
KVH = 4
BLOCK = 128
LEN_ROWS = 16
LOW = 32
NEG = -1e30
VMEM_LIMIT = 24 * 1024 * 1024
F32 = jnp.float32
BF16 = jnp.bfloat16
NT = (((1,), (1,)), ((), ()))


SMEM = pl.BlockSpec(memory_space=pltpu.SMEM)
VMEM = pl.BlockSpec(memory_space=pltpu.VMEM)
HBM = pl.BlockSpec(memory_space=pltpu.HBM)
PARAMS = pltpu.CompilerParams(vmem_limit_bytes=VMEM_LIMIT)


def cost(flops, nbytes, transcendentals=0):
    return pl.CostEstimate(
        flops=int(flops), bytes_accessed=int(nbytes), transcendentals=int(transcendentals)
    )


def rotated(x, cosine, sine):
    return x * cosine + pltpu.roll(x, HD // 2, 1) * sine


def pack_first_kernel(info_ref, k_ref, v_ref, out_ref, sems):
    count = out_ref.shape[1] - LEN_ROWS
    head = info_ref[0]
    copies = [
        pltpu.make_async_copy(
            ref.at[head, pl.ds(0, count)], out_ref.at[at, pl.ds(0, count)], sems.at[at]
        )
        for at, ref in enumerate((k_ref, v_ref))
    ]
    for copy in copies:
        copy.start()
    live = info_ref[1]
    high = (live // LOW).astype(F32)
    low = (live % LOW).astype(F32)
    out_ref[0, count:] = jnp.full((LEN_ROWS, HD), high, F32).astype(BF16)
    out_ref[1, count:] = jnp.full((LEN_ROWS, HD), low, F32).astype(BF16)
    for copy in copies:
        copy.wait()


def pack_first(info, key_cache, value_cache, count):
    return pl.pallas_call(
        pack_first_kernel,
        out_shape=jax.ShapeDtypeStruct((2, count + LEN_ROWS, HD), BF16),
        in_specs=[SMEM, HBM, HBM],
        out_specs=VMEM,
        scratch_shapes=[pltpu.SemaphoreType.DMA((2,))],
        compiler_params=PARAMS,
        cost_estimate=cost(0, 4 * count * HD * 2),
        name="pack_first",
    )(info, key_cache, value_cache)


def pack_second_kernel(
    first, info_ref, k_ref, v_ref, nk_ref, nv_ref, cos_ref, sin_ref, out_ref, raw, sems
):
    rows = raw.shape[0]
    count = out_ref.shape[1] - rows
    head = info_ref[0]
    columns = pl.ds(pl.multiple_of(head * HD, HD), HD)
    copies = [
        pltpu.make_async_copy(nk_ref.at[:, columns], raw, sems.at[0]),
        pltpu.make_async_copy(nv_ref.at[:, columns], out_ref.at[1, pl.ds(count, rows)], sems.at[1]),
        pltpu.make_async_copy(
            k_ref.at[head, pl.ds(first, count)], out_ref.at[0, pl.ds(0, count)], sems.at[2]
        ),
        pltpu.make_async_copy(
            v_ref.at[head, pl.ds(first, count)], out_ref.at[1, pl.ds(0, count)], sems.at[3]
        ),
    ]
    for copy in copies:
        copy.start()
    copies[0].wait()
    out_ref[0, count:] = rotated(raw[...].astype(F32), cos_ref[...], sin_ref[...]).astype(BF16)
    for copy in copies[1:]:
        copy.wait()


def pack_second(info, key_cache, value_cache, new_keys, new_values, cosine, sine, first):
    rows = new_keys.shape[0]
    size = key_cache.shape[1] - first + rows
    return pl.pallas_call(
        functools.partial(pack_second_kernel, first),
        out_shape=jax.ShapeDtypeStruct((2, size, HD), BF16),
        in_specs=[SMEM, HBM, HBM, HBM, HBM, VMEM, VMEM],
        out_specs=VMEM,
        scratch_shapes=[pltpu.VMEM((rows, HD), BF16), pltpu.SemaphoreType.DMA((4,))],
        compiler_params=PARAMS,
        cost_estimate=cost(0, 4 * size * HD * 2),
        name="pack_second",
    )(info, key_cache, value_cache, new_keys, new_values, cosine, sine)


def rope_kernel(q_ref, cos_ref, sin_ref, out_ref):
    factor = math.log2(math.e) / math.sqrt(HD)
    cosine = cos_ref[...] * factor
    sine = sin_ref[...] * factor
    for head in range(q_ref.shape[1] // HD):
        at = slice(head * HD, (head + 1) * HD)
        out_ref[:, at] = rotated(q_ref[:, at].astype(F32), cosine, sine).astype(BF16)


def rope_queries(queries, cosine, sine):
    return pl.pallas_call(
        rope_kernel,
        out_shape=jax.ShapeDtypeStruct(queries.shape, BF16),
        compiler_params=PARAMS,
        cost_estimate=cost(queries.size * 4, queries.size * 4),
        name="rope_queries",
    )(queries, cosine, sine)


def lane_max(x):
    parts = [x[:, i : i + HD] for i in range(0, x.shape[1], HD)]
    return functools.reduce(jnp.maximum, parts)


def lane_sum(x):
    parts = [x[:, i : i + HD] for i in range(0, x.shape[1], HD)]
    return functools.reduce(jnp.add, parts)


def attend_kernel(plan, lens, first, last, n_kv, offs_ref, q_ref, *refs):
    kv_refs = refs[:n_kv]
    refs = refs[n_kv:]
    if not first:
        acc_in, stats_in = refs[:2]
        refs = refs[2:]
    rows = q_ref.shape[0]
    heads = q_ref.shape[1] // HD
    masks = []
    for array, begin, count, kind, argument in plan:
        if kind == "live":
            ref = kv_refs[lens[array]]
            at = ref.shape[1] - LEN_ROWS
            live = ref[0, at:, :].astype(F32) * LOW + ref[1, at:, :].astype(F32)
            live = live[:1, :]
            slot = lax.broadcasted_iota(jnp.int32, (1, HD), 1).astype(F32)
            pieces = [
                jnp.where(slot + float(argument + i) < live, 0.0, NEG)
                for i in range(0, count, HD)
            ]
            masks.append(jnp.concatenate(pieces, axis=1))
        else:
            row = lax.broadcasted_iota(jnp.int32, (rows, count), 0)
            column = lax.broadcasted_iota(jnp.int32, (rows, count), 1)
            masks.append(jnp.where(column <= row + offs_ref[argument], 0.0, NEG))

    def score(head):
        query = q_ref[:, head * HD : (head + 1) * HD]
        scores = []
        for (array, begin, count, kind, argument), mask in zip(plan, masks):
            keys = kv_refs[array][0, begin : begin + count, :]
            scores.append(lax.dot_general(query, keys, NT, preferred_element_type=F32) + mask)
        return scores

    lane = lax.broadcasted_iota(jnp.int32, (rows, HD), 1)
    stats = jnp.zeros((rows, HD), F32)
    following = score(0)
    for head in range(heads):
        scores = following
        if head + 1 < heads:
            following = score(head + 1)
        at = slice(head * HD, (head + 1) * HD)
        peak = functools.reduce(jnp.maximum, [lane_max(x) for x in scores])
        peak = jnp.max(peak, axis=1, keepdims=True)
        if not first:
            before = stats_in[:, head : head + 1]
            peak = jnp.maximum(before, peak)
            shrink = jnp.exp2(before - peak)
        total = None
        out = None
        for (array, begin, count, kind, argument), part in zip(plan, scores):
            weights = jnp.exp2(part - peak)
            subtotal = lane_sum(weights)
            total = subtotal if total is None else total + subtotal
            values = kv_refs[array][1, begin : begin + count, :]
            update = jnp.dot(weights.astype(BF16), values, preferred_element_type=F32)
            out = update if out is None else out + update
        total = jnp.sum(total, axis=1, keepdims=True)
        if not first:
            total = total + stats_in[:, HD // 2 + head : HD // 2 + head + 1] * shrink
            out = out + acc_in[:, at] * shrink
        if last:
            refs[0][:, at] = (out / total).astype(BF16)
        else:
            refs[0][:, at] = out
            stats = jnp.where(lane == head, peak, stats)
            stats = jnp.where(lane == HD // 2 + head, total, stats)
    if not last:
        refs[1][...] = stats


def attend(name, query, arrays, plan, lens, offs, state, last):
    rows, width = query.shape
    first = state is None
    state = () if first else state
    if last:
        out_shape = jax.ShapeDtypeStruct((rows, width), BF16)
        out_specs = VMEM
    else:
        out_shape = (
            jax.ShapeDtypeStruct((rows, width), F32),
            jax.ShapeDtypeStruct((rows, HD), F32),
        )
        out_specs = (VMEM, VMEM)
    keys = sum(p[2] for p in plan)
    return pl.pallas_call(
        functools.partial(attend_kernel, plan, lens, first, last, len(arrays)),
        out_shape=out_shape,
        in_specs=[SMEM] + [VMEM] * (1 + len(arrays) + len(state)),
        out_specs=out_specs,
        compiler_params=PARAMS,
        cost_estimate=cost(
            8 * rows * width * keys, rows * width * 8 + keys * HD * 4, rows * (width // HD) * keys
        ),
        name=name,
    )(offs, query, *arrays, *state)


def project_kernel(order_ref, x_ref, w_ref, *out_refs):
    out = jnp.dot(x_ref[...], w_ref[...], preferred_element_type=F32).astype(BF16)
    rows = out_refs[0].shape[0]
    for i, ref in enumerate(out_refs):
        ref[...] = out[i * rows : (i + 1) * rows]


def project(name, order, at, attended, out_weight, chunk, halves, tile=512):
    rows, depth = attended.shape
    tile = min(tile, chunk)
    per = chunk // tile
    cut = rows // halves
    return pl.pallas_call(
        project_kernel,
        out_shape=(jax.ShapeDtypeStruct((cut, chunk), BF16),) * halves,
        grid_spec=pltpu.PrefetchScalarGridSpec(
            num_scalar_prefetch=1,
            grid=(per,),
            in_specs=[
                pl.BlockSpec((rows, depth), lambda j, order: (0, 0)),
                pl.BlockSpec((depth, tile), lambda j, order: (0, order[at] * per + j)),
            ],
            out_specs=(pl.BlockSpec((cut, tile), lambda j, order: (0, j)),) * halves,
        ),
        compiler_params=PARAMS,
        cost_estimate=cost(2 * rows * depth * chunk, depth * chunk * 2),
        name=name,
    )(order, attended, out_weight)


def add_kernel(a_ref, b_ref, out_ref):
    out_ref[...] = (a_ref[...].astype(F32) + b_ref[...].astype(F32)).astype(BF16)


def added(name, a, b):
    return pl.pallas_call(
        add_kernel,
        out_shape=jax.ShapeDtypeStruct(a.shape, BF16),
        in_specs=[VMEM, VMEM],
        out_specs=VMEM,
        compiler_params=PARAMS,
        cost_estimate=cost(a.size, a.size * 6),
        name=name,
    )(a, b)


def finish(name, flag, either, parts, begin, rows_all, into=None):
    rows, columns = parts[0].shape
    blocks = columns // BLOCK
    n_either, n_parts = len(either), len(parts)

    def kernel(flag_ref, *refs):
        out_ref, scale_ref = refs[-2:]
        chosen = flag_ref[0] == 1
        lane = lax.broadcasted_iota(jnp.int32, (rows, blocks), 1)
        scales = jnp.zeros((rows, blocks), F32)
        for block in range(blocks):
            at = slice(block * BLOCK, (block + 1) * BLOCK)
            terms = [ref[:, at].astype(F32) for ref in refs[: n_either + n_parts]]
            if n_either:
                terms = [jnp.where(chosen, terms[0], terms[1])] + terms[2:]
            total = functools.reduce(jnp.add, terms)
            scale = jnp.max(jnp.abs(total), axis=1, keepdims=True) + 1e-06
            out_ref[:, at] = (total / scale).astype(BF16)
            scales = jnp.where(lane == block, scale, scales)
        scale_ref[...] = scales

    whole = pl.BlockSpec((rows, columns), lambda i: (0, 0))
    into = () if into is None else into
    n = n_either + n_parts
    return pl.pallas_call(
        kernel,
        out_shape=(
            jax.ShapeDtypeStruct((rows_all, columns), BF16),
            jax.ShapeDtypeStruct((rows_all, blocks), F32),
        ),
        grid=(1,),
        in_specs=[SMEM] + [whole] * n + [pl.BlockSpec(memory_space=pl.ANY)] * len(into),
        out_specs=(
            pl.BlockSpec((rows, columns), lambda i: (begin // rows, 0)),
            pl.BlockSpec((rows, blocks), lambda i: (begin // rows, 0)),
        ),
        input_output_aliases={n + 1: 0, n + 2: 1} if into else {},
        compiler_params=PARAMS,
        cost_estimate=cost(rows * columns * 6, rows * columns * 2 * (n + 1)),
        name=name,
    )(flag, *either, *parts, *into)


def local(
    queries, new_keys, new_values, key_cache, value_cache, prefix_len, stretch_start, out_weight
):
    rows = queries.shape[0]
    heads_here = queries.shape[1] // HD
    group = HQ // KVH
    tensor_pos = lax.axis_index("tensor")
    lanes = lax.axis_size("tensor")
    n_seq, n_pipe = lax.axis_size("seq"), lax.axis_size("pipe")
    shards = n_seq * n_pipe
    assert heads_here <= group
    slots = key_cache.shape[1]
    split = slots * 3 // 4
    kv_head = tensor_pos * heads_here // group
    me = lax.axis_index("seq") * n_pipe + lax.axis_index("pipe")
    info = jnp.stack([kv_head.astype(jnp.int32), prefix_len[0]])

    positions = stretch_start[0] + me * rows + jnp.arange(rows, dtype=jnp.int32)
    lane = jnp.arange(HD)
    freq = 500000.0 ** (-((lane % (HD // 2)).astype(F32) * 2.0 / HD))
    angle = positions.astype(F32)[:, None] * freq[None, :]
    cosine = jnp.cos(angle)
    sine = jnp.sin(angle) * jnp.where(lane < HD // 2, -1.0, 1.0)[None, :]

    own_a = pack_first(info, key_cache, value_cache, split)
    own_b = pack_second(info, key_cache, value_cache, new_keys, new_values, cosine, sine, split)
    query = rope_queries(queries, cosine, sine)

    def whole_plan(off):
        return [
            (0, 0, split, "live", 0),
            (1, 0, slots - split, "live", split),
            (1, slots - split, rows, "rows", off),
        ]

    lens = {0: 0, 1: 0}
    if n_seq == 2 and n_pipe == 2:
        swap = [(0, 1), (1, 0)]
        far_a = lax.ppermute(own_a, "seq", swap)
        near_a = lax.ppermute(own_a, "pipe", swap)
        far_b = lax.ppermute(own_b, "seq", swap)
        near_b = lax.ppermute(own_b, "pipe", swap)
        cross_a = lax.ppermute(far_a, "pipe", swap)
        cross_b = lax.ppermute(far_b, "pipe", swap)
        offs = (me - jnp.stack([me, me ^ 1, me ^ 2, me ^ 3])).astype(jnp.int32) * rows
        state = attend("attend_own", query, [own_a, own_b], whole_plan(0), lens, offs, None, False)
        state = attend(
            "attend_near", query, [near_a, near_b], whole_plan(1), lens, offs, state, False
        )
        state = attend(
            "attend_far_a",
            query,
            [far_a, cross_a],
            [(0, 0, split, "live", 0), (1, 0, split, "live", 0)],
            {0: 0, 1: 1},
            offs,
            state,
            False,
        )
        attended = attend(
            "attend_far_b",
            query,
            [far_b, cross_b, far_a[:, split:], cross_a[:, split:]],
            [
                (0, 0, slots - split, "live", split),
                (0, slots - split, rows, "rows", 2),
                (1, 0, slots - split, "live", split),
                (1, slots - split, rows, "rows", 3),
            ],
            {0: 2, 1: 3},
            offs,
            state,
            True,
        )
    else:
        all_a = lax.all_gather(own_a, ("seq", "pipe"), axis=0)
        all_b = lax.all_gather(own_b, ("seq", "pipe"), axis=0)
        offs = (me - jnp.arange(shards)).astype(jnp.int32) * rows
        state = None
        for shard in range(shards):
            arrays = [all_a[shard], all_b[shard]]
            state = attend(
                "attend", query, arrays, whole_plan(shard), lens, offs, state, shard == shards - 1
            )
        attended = state

    columns = D // lanes
    flag = ((tensor_pos == 0) | (tensor_pos == lanes - 1)).astype(jnp.int32).reshape(1)
    if lanes == 4:
        step = jnp.arange(4, dtype=jnp.int32)
        order = jnp.where(tensor_pos < 2, 3 - step, step)
        inward = [(0, 1), (3, 2)]
        middle = [(1, 2), (2, 1)]
        outward = [(1, 0), (2, 3)]
        part = [project(f"project_{k}", order, k, attended, out_weight, columns, 2) for k in range(4)]
        come = [[lax.ppermute(p, "tensor", inward) for p in part[k]] for k in range(3)]
        done = None
        for i in range(2):
            across = lax.ppermute(added(f"add_0{i}", part[0][i], come[0][i]), "tensor", middle)
            second = lax.ppermute(added(f"add_1{i}", part[1][i], come[1][i]), "tensor", middle)
            back = lax.ppermute(added(f"add_3{i}", part[3][i], across), "tensor", outward)
            done = finish(
                f"finish_{i}",
                flag,
                [part[3][i], part[2][i]],
                [come[2][i], second, back],
                i * (rows // 2),
                rows,
                done,
            )
        return tuple(done)
    order = jnp.arange(lanes, dtype=jnp.int32)
    partial = [
        project(f"project_{k}", order, k, attended, out_weight, columns, 1)[0] for k in range(lanes)
    ]
    total = lax.psum_scatter(jnp.stack(partial), "tensor", scatter_dimension=0, tiled=True)[0]
    return tuple(finish("finish", flag, [], [total], 0, rows))


def solution(mesh):
    return jax.shard_map(
        local,
        mesh=mesh,
        in_specs=(
            P(("groups", "seq", "pipe"), "tensor"),
            P(("groups", "seq", "pipe"), None),
            P(("groups", "seq", "pipe"), None),
            P(None, ("groups", "seq", "pipe"), None),
            P(None, ("groups", "seq", "pipe"), None),
            P(("groups", "seq", "pipe")),
            P("groups"),
            P("tensor", None),
        ),
        out_specs=(P(("groups", "seq", "pipe"), "tensor"), P(("groups", "seq", "pipe"), "tensor")),
        check_vma=False,
    )
```

```python
import functools
import math

import jax
import jax.numpy as jnp
from jax import lax
from jax.experimental import pallas as pl
from jax.experimental.pallas import tpu as pltpu
from jax.sharding import PartitionSpec as P

D = 8192
HD = 128
HQ = 32
KVH = 4
BLOCK = 128
LEN_ROWS = 16
LOW = 32
NEG = -1e30
VMEM_LIMIT = 48 * 1024 * 1024
VMEM_MOST = 60 * 1024 * 1024
F32 = jnp.float32
BF16 = jnp.bfloat16
NT = (((1,), (1,)), ((), ()))


SMEM = pl.BlockSpec(memory_space=pltpu.SMEM)
VMEM = pl.BlockSpec(memory_space=pltpu.VMEM)
HBM = pl.BlockSpec(memory_space=pltpu.HBM)
PARAMS = pltpu.CompilerParams(vmem_limit_bytes=VMEM_LIMIT)
PARAMS_MOST = pltpu.CompilerParams(vmem_limit_bytes=VMEM_MOST)


def cost(flops, nbytes, transcendentals=0):
    return pl.CostEstimate(
        flops=int(flops), bytes_accessed=int(nbytes), transcendentals=int(transcendentals)
    )


def rotated(x, cosine, sine):
    return x * cosine + pltpu.roll(x, HD // 2, 1) * sine


def pack_first_kernel(info_ref, k_ref, v_ref, out_ref, sems):
    count = out_ref.shape[1] - LEN_ROWS
    head = info_ref[0]
    copies = [
        pltpu.make_async_copy(
            ref.at[head, pl.ds(0, count)], out_ref.at[at, pl.ds(0, count)], sems.at[at]
        )
        for at, ref in enumerate((k_ref, v_ref))
    ]
    for copy in copies:
        copy.start()
    live = info_ref[1]
    high = (live // LOW).astype(F32)
    low = (live % LOW).astype(F32)
    out_ref[0, count:] = jnp.full((LEN_ROWS, HD), high, F32).astype(BF16)
    out_ref[1, count:] = jnp.full((LEN_ROWS, HD), low, F32).astype(BF16)
    for copy in copies:
        copy.wait()


def pack_first(info, key_cache, value_cache, count):
    return pl.pallas_call(
        pack_first_kernel,
        out_shape=jax.ShapeDtypeStruct((2, count + LEN_ROWS, HD), BF16),
        in_specs=[SMEM, HBM, HBM],
        out_specs=VMEM,
        scratch_shapes=[pltpu.SemaphoreType.DMA((2,))],
        compiler_params=PARAMS_MOST,
        cost_estimate=cost(0, 4 * count * HD * 2),
        name="pack_first",
    )(info, key_cache, value_cache)


def pack_second_kernel(
    first, info_ref, k_ref, v_ref, nk_ref, nv_ref, cos_ref, sin_ref, out_ref, raw, sems
):
    rows = raw.shape[0]
    count = out_ref.shape[1] - rows
    head = info_ref[0]
    columns = pl.ds(pl.multiple_of(head * HD, HD), HD)
    copies = [
        pltpu.make_async_copy(nk_ref.at[:, columns], raw, sems.at[0]),
        pltpu.make_async_copy(nv_ref.at[:, columns], out_ref.at[1, pl.ds(count, rows)], sems.at[1]),
        pltpu.make_async_copy(
            k_ref.at[head, pl.ds(first, count)], out_ref.at[0, pl.ds(0, count)], sems.at[2]
        ),
        pltpu.make_async_copy(
            v_ref.at[head, pl.ds(first, count)], out_ref.at[1, pl.ds(0, count)], sems.at[3]
        ),
    ]
    for copy in copies:
        copy.start()
    copies[0].wait()
    out_ref[0, count:] = rotated(raw[...].astype(F32), cos_ref[...], sin_ref[...]).astype(BF16)
    for copy in copies[1:]:
        copy.wait()


def pack_second(info, key_cache, value_cache, new_keys, new_values, cosine, sine, first):
    rows = new_keys.shape[0]
    size = key_cache.shape[1] - first + rows
    return pl.pallas_call(
        functools.partial(pack_second_kernel, first),
        out_shape=jax.ShapeDtypeStruct((2, size, HD), BF16),
        in_specs=[SMEM, HBM, HBM, HBM, HBM, VMEM, VMEM],
        out_specs=VMEM,
        scratch_shapes=[pltpu.VMEM((rows, HD), BF16), pltpu.SemaphoreType.DMA((4,))],
        compiler_params=PARAMS_MOST,
        cost_estimate=cost(0, 4 * size * HD * 2),
        name="pack_second",
    )(info, key_cache, value_cache, new_keys, new_values, cosine, sine)


def lane_max(x):
    parts = [x[:, i : i + HD] for i in range(0, x.shape[1], HD)]
    return functools.reduce(jnp.maximum, parts)


def lane_sum(x):
    parts = [x[:, i : i + HD] for i in range(0, x.shape[1], HD)]
    return functools.reduce(jnp.add, parts)


def attend_kernel(plan, lens, first, last, chunk, span, n_kv, offs_ref, q_ref, *refs):
    kv_refs = refs[:n_kv]
    refs = refs[n_kv:]
    begin_row, rows = span
    at_rows = slice(begin_row, begin_row + rows)
    if first:
        cos_ref, sin_ref, acc_out, stats_out, query_out, raw, sem = refs
        copy = pltpu.make_async_copy(q_ref, raw, sem)
        copy.start()
        heads = q_ref.shape[1] // HD
    else:
        acc_in, stats_in = refs[:2]
        refs = refs[2:]
        heads = q_ref.shape[1] // HD
        if chunk:
            w_ref, attended_out, part_out, w_held, sem = refs
            columns = pl.ds(pl.multiple_of(offs_ref[offs_ref.shape[0] - 1] * chunk, chunk), chunk)
            copy = pltpu.make_async_copy(w_ref.at[:, columns], w_held, sem)
            copy.start()
        elif last:
            (attended_out,) = refs
        else:
            acc_out, stats_out = refs
    masks = []
    for array, begin, count, kind, argument in plan:
        if kind == "live":
            ref = kv_refs[lens[array]]
            at = ref.shape[1] - LEN_ROWS
            live = ref[0, at:, :].astype(F32) * LOW + ref[1, at:, :].astype(F32)
            live = live[:1, :]
            slot = lax.broadcasted_iota(jnp.int32, (1, HD), 1).astype(F32)
            pieces = [
                jnp.where(slot + float(argument + i) < live, 0.0, NEG)
                for i in range(0, count, HD)
            ]
            masks.append(jnp.concatenate(pieces, axis=1))
        else:
            row = lax.broadcasted_iota(jnp.int32, (rows, count), 0) + begin_row
            column = lax.broadcasted_iota(jnp.int32, (rows, count), 1)
            masks.append(jnp.where(column <= row + offs_ref[argument], 0.0, NEG))
    if first:
        factor = math.log2(math.e) / math.sqrt(HD)
        cosine = cos_ref[...] * factor
        sine = sin_ref[...] * factor
        copy.wait()
        for head in range(heads):
            at = slice(head * HD, (head + 1) * HD)
            query_out[:, at] = rotated(raw[:, at].astype(F32), cosine, sine).astype(BF16)
        q_ref = query_out

    def score(head):
        query = q_ref[at_rows, head * HD : (head + 1) * HD]
        scores = []
        for (array, begin, count, kind, argument), mask in zip(plan, masks):
            keys = kv_refs[array][0, begin : begin + count, :]
            scores.append(lax.dot_general(query, keys, NT, preferred_element_type=F32) + mask)
        return scores

    lane = lax.broadcasted_iota(jnp.int32, (rows, HD), 1)
    stats = jnp.zeros((rows, HD), F32)
    following = score(0)
    for head in range(heads):
        scores = following
        if head + 1 < heads:
            following = score(head + 1)
        at = slice(head * HD, (head + 1) * HD)
        peak = functools.reduce(jnp.maximum, [lane_max(x) for x in scores])
        peak = jnp.max(peak, axis=1, keepdims=True)
        if not first:
            before = stats_in[at_rows, head : head + 1]
            peak = jnp.maximum(before, peak)
            shrink = jnp.exp2(before - peak)
        total = None
        out = None
        for (array, begin, count, kind, argument), part in zip(plan, scores):
            weights = jnp.exp2(part - peak)
            subtotal = lane_sum(weights)
            total = subtotal if total is None else total + subtotal
            values = kv_refs[array][1, begin : begin + count, :]
            update = jnp.dot(weights.astype(BF16), values, preferred_element_type=F32)
            out = update if out is None else out + update
        total = jnp.sum(total, axis=1, keepdims=True)
        if not first:
            total = total + stats_in[at_rows, HD // 2 + head : HD // 2 + head + 1] * shrink
            out = out + acc_in[at_rows, at] * shrink
        if last:
            attended_out[:, at] = (out / total).astype(BF16)
        else:
            acc_out[:, at] = out
            stats = jnp.where(lane == head, peak, stats)
            stats = jnp.where(lane == HD // 2 + head, total, stats)
    if not last:
        stats_out[...] = stats
    if chunk:
        copy.wait()
        tile = 512
        for i in range(0, chunk, tile):
            part_out[:, i : i + tile] = jnp.dot(
                attended_out[...], w_held[:, i : i + tile], preferred_element_type=F32
            ).astype(BF16)


def attend(name, query, arrays, plan, lens, offs, state, last, tables=None, weight=None, chunk=0, span=None):
    rows, width = query.shape
    first = state is None
    span = (0, rows) if span is None else span
    operands = [offs, query, *arrays]
    in_specs = [SMEM, HBM if first else VMEM] + [VMEM] * len(arrays)
    scratch = []
    if first:
        operands += tables
        in_specs += [VMEM] * 2
        scratch = [pltpu.VMEM((rows, width), BF16), pltpu.SemaphoreType.DMA]
    else:
        operands += state
        in_specs += [VMEM] * 2
    if last:
        out_shape = [jax.ShapeDtypeStruct((span[1], width), BF16)]
        if chunk:
            operands.append(weight)
            in_specs.append(HBM)
            out_shape.append(jax.ShapeDtypeStruct((span[1], chunk), BF16))
            scratch = [pltpu.VMEM((width, chunk), BF16), pltpu.SemaphoreType.DMA]
    else:
        out_shape = [
            jax.ShapeDtypeStruct((rows, width), F32),
            jax.ShapeDtypeStruct((rows, HD), F32),
        ]
        if first:
            out_shape.append(jax.ShapeDtypeStruct((rows, width), BF16))
    keys = sum(p[2] for p in plan)
    return pl.pallas_call(
        functools.partial(attend_kernel, plan, lens, first, last, chunk, span, len(arrays)),
        out_shape=out_shape,
        in_specs=in_specs,
        out_specs=[VMEM] * len(out_shape),
        scratch_shapes=scratch,
        compiler_params=PARAMS,
        cost_estimate=cost(
            span[1] * width * keys // 2, rows * width, span[1] * (width // HD) * keys // 8
        ),
        name=name,
    )(*operands)


def project_kernel(pieces, order_ref, *refs):
    w_ref = refs[pieces]
    for x_ref, out_ref in zip(refs[:pieces], refs[pieces + 1 :]):
        out_ref[...] = jnp.dot(x_ref[...], w_ref[...], preferred_element_type=F32).astype(BF16)


def project(name, order, at, attended, out_weight, chunk, tile=512):
    cut, depth = attended[0].shape
    pieces = len(attended)
    tile = min(tile, chunk)
    per = chunk // tile
    return pl.pallas_call(
        functools.partial(project_kernel, pieces),
        out_shape=(jax.ShapeDtypeStruct((cut, chunk), BF16),) * pieces,
        grid_spec=pltpu.PrefetchScalarGridSpec(
            num_scalar_prefetch=1,
            grid=(per,),
            in_specs=[pl.BlockSpec((cut, depth), lambda j, order: (0, 0))] * pieces
            + [pl.BlockSpec((depth, tile), lambda j, order: (0, order[at] * per + j))],
            out_specs=(pl.BlockSpec((cut, tile), lambda j, order: (0, j)),) * pieces,
        ),
        compiler_params=PARAMS,
        cost_estimate=cost(2 * pieces * cut * depth * chunk, depth * chunk * 2),
        name=name,
    )(order, *attended, out_weight)


def add_kernel(a_ref, b_ref, out_ref):
    out_ref[...] = (a_ref[...].astype(F32) + b_ref[...].astype(F32)).astype(BF16)


def added(name, a, b):
    return pl.pallas_call(
        add_kernel,
        out_shape=jax.ShapeDtypeStruct(a.shape, BF16),
        in_specs=[VMEM, VMEM],
        out_specs=VMEM,
        compiler_params=PARAMS,
        cost_estimate=cost(a.size, a.size * 6),
        name=name,
    )(a, b)


def finish(name, flag, parts, begin, rows_all, into=None):
    rows, columns = parts[0].shape
    blocks = columns // BLOCK
    steps = 2 if blocks % 16 == 0 else 1
    per = blocks // steps
    count = len(parts)
    flags = () if flag is None else (flag,)

    def kernel(*refs):
        if flags:
            chosen = refs[0][0] == 1
            refs = refs[1:]
        out_ref, scale_ref = refs[-2:]
        lane = lax.broadcasted_iota(jnp.int32, (rows, HD), 1)
        scales = jnp.zeros((rows, HD), F32)
        for block in range(per):
            at = slice(block * BLOCK, (block + 1) * BLOCK)
            terms = [ref[:, at].astype(F32) for ref in refs[:count]]
            if flags:
                terms = [jnp.where(chosen, terms[0], terms[1])] + terms[2:]
            total = functools.reduce(jnp.add, terms)
            scale = jnp.max(jnp.abs(total), axis=1, keepdims=True) + 1e-06
            out_ref[:, at] = (total / scale).astype(BF16)
            scales = jnp.where(lane == block, scale, scales)
        scale_ref[...] = scales.T[:per]

    part_spec = pl.BlockSpec((rows, columns // steps), lambda i: (0, i))
    into = () if into is None else into
    return pl.pallas_call(
        kernel,
        out_shape=(
            jax.ShapeDtypeStruct((rows_all, columns), BF16),
            jax.ShapeDtypeStruct((blocks, rows_all), F32),
        ),
        grid=(steps,),
        in_specs=[SMEM] * len(flags) + [part_spec] * count + [pl.BlockSpec(memory_space=pl.ANY)] * len(into),
        out_specs=(
            pl.BlockSpec((rows, columns // steps), lambda i: (begin // rows, i)),
            pl.BlockSpec((per, rows), lambda i: (i, begin // rows)),
        ),
        input_output_aliases={len(flags) + count: 0, len(flags) + count + 1: 1} if into else {},
        compiler_params=PARAMS,
        cost_estimate=cost(rows * columns * 6, rows * columns * 2 * (count + 1)),
        name=name,
    )(*flags, *parts, *into)


def after(value, *others):
    return lax.optimization_barrier((value, *others))[0]


def local(
    queries, new_keys, new_values, key_cache, value_cache, prefix_len, stretch_start, out_weight
):
    rows = queries.shape[0]
    heads_here = queries.shape[1] // HD
    group = HQ // KVH
    tensor_pos = lax.axis_index("tensor")
    lanes = lax.axis_size("tensor")
    n_seq, n_pipe = lax.axis_size("seq"), lax.axis_size("pipe")
    shards = n_seq * n_pipe
    assert heads_here <= group
    slots = key_cache.shape[1]
    split = slots * 3 // 4
    kv_head = tensor_pos * heads_here // group
    me = lax.axis_index("seq") * n_pipe + lax.axis_index("pipe")
    info = jnp.stack([kv_head.astype(jnp.int32), prefix_len[0]])

    positions = stretch_start[0] + me * rows + jnp.arange(rows, dtype=jnp.int32)
    lane = jnp.arange(HD)
    freq = 500000.0 ** (-((lane % (HD // 2)).astype(F32) * 2.0 / HD))
    angle = positions.astype(F32)[:, None] * freq[None, :]
    cosine = jnp.cos(angle)
    sine = jnp.sin(angle) * jnp.where(lane < HD // 2, -1.0, 1.0)[None, :]

    own_a = pack_first(info, key_cache, value_cache, split)
    own_b = pack_second(info, key_cache, value_cache, new_keys, new_values, cosine, sine, split)
    tables = [cosine, sine]
    columns = D // lanes
    step = jnp.arange(lanes, dtype=jnp.int32)

    def whole_plan(at, off):
        return [
            (at, 0, split, "live", 0),
            (at + 1, 0, slots - split, "live", split),
            (at + 1, slots - split, rows, "rows", off),
        ]

    if n_seq == 2 and n_pipe == 2 and lanes == 4:
        order = jnp.where(tensor_pos < 2, 3 - step, step)
        flag = ((tensor_pos == 0) | (tensor_pos == lanes - 1)).astype(jnp.int32).reshape(1)
        inward = [(0, 1), (3, 2)]
        middle = [(1, 2), (2, 1)]
        outward = [(1, 0), (2, 3)]
        swap = [(0, 1), (1, 0)]
        far_a = lax.ppermute(own_a, "seq", swap)
        near_a = lax.ppermute(own_a, "pipe", swap)
        far_b = lax.ppermute(own_b, "seq", swap)
        near_b = lax.ppermute(own_b, "pipe", swap)
        offs = (me - jnp.stack([me, me ^ 1, me ^ 2, me ^ 3])).astype(jnp.int32) * rows
        offs = jnp.concatenate([offs, order[:1]])
        acc, stats, query = attend(
            "attend_near",
            queries,
            [own_a, own_b, near_a, near_b],
            whole_plan(0, 0) + whole_plan(2, 1),
            {0: 0, 1: 0, 2: 2, 3: 2},
            offs,
            None,
            False,
            tables,
        )
        cross_a = lax.ppermute(after(far_a, stats), "pipe", swap)
        cross_b = lax.ppermute(after(far_b, stats), "pipe", swap)
        acc, stats = attend(
            "attend_far_a",
            query,
            [far_a, cross_a],
            [(0, 0, split, "live", 0), (1, 0, split, "live", 0)],
            {0: 0, 1: 1},
            offs,
            (acc, stats),
            False,
        )
        cut = rows // 2
        attended, first_part, come = [], [], [[], [], []]
        for i in range(2):
            x, p = attend(
                f"attend_far_b{i}",
                query,
                [far_b, cross_b, far_a[:, split:], cross_a[:, split:]],
                [
                    (0, 0, slots - split, "live", split),
                    (0, slots - split, rows, "rows", 2),
                    (1, 0, slots - split, "live", split),
                    (1, slots - split, rows, "rows", 3),
                ],
                {0: 2, 1: 3},
                offs,
                (acc, stats) if i == 0 else (acc, after(stats, first_part[0])),
                True,
                weight=out_weight,
                chunk=columns,
                span=(i * cut, cut),
            )
            attended.append(x)
            first_part.append(p)
            come[0].append(lax.ppermute(p, "tensor", inward))
        part = [first_part]
        for k in range(1, 4):
            part.append(project(f"project_{k}", order, k, attended, out_weight, columns))
            if k < 3:
                come[k] = [lax.ppermute(p, "tensor", inward) for p in part[k]]
        done = None
        for i in range(2):
            across = lax.ppermute(added(f"add_0{i}", part[0][i], come[0][i]), "tensor", middle)
            second = lax.ppermute(added(f"add_1{i}", part[1][i], come[1][i]), "tensor", middle)
            back = lax.ppermute(added(f"add_3{i}", part[3][i], across), "tensor", outward)
            parts = [part[3][i], part[2][i], come[2][i], second, back]
            done = finish(f"finish_{i}", flag, parts, i * cut, rows, done)
        return done[0], done[1].T
    all_a = lax.all_gather(own_a, ("seq", "pipe"), axis=0)
    all_b = lax.all_gather(own_b, ("seq", "pipe"), axis=0)
    offs = (me - jnp.arange(shards)).astype(jnp.int32) * rows
    state = None
    query = queries
    for shard in range(shards):
        arrays = [all_a[shard], all_b[shard]]
        state = attend(
            "attend",
            query,
            arrays,
            whole_plan(0, shard),
            {0: 0, 1: 0},
            offs,
            state,
            shard == shards - 1,
            tables,
        )
        if shard == 0:
            query = state[2]
            state = state[:2]
    partial = [
        project(f"project_{k}", step, k, state[:1], out_weight, columns)[0] for k in range(lanes)
    ]
    total = lax.psum_scatter(jnp.stack(partial), "tensor", scatter_dimension=0, tiled=True)[0]
    values, scales = finish("finish", None, [total], 0, rows)
    return values, scales.T


def solution(mesh):
    return jax.shard_map(
        local,
        mesh=mesh,
        in_specs=(
            P(("groups", "seq", "pipe"), "tensor"),
            P(("groups", "seq", "pipe"), None),
            P(("groups", "seq", "pipe"), None),
            P(None, ("groups", "seq", "pipe"), None),
            P(None, ("groups", "seq", "pipe"), None),
            P(("groups", "seq", "pipe")),
            P("groups"),
            P("tensor", None),
        ),
        out_specs=(P(("groups", "seq", "pipe"), "tensor"), P(("groups", "seq", "pipe"), "tensor")),
        check_vma=False,
    )
```

```python
import functools
import math

import jax
import jax.numpy as jnp
from jax import lax
from jax.experimental import pallas as pl
from jax.experimental.pallas import tpu as pltpu
from jax.sharding import PartitionSpec as P

D = 8192
HD = 128
HQ = 32
KVH = 4
BLOCK = 128
LEN_ROWS = 16
LOW = 32
NEG = -1e30
VMEM_LIMIT = 48 * 1024 * 1024
VMEM_MOST = 60 * 1024 * 1024
F32 = jnp.float32
BF16 = jnp.bfloat16
NT = (((1,), (1,)), ((), ()))


SMEM = pl.BlockSpec(memory_space=pltpu.SMEM)
VMEM = pl.BlockSpec(memory_space=pltpu.VMEM)
HBM = pl.BlockSpec(memory_space=pltpu.HBM)
PARAMS = pltpu.CompilerParams(vmem_limit_bytes=VMEM_LIMIT)
PARAMS_MOST = pltpu.CompilerParams(vmem_limit_bytes=VMEM_MOST)


def cost(flops, nbytes, transcendentals=0):
    return pl.CostEstimate(
        flops=int(flops), bytes_accessed=int(nbytes), transcendentals=int(transcendentals)
    )


def rotated(x, cosine, sine):
    return x * cosine + pltpu.roll(x, HD // 2, 1) * sine


def pack_kernel(per_kv_head, heads_here, len_ref, k_ref, v_ref, nk_ref, nv_ref, out_ref, live_rows, sems):
    slots, rows = k_ref.shape[1], nk_ref.shape[0]
    head = lax.axis_index("tensor") * heads_here // per_kv_head
    columns = pl.ds(pl.multiple_of(head * HD, HD), HD)
    copies = []
    for i, (cache, new) in enumerate(((k_ref, nk_ref), (v_ref, nv_ref))):
        copies.append((cache.at[head], out_ref.at[i, pl.ds(0, slots)]))
        copies.append((new.at[:, columns], out_ref.at[i, pl.ds(slots, rows)]))
    copies.append((live_rows, out_ref.at[:, pl.ds(slots + rows, LEN_ROWS)]))
    copies = [pltpu.make_async_copy(*pair, sems.at[i]) for i, pair in enumerate(copies)]
    for copy in copies[:-1]:
        copy.start()
    live = len_ref[0]
    live_rows[0] = jnp.full((LEN_ROWS, HD), (live // LOW).astype(F32), F32).astype(BF16)
    live_rows[1] = jnp.full((LEN_ROWS, HD), (live % LOW).astype(F32), F32).astype(BF16)
    copies[-1].start()
    for copy in copies:
        copy.wait()


def pack(prefix_len, key_cache, value_cache, new_keys, new_values, heads_here):
    size = key_cache.shape[1] + new_keys.shape[0] + LEN_ROWS
    return pl.pallas_call(
        functools.partial(pack_kernel, HQ // KVH, heads_here),
        out_shape=jax.ShapeDtypeStruct((2, size, HD), BF16),
        in_specs=[SMEM, HBM, HBM, HBM, HBM],
        out_specs=HBM,
        scratch_shapes=[pltpu.VMEM((2, LEN_ROWS, HD), BF16), pltpu.SemaphoreType.DMA((5,))],
        compiler_params=PARAMS_MOST,
        cost_estimate=cost(0, 4 * size * HD * 2),
        name="pack",
    )(prefix_len, key_cache, value_cache, new_keys, new_values)


def lane_max(x):
    parts = [x[:, i : i + HD] for i in range(0, x.shape[1], HD)]
    return functools.reduce(jnp.maximum, parts)


def lane_sum(x):
    parts = [x[:, i : i + HD] for i in range(0, x.shape[1], HD)]
    return functools.reduce(jnp.add, parts)


def attend_kernel(first, last, chunk, slots, shards_at, place_ref, q_ref, cos_ref, sin_ref, *refs):
    n = len(shards_at)
    kv_refs = refs[:n]
    refs = refs[n:]
    rows = q_ref.shape[0]
    heads = q_ref.shape[1] // HD
    me = place_ref[0]
    if first:
        acc_out, stats_out, query_out, raw, sem = refs
        copy = pltpu.make_async_copy(q_ref, raw, sem)
        copy.start()
    else:
        acc_in, stats_in = refs[:2]
        refs = refs[2:]
        if chunk:
            w_ref, attended_out, part_a, part_b, w_held, sem = refs
            columns = pl.ds(pl.multiple_of(place_ref[1] * chunk, chunk), chunk)
            copy = pltpu.make_async_copy(w_ref.at[:, columns], w_held, sem)
            copy.start()
        elif last:
            (attended_out,) = refs
        else:
            acc_out, stats_out = refs
    row = lax.broadcasted_iota(jnp.int32, (rows, rows), 0)
    column = lax.broadcasted_iota(jnp.int32, (rows, rows), 1)
    slot = lax.broadcasted_iota(jnp.int32, (1, HD), 1).astype(F32)
    segments = []
    for ref, at in zip(kv_refs, shards_at):
        shard = place_ref[2 + at]
        high = ref[0, slots + rows :, :].astype(F32)
        live = (high * LOW + ref[1, slots + rows :, :].astype(F32))[:1, :]
        pieces = [jnp.where(slot + float(i) < live, 0.0, NEG) for i in range(0, slots, HD)]
        segments.append((ref, None, 0, slots, jnp.concatenate(pieces, axis=1)))
        table = pl.ds(pl.multiple_of(shard * rows, rows), rows)
        keys = rotated(ref[0, slots : slots + rows, :].astype(F32), cos_ref[table], sin_ref[table])
        mask = jnp.where(column <= row + (me - shard) * rows, 0.0, NEG)
        segments.append((ref, keys.astype(BF16), slots, rows, mask))
    if first:
        factor = math.log2(math.e) / math.sqrt(HD)
        table = pl.ds(pl.multiple_of(me * rows, rows), rows)
        cosine = cos_ref[table] * factor
        sine = sin_ref[table] * factor
        copy.wait()
        for head in range(heads):
            at = slice(head * HD, (head + 1) * HD)
            query_out[:, at] = rotated(raw[:, at].astype(F32), cosine, sine).astype(BF16)
        q_ref = query_out

    def score(head):
        query = q_ref[:, head * HD : (head + 1) * HD]
        scores = []
        for ref, keys, begin, count, mask in segments:
            keys = ref[0, begin : begin + count, :] if keys is None else keys
            scores.append(lax.dot_general(query, keys, NT, preferred_element_type=F32) + mask)
        return scores

    lane = lax.broadcasted_iota(jnp.int32, (rows, HD), 1)
    stats = jnp.zeros((rows, HD), F32)
    following = score(0)
    for head in range(heads):
        scores = following
        if head + 1 < heads:
            following = score(head + 1)
        at = slice(head * HD, (head + 1) * HD)
        peak = functools.reduce(jnp.maximum, [lane_max(x) for x in scores])
        peak = jnp.max(peak, axis=1, keepdims=True)
        if not first:
            before = stats_in[:, head : head + 1]
            peak = jnp.maximum(before, peak)
            shrink = jnp.exp2(before - peak)
        total = None
        out = None
        for (ref, keys, begin, count, mask), part in zip(segments, scores):
            weights = jnp.exp2(part - peak)
            subtotal = lane_sum(weights)
            total = subtotal if total is None else total + subtotal
            values = ref[1, begin : begin + count, :]
            update = jnp.dot(weights.astype(BF16), values, preferred_element_type=F32)
            out = update if out is None else out + update
        total = jnp.sum(total, axis=1, keepdims=True)
        if not first:
            total = total + stats_in[:, HD // 2 + head : HD // 2 + head + 1] * shrink
            out = out + acc_in[:, at] * shrink
        if last:
            attended_out[:, at] = (out / total).astype(BF16)
        else:
            acc_out[:, at] = out
            stats = jnp.where(lane == head, peak, stats)
            stats = jnp.where(lane == HD // 2 + head, total, stats)
    if not last:
        stats_out[...] = stats
    if chunk:
        copy.wait()
        tile = 512
        cut = rows // 2
        for i in range(0, chunk, tile):
            part = jnp.dot(attended_out[...], w_held[:, i : i + tile], preferred_element_type=F32)
            part_a[:, i : i + tile] = part[:cut].astype(BF16)
            part_b[:, i : i + tile] = part[cut:].astype(BF16)


def attend(name, place, query, tables, arrays, shards_at, state, last, weight=None, chunk=0):
    rows, width = query.shape
    slots = arrays[0].shape[1] - rows - LEN_ROWS
    first = state is None
    operands = [place, query, *tables, *arrays]
    in_specs = [SMEM, HBM if first else VMEM] + [VMEM] * (2 + len(arrays))
    scratch = []
    if first:
        scratch = [pltpu.VMEM((rows, width), BF16), pltpu.SemaphoreType.DMA]
    else:
        operands += state
        in_specs += [VMEM] * 2
    if last:
        out_shape = [jax.ShapeDtypeStruct((rows, width), BF16)]
        if chunk:
            operands.append(weight)
            in_specs.append(HBM)
            out_shape += [jax.ShapeDtypeStruct((rows // 2, chunk), BF16)] * 2
            scratch = [pltpu.VMEM((width, chunk), BF16), pltpu.SemaphoreType.DMA]
    else:
        out_shape = [
            jax.ShapeDtypeStruct((rows, width), F32),
            jax.ShapeDtypeStruct((rows, HD), F32),
        ]
        if first:
            out_shape.append(jax.ShapeDtypeStruct((rows, width), BF16))
    keys = len(arrays) * (slots + rows)
    return pl.pallas_call(
        functools.partial(attend_kernel, first, last, chunk, slots, shards_at),
        out_shape=out_shape,
        in_specs=in_specs,
        out_specs=[VMEM] * len(out_shape),
        scratch_shapes=scratch,
        compiler_params=PARAMS,
        cost_estimate=cost(
            rows * width * keys // 2, rows * width, rows * (width // HD) * keys // 8
        ),
        name=name,
    )(*operands)


def project_kernel(order_ref, x_ref, w_ref, *out_refs):
    out = jnp.dot(x_ref[...], w_ref[...], preferred_element_type=F32)
    cut = out_refs[0].shape[0]
    for i, ref in enumerate(out_refs):
        ref[...] = out[i * cut : (i + 1) * cut].astype(BF16)


def project(name, order, at, attended, out_weight, chunk, pieces, tile=512):
    rows, depth = attended.shape
    cut = rows // pieces
    tile = min(tile, chunk)
    per = chunk // tile
    return pl.pallas_call(
        project_kernel,
        out_shape=(jax.ShapeDtypeStruct((cut, chunk), BF16),) * pieces,
        grid_spec=pltpu.PrefetchScalarGridSpec(
            num_scalar_prefetch=1,
            grid=(per,),
            in_specs=[
                pl.BlockSpec((rows, depth), lambda j, order: (0, 0)),
                pl.BlockSpec((depth, tile), lambda j, order: (0, order[at] * per + j)),
            ],
            out_specs=(pl.BlockSpec((cut, tile), lambda j, order: (0, j)),) * pieces,
        ),
        compiler_params=PARAMS,
        cost_estimate=cost(2 * rows * depth * chunk, depth * chunk * 2),
        name=name,
    )(order, attended, out_weight)


def add_kernel(a_ref, b_ref, out_ref):
    out_ref[...] = (a_ref[...].astype(F32) + b_ref[...].astype(F32)).astype(BF16)


def added(name, a, b):
    return pl.pallas_call(
        add_kernel,
        out_shape=jax.ShapeDtypeStruct(a.shape, BF16),
        in_specs=[VMEM, VMEM],
        out_specs=VMEM,
        compiler_params=PARAMS,
        cost_estimate=cost(a.size, a.size * 6),
        name=name,
    )(a, b)


def finish(name, flag, parts, begin, rows_all, into=None):
    rows, columns = parts[0].shape
    blocks = columns // BLOCK
    steps = 2 if blocks % 16 == 0 else 1
    per = blocks // steps
    count = len(parts)
    flags = () if flag is None else (flag,)

    def kernel(*refs):
        if flags:
            chosen = refs[0][0] == 1
            refs = refs[1:]
        out_ref, scale_ref = refs[-2:]
        lane = lax.broadcasted_iota(jnp.int32, (rows, HD), 1)
        scales = jnp.zeros((rows, HD), F32)
        for block in range(per):
            at = slice(block * BLOCK, (block + 1) * BLOCK)
            terms = [ref[:, at].astype(F32) for ref in refs[:count]]
            if flags:
                terms = [jnp.where(chosen, terms[0], terms[1])] + terms[2:]
            total = functools.reduce(jnp.add, terms)
            scale = jnp.max(jnp.abs(total), axis=1, keepdims=True) + 1e-06
            out_ref[:, at] = (total / scale).astype(BF16)
            scales = jnp.where(lane == block, scale, scales)
        scale_ref[...] = scales.T[:per]

    part_spec = pl.BlockSpec((rows, columns // steps), lambda i: (0, i))
    into = () if into is None else into
    return pl.pallas_call(
        kernel,
        out_shape=(
            jax.ShapeDtypeStruct((rows_all, columns), BF16),
            jax.ShapeDtypeStruct((blocks, rows_all), F32),
        ),
        grid=(steps,),
        in_specs=[SMEM] * len(flags) + [part_spec] * count + [pl.BlockSpec(memory_space=pl.ANY)] * len(into),
        out_specs=(
            pl.BlockSpec((rows, columns // steps), lambda i: (begin // rows, i)),
            pl.BlockSpec((per, rows), lambda i: (i, begin // rows)),
        ),
        input_output_aliases={len(flags) + count: 0, len(flags) + count + 1: 1} if into else {},
        compiler_params=PARAMS,
        cost_estimate=cost(rows * columns * 6, rows * columns * 2 * (count + 1)),
        name=name,
    )(*flags, *parts, *into)


def after(value, *others):
    return lax.optimization_barrier((value, *others))[0]


def local(
    queries, new_keys, new_values, key_cache, value_cache, prefix_len, stretch_start, out_weight
):
    rows = queries.shape[0]
    heads_here = queries.shape[1] // HD
    group = HQ // KVH
    tensor_pos = lax.axis_index("tensor")
    lanes = lax.axis_size("tensor")
    n_seq, n_pipe = lax.axis_size("seq"), lax.axis_size("pipe")
    shards = n_seq * n_pipe
    assert heads_here <= group
    me = lax.axis_index("seq") * n_pipe + lax.axis_index("pipe")
    own = pack(prefix_len, key_cache, value_cache, new_keys, new_values, heads_here)

    positions = stretch_start[0] + jnp.arange(shards * rows, dtype=jnp.int32)
    lane = jnp.arange(HD)
    freq = 500000.0 ** (-((lane % (HD // 2)).astype(F32) * 2.0 / HD))
    angle = positions.astype(F32)[:, None] * freq[None, :]
    tables = [jnp.cos(angle), jnp.sin(angle) * jnp.where(lane < HD // 2, -1.0, 1.0)[None, :]]

    columns = D // lanes
    step = jnp.arange(lanes, dtype=jnp.int32)
    if n_seq == 2 and n_pipe == 2 and lanes == 4:
        order = jnp.where(tensor_pos < 2, 3 - step, step)
        flag = ((tensor_pos == 0) | (tensor_pos == lanes - 1)).astype(jnp.int32).reshape(1)
        inward = [(0, 1), (3, 2)]
        middle = [(1, 2), (2, 1)]
        outward = [(1, 0), (2, 3)]
        swap = [(0, 1), (1, 0)]
        far = lax.ppermute(own, "seq", swap)
        near = lax.ppermute(own, "pipe", swap)
        place = jnp.stack([me, order[0], me, me ^ 1, me ^ 2, me ^ 3]).astype(jnp.int32)
        acc, stats, query = attend(
            "attend_near", place, queries, tables, [own, near], (0, 1), None, False
        )
        far = after(far, stats)
        cross = lax.ppermute(far, "pipe", swap)
        acc, stats = attend(
            "attend_far", place, query, tables, [far], (2,), (acc, stats), False
        )
        attended, *first_part = attend(
            "attend_cross",
            place,
            query,
            tables,
            [cross],
            (3,),
            (acc, stats),
            True,
            weight=out_weight,
            chunk=columns,
        )
        part = [first_part]
        for k in range(1, 4):
            part.append(project(f"project_{k}", order, k, attended, out_weight, columns, 2))
        come = [[lax.ppermute(p, "tensor", inward) for p in part[k]] for k in range(3)]
        cut = rows // 2
        done = None
        for i in range(2):
            across = lax.ppermute(added(f"add_0{i}", part[0][i], come[0][i]), "tensor", middle)
            second = lax.ppermute(added(f"add_1{i}", part[1][i], come[1][i]), "tensor", middle)
            back = lax.ppermute(added(f"add_3{i}", part[3][i], across), "tensor", outward)
            parts = [part[3][i], part[2][i], come[2][i], second, back]
            done = finish(f"finish_{i}", flag, parts, i * cut, rows, done)
        return done[0], done[1].T
    every = lax.all_gather(own, ("seq", "pipe"), axis=0)
    place = jnp.concatenate([jnp.stack([me, me]), jnp.arange(shards)]).astype(jnp.int32)
    state = None
    query = queries
    for shard in range(shards):
        state = attend(
            "attend", place, query, tables, [every[shard]], (shard,), state, shard == shards - 1
        )
        if shard == 0:
            query = state[2]
            state = state[:2]
    partial = [
        project(f"project_{k}", step, k, state[0], out_weight, columns, 1)[0] for k in range(lanes)
    ]
    total = lax.psum_scatter(jnp.stack(partial), "tensor", scatter_dimension=0, tiled=True)[0]
    values, scales = finish("finish", None, [total], 0, rows)
    return values, scales.T


def solution(mesh):
    return jax.shard_map(
        local,
        mesh=mesh,
        in_specs=(
            P(("groups", "seq", "pipe"), "tensor"),
            P(("groups", "seq", "pipe"), None),
            P(("groups", "seq", "pipe"), None),
            P(None, ("groups", "seq", "pipe"), None),
            P(None, ("groups", "seq", "pipe"), None),
            P(("groups", "seq", "pipe")),
            P("groups"),
            P("tensor", None),
        ),
        out_specs=(P(("groups", "seq", "pipe"), "tensor"), P(("groups", "seq", "pipe"), "tensor")),
        check_vma=False,
    )
```

```python
import functools
import math

import jax
import jax.numpy as jnp
from jax import lax
from jax.experimental import pallas as pl
from jax.experimental.pallas import tpu as pltpu
from jax.sharding import PartitionSpec as P

D = 8192
HD = 128
HQ = 32
KVH = 4
BLOCK = 128
LEN_ROWS = 16
LOW = 32
W_COPIES = 8
NEG = -1e30
VMEM_LIMIT = 48 * 1024 * 1024
VMEM_MOST = 60 * 1024 * 1024
F32 = jnp.float32
BF16 = jnp.bfloat16
NT = (((1,), (1,)), ((), ()))


SMEM = pl.BlockSpec(memory_space=pltpu.SMEM)
VMEM = pl.BlockSpec(memory_space=pltpu.VMEM)
HBM = pl.BlockSpec(memory_space=pltpu.HBM)
PARAMS = pltpu.CompilerParams(vmem_limit_bytes=VMEM_LIMIT)
PARAMS_MOST = pltpu.CompilerParams(vmem_limit_bytes=VMEM_MOST)


def cost(flops, nbytes, transcendentals=0):
    return pl.CostEstimate(
        flops=int(flops), bytes_accessed=int(nbytes), transcendentals=int(transcendentals)
    )


def rotated(x, cosine, sine):
    return x * cosine + pltpu.roll(x, HD // 2, 1) * sine


def pack_kernel(per_kv_head, heads_here, len_ref, k_ref, v_ref, nk_ref, nv_ref, out_ref, sems):
    slots, rows = k_ref.shape[1], nk_ref.shape[0]
    head = lax.axis_index("tensor") * heads_here // per_kv_head
    columns = pl.ds(pl.multiple_of(head * HD, HD), HD)
    copies = []
    for i, (cache, new) in enumerate(((k_ref, nk_ref), (v_ref, nv_ref))):
        copies.append((cache.at[head], out_ref.at[i, pl.ds(0, slots)]))
        copies.append((new.at[:, columns], out_ref.at[i, pl.ds(slots, rows)]))
    copies = [pltpu.make_async_copy(*pair, sems.at[i]) for i, pair in enumerate(copies)]
    for copy in copies:
        copy.start()
    live = len_ref[0]
    for i, part in enumerate((live // LOW, live % LOW)):
        part = jnp.full((LEN_ROWS, HD), part.astype(F32), F32).astype(BF16)
        out_ref[i, slots + rows :] = part
    for copy in copies:
        copy.wait()


def pack(prefix_len, key_cache, value_cache, new_keys, new_values, heads_here):
    size = key_cache.shape[1] + new_keys.shape[0] + LEN_ROWS
    return pl.pallas_call(
        functools.partial(pack_kernel, HQ // KVH, heads_here),
        out_shape=jax.ShapeDtypeStruct((2, size, HD), BF16),
        in_specs=[SMEM, HBM, HBM, HBM, HBM],
        out_specs=VMEM,
        scratch_shapes=[pltpu.SemaphoreType.DMA((4,))],
        compiler_params=PARAMS_MOST,
        cost_estimate=cost(0, 4 * size * HD * 2),
        name="pack",
    )(prefix_len, key_cache, value_cache, new_keys, new_values)


def lane_max(x):
    parts = [x[:, i : i + HD] for i in range(0, x.shape[1], HD)]
    return functools.reduce(jnp.maximum, parts)


def lane_sum(x):
    parts = [x[:, i : i + HD] for i in range(0, x.shape[1], HD)]
    return functools.reduce(jnp.add, parts)


def attend_kernel(
    first, last, chunk, slots, shards_at, span, held, place_ref, q_ref, cos_ref, sin_ref, *refs
):
    n = len(shards_at)
    kv_refs = refs[:n]
    refs = refs[n:]
    rows = q_ref.shape[0]
    heads = q_ref.shape[1] // HD
    begin_row, n_rows = span
    at_rows = slice(begin_row, begin_row + n_rows)
    at_held = slice(held, held + n_rows)
    me = place_ref[0]
    if first:
        acc_out, stats_out, query_out, raw, sem = refs
        copy = pltpu.make_async_copy(q_ref, raw, sem)
        copy.start()
    else:
        acc_in, stats_in = refs[:2]
        refs = refs[2:]
        if chunk:
            w_ref, attended_out, part_out, w_held, sems = refs
            columns = pl.ds(pl.multiple_of(place_ref[1] * chunk, chunk), chunk)
            depth = w_ref.shape[0] // W_COPIES
            copies = []
            for i in range(W_COPIES):
                at = pl.ds(i * depth, depth)
                copies.append(pltpu.make_async_copy(w_ref.at[at, columns], w_held.at[at], sems.at[i]))
                copies[i].start()
        elif last:
            (attended_out,) = refs
        else:
            acc_out, stats_out = refs
    row = lax.broadcasted_iota(jnp.int32, (n_rows, rows), 0) + begin_row
    column = lax.broadcasted_iota(jnp.int32, (n_rows, rows), 1)
    slot = lax.broadcasted_iota(jnp.int32, (1, HD), 1).astype(F32)
    segments = []
    for ref, at in zip(kv_refs, shards_at):
        shard = place_ref[2 + at]
        high = ref[0, slots + rows :, :].astype(F32)
        live = (high * LOW + ref[1, slots + rows :, :].astype(F32))[:1, :]
        pieces = [jnp.where(slot + float(i) < live, 0.0, NEG) for i in range(0, slots, HD)]
        segments.append((ref, None, 0, slots, jnp.concatenate(pieces, axis=1)))
        table = pl.ds(pl.multiple_of(shard * rows, rows), rows)
        keys = rotated(ref[0, slots : slots + rows, :].astype(F32), cos_ref[table], sin_ref[table])
        mask = jnp.where(column <= row + (me - shard) * rows, 0.0, NEG)
        segments.append((ref, keys.astype(BF16), slots, rows, mask))
    if first:
        factor = math.log2(math.e) / math.sqrt(HD)
        table = pl.ds(pl.multiple_of(me * rows, rows), rows)
        cosine = cos_ref[table] * factor
        sine = sin_ref[table] * factor
        copy.wait()
        for head in range(heads):
            at = slice(head * HD, (head + 1) * HD)
            query_out[:, at] = rotated(raw[:, at].astype(F32), cosine, sine).astype(BF16)
        q_ref = query_out

    def score(head):
        query = q_ref[at_rows, head * HD : (head + 1) * HD]
        scores = []
        for ref, keys, begin, count, mask in segments:
            keys = ref[0, begin : begin + count, :] if keys is None else keys
            scores.append(lax.dot_general(query, keys, NT, preferred_element_type=F32) + mask)
        return scores

    lane = lax.broadcasted_iota(jnp.int32, (n_rows, HD), 1)
    stats = jnp.zeros((n_rows, HD), F32)
    following = score(0)
    for head in range(heads):
        scores = following
        if head + 1 < heads:
            following = score(head + 1)
        at = slice(head * HD, (head + 1) * HD)
        peak = functools.reduce(jnp.maximum, [lane_max(x) for x in scores])
        peak = jnp.max(peak, axis=1, keepdims=True)
        if not first:
            before = stats_in[at_held, head : head + 1]
            peak = jnp.maximum(before, peak)
            shrink = jnp.exp2(before - peak)
        total = None
        out = None
        for (ref, keys, begin, count, mask), part in zip(segments, scores):
            weights = jnp.exp2(part - peak)
            subtotal = lane_sum(weights)
            total = subtotal if total is None else total + subtotal
            values = ref[1, begin : begin + count, :]
            update = jnp.dot(weights.astype(BF16), values, preferred_element_type=F32)
            out = update if out is None else out + update
        total = jnp.sum(total, axis=1, keepdims=True)
        if not first:
            total = total + stats_in[at_held, HD // 2 + head : HD // 2 + head + 1] * shrink
            out = out + acc_in[at_held, at] * shrink
        if last:
            attended_out[:, at] = (out / total).astype(BF16)
        else:
            acc_out[:, at] = out
            stats = jnp.where(lane == head, peak, stats)
            stats = jnp.where(lane == HD // 2 + head, total, stats)
    if not last:
        stats_out[...] = stats
    if chunk:
        for copy in copies:
            copy.wait()
        tile = 512
        for i in range(0, chunk, tile):
            part = jnp.dot(attended_out[...], w_held[:, i : i + tile], preferred_element_type=F32)
            part_out[:, i : i + tile] = part.astype(BF16)


def attend(
    name, place, query, tables, arrays, shards_at, state, last, weight=None, chunk=0, span=None, held=0
):
    rows, width = query.shape
    slots = arrays[0].shape[1] - rows - LEN_ROWS
    span = (0, rows) if span is None else span
    first = state is None
    operands = [place, query, *tables, *arrays]
    in_specs = [SMEM, HBM if first else VMEM] + [VMEM] * (2 + len(arrays))
    scratch = []
    if first:
        scratch = [pltpu.VMEM((rows, width), BF16), pltpu.SemaphoreType.DMA]
    else:
        operands += state
        in_specs += [VMEM] * 2
    if last:
        out_shape = [jax.ShapeDtypeStruct((span[1], width), BF16)]
        if chunk:
            operands.append(weight)
            in_specs.append(HBM)
            out_shape.append(jax.ShapeDtypeStruct((span[1], chunk), BF16))
            scratch = [pltpu.VMEM((width, chunk), BF16), pltpu.SemaphoreType.DMA((W_COPIES,))]
    else:
        out_shape = [
            jax.ShapeDtypeStruct((span[1], width), F32),
            jax.ShapeDtypeStruct((span[1], HD), F32),
        ]
        if first:
            out_shape.append(jax.ShapeDtypeStruct((rows, width), BF16))
    keys = len(arrays) * (slots + rows)
    return pl.pallas_call(
        functools.partial(attend_kernel, first, last, chunk, slots, shards_at, span, held),
        out_shape=out_shape,
        in_specs=in_specs,
        out_specs=[VMEM] * len(out_shape),
        scratch_shapes=scratch,
        compiler_params=PARAMS,
        cost_estimate=cost(
            rows * width * keys // 2, rows * width, rows * (width // HD) * keys // 8
        ),
        name=name,
    )(*operands)


def project_kernel(pieces, order_ref, *refs):
    x = jnp.concatenate([ref[...] for ref in refs[:pieces]], axis=0)
    out = jnp.dot(x, refs[pieces][...], preferred_element_type=F32)
    cut = refs[0].shape[0]
    for i, ref in enumerate(refs[pieces + 1 :]):
        ref[...] = out[i * cut : (i + 1) * cut].astype(BF16)


def project(name, order, at, attended, out_weight, chunk, tile=512):
    cut, depth = attended[0].shape
    pieces = len(attended)
    tile = min(tile, chunk)
    per = chunk // tile
    return pl.pallas_call(
        functools.partial(project_kernel, pieces),
        out_shape=(jax.ShapeDtypeStruct((cut, chunk), BF16),) * pieces,
        grid_spec=pltpu.PrefetchScalarGridSpec(
            num_scalar_prefetch=1,
            grid=(per,),
            in_specs=[pl.BlockSpec((cut, depth), lambda j, order: (0, 0))] * pieces
            + [pl.BlockSpec((depth, tile), lambda j, order: (0, order[at] * per + j))],
            out_specs=(pl.BlockSpec((cut, tile), lambda j, order: (0, j)),) * pieces,
        ),
        compiler_params=PARAMS,
        cost_estimate=cost(2 * pieces * cut * depth * chunk, depth * chunk * 2),
        name=name,
    )(order, *attended, out_weight)


def add_kernel(a_ref, b_ref, out_ref):
    out_ref[...] = (a_ref[...].astype(F32) + b_ref[...].astype(F32)).astype(BF16)


def added(name, a, b):
    return pl.pallas_call(
        add_kernel,
        out_shape=jax.ShapeDtypeStruct(a.shape, BF16),
        in_specs=[VMEM, VMEM],
        out_specs=VMEM,
        compiler_params=PARAMS,
        cost_estimate=cost(a.size, a.size * 6),
        name=name,
    )(a, b)


def finish(name, flag, parts, begin, rows_all, into=None):
    rows, columns = parts[0].shape
    blocks = columns // BLOCK
    steps = 2 if blocks % 16 == 0 else 1
    per = blocks // steps
    count = len(parts)
    flags = () if flag is None else (flag,)

    def kernel(*refs):
        if flags:
            chosen = refs[0][0] == 1
            refs = refs[1:]
        out_ref, scale_ref = refs[-2:]
        lane = lax.broadcasted_iota(jnp.int32, (rows, HD), 1)
        scales = jnp.zeros((rows, HD), F32)
        for block in range(per):
            at = slice(block * BLOCK, (block + 1) * BLOCK)
            terms = [ref[:, at].astype(F32) for ref in refs[:count]]
            if flags:
                terms = [jnp.where(chosen, terms[0], terms[1])] + terms[2:]
            total = functools.reduce(jnp.add, terms)
            scale = jnp.max(jnp.abs(total), axis=1, keepdims=True) + 1e-06
            out_ref[:, at] = (total / scale).astype(BF16)
            scales = jnp.where(lane == block, scale, scales)
        scale_ref[...] = scales.T[:per]

    part_spec = pl.BlockSpec((rows, columns // steps), lambda i: (0, i))
    into = () if into is None else into
    return pl.pallas_call(
        kernel,
        out_shape=(
            jax.ShapeDtypeStruct((rows_all, columns), BF16),
            jax.ShapeDtypeStruct((blocks, rows_all), F32),
        ),
        grid=(steps,),
        in_specs=[SMEM] * len(flags) + [part_spec] * count + [pl.BlockSpec(memory_space=pl.ANY)] * len(into),
        out_specs=(
            pl.BlockSpec((rows, columns // steps), lambda i: (begin // rows, i)),
            pl.BlockSpec((per, rows), lambda i: (i, begin // rows)),
        ),
        input_output_aliases={len(flags) + count: 0, len(flags) + count + 1: 1} if into else {},
        compiler_params=PARAMS,
        cost_estimate=cost(rows * columns * 6, rows * columns * 2 * (count + 1)),
        name=name,
    )(*flags, *parts, *into)


def after(value, *others):
    return lax.optimization_barrier((value, *others))[0]


def local(
    queries, new_keys, new_values, key_cache, value_cache, prefix_len, stretch_start, out_weight
):
    rows = queries.shape[0]
    heads_here = queries.shape[1] // HD
    group = HQ // KVH
    tensor_pos = lax.axis_index("tensor")
    lanes = lax.axis_size("tensor")
    n_seq, n_pipe = lax.axis_size("seq"), lax.axis_size("pipe")
    shards = n_seq * n_pipe
    assert heads_here <= group
    me = lax.axis_index("seq") * n_pipe + lax.axis_index("pipe")
    own = pack(prefix_len, key_cache, value_cache, new_keys, new_values, heads_here)

    positions = stretch_start[0] + jnp.arange(shards * rows, dtype=jnp.int32)
    lane = jnp.arange(HD)
    freq = 500000.0 ** (-((lane % (HD // 2)).astype(F32) * 2.0 / HD))
    angle = positions.astype(F32)[:, None] * freq[None, :]
    tables = [jnp.cos(angle), jnp.sin(angle) * jnp.where(lane < HD // 2, -1.0, 1.0)[None, :]]

    columns = D // lanes
    step = jnp.arange(lanes, dtype=jnp.int32)
    if n_seq == 2 and n_pipe == 2 and lanes == 4:
        order = jnp.where(tensor_pos < 2, 3 - step, step)
        flag = ((tensor_pos == 0) | (tensor_pos == lanes - 1)).astype(jnp.int32).reshape(1)
        inward = [(0, 1), (3, 2)]
        middle = [(1, 2), (2, 1)]
        outward = [(1, 0), (2, 3)]
        swap = [(0, 1), (1, 0)]
        far = lax.ppermute(own, "seq", swap)
        near = lax.ppermute(own, "pipe", swap)
        place = jnp.stack([me, order[0], me, me ^ 1, me ^ 2, me ^ 3]).astype(jnp.int32)
        acc, stats, query = attend(
            "attend_near", place, queries, tables, [own, near], (0, 1), None, False
        )
        far = after(far, stats)
        cross = lax.ppermute(far, "pipe", swap)
        cut = rows // 2
        state = attend(
            "attend_far", place, query, tables, [far], (2,), (acc, stats), False, span=(0, cut)
        )
        attended, first_part = [None, None], [None, None]
        attended[0], first_part[0] = attend(
            "attend_cross",
            place,
            query,
            tables,
            [cross],
            (3,),
            tuple(state),
            True,
            weight=out_weight,
            chunk=columns,
            span=(0, cut),
        )
        attended[1], first_part[1] = attend(
            "attend_rest",
            place,
            query,
            tables,
            [far, cross],
            (2, 3),
            (acc, after(stats, first_part[0])),
            True,
            weight=out_weight,
            chunk=columns,
            span=(cut, cut),
            held=cut,
        )
        part = [first_part]
        for k in range(1, 4):
            part.append(project(f"project_{k}", order, k, attended, out_weight, columns))
        come = [[lax.ppermute(p, "tensor", inward) for p in part[k]] for k in range(3)]
        done = None
        for i in range(2):
            across = lax.ppermute(added(f"add_0{i}", part[0][i], come[0][i]), "tensor", middle)
            second = lax.ppermute(added(f"add_1{i}", part[1][i], come[1][i]), "tensor", middle)
            back = lax.ppermute(added(f"add_3{i}", part[3][i], across), "tensor", outward)
            parts = [part[3][i], part[2][i], come[2][i], second, back]
            done = finish(f"finish_{i}", flag, parts, i * cut, rows, done)
        return done[0], done[1].T
    every = lax.all_gather(own, ("seq", "pipe"), axis=0)
    place = jnp.concatenate([jnp.stack([me, me]), jnp.arange(shards)]).astype(jnp.int32)
    state = None
    query = queries
    for shard in range(shards):
        state = attend(
            "attend", place, query, tables, [every[shard]], (shard,), state, shard == shards - 1
        )
        if shard == 0:
            query = state[2]
            state = state[:2]
    partial = [
        project(f"project_{k}", step, k, state[:1], out_weight, columns)[0] for k in range(lanes)
    ]
    total = lax.psum_scatter(jnp.stack(partial), "tensor", scatter_dimension=0, tiled=True)[0]
    values, scales = finish("finish", None, [total], 0, rows)
    return values, scales.T


def solution(mesh):
    return jax.shard_map(
        local,
        mesh=mesh,
        in_specs=(
            P(("groups", "seq", "pipe"), "tensor"),
            P(("groups", "seq", "pipe"), None),
            P(("groups", "seq", "pipe"), None),
            P(None, ("groups", "seq", "pipe"), None),
            P(None, ("groups", "seq", "pipe"), None),
            P(("groups", "seq", "pipe")),
            P("groups"),
            P("tensor", None),
        ),
        out_specs=(P(("groups", "seq", "pipe"), "tensor"), P(("groups", "seq", "pipe"), "tensor")),
        check_vma=False,
    )
```

```python
import functools
import math

import jax
import jax.numpy as jnp
from jax import lax
from jax.experimental import pallas as pl
from jax.experimental.pallas import tpu as pltpu
from jax.sharding import PartitionSpec as P

D = 8192
HD = 128
HQ = 32
KVH = 4
BLOCK = 128
LEN_ROWS = 16
LOW = 32
W_COPIES = 8
NEG = -1e30
VMEM_LIMIT = 44 * 1024 * 1024
VMEM_MOST = 60 * 1024 * 1024
F32 = jnp.float32
BF16 = jnp.bfloat16
NT = (((1,), (1,)), ((), ()))


SMEM = pl.BlockSpec(memory_space=pltpu.SMEM)
VMEM = pl.BlockSpec(memory_space=pltpu.VMEM)
HBM = pl.BlockSpec(memory_space=pltpu.HBM)
PARAMS = pltpu.CompilerParams(vmem_limit_bytes=VMEM_LIMIT)
PARAMS_LESS = pltpu.CompilerParams(vmem_limit_bytes=28 * 1024 * 1024)
PARAMS_MOST = pltpu.CompilerParams(vmem_limit_bytes=VMEM_MOST)


def cost(flops, nbytes, transcendentals=0):
    return pl.CostEstimate(
        flops=int(flops), bytes_accessed=int(nbytes), transcendentals=int(transcendentals)
    )


def rotated(x, cosine, sine):
    return x * cosine + pltpu.roll(x, HD // 2, 1) * sine


def pack_kernel(per_kv_head, heads_here, len_ref, k_ref, v_ref, nk_ref, nv_ref, out_ref, sems):
    slots, rows = k_ref.shape[1], nk_ref.shape[0]
    head = lax.axis_index("tensor") * heads_here // per_kv_head
    columns = pl.ds(pl.multiple_of(head * HD, HD), HD)
    copies = []
    for i, (cache, new) in enumerate(((k_ref, nk_ref), (v_ref, nv_ref))):
        copies.append((cache.at[head], out_ref.at[i, pl.ds(0, slots)]))
        copies.append((new.at[:, columns], out_ref.at[i, pl.ds(slots, rows)]))
    copies = [pltpu.make_async_copy(*pair, sems.at[i]) for i, pair in enumerate(copies)]
    for copy in copies:
        copy.start()
    live = len_ref[0]
    for i, part in enumerate((live // LOW, live % LOW)):
        part = jnp.full((LEN_ROWS, HD), part.astype(F32), F32).astype(BF16)
        out_ref[i, slots + rows :] = part
    for copy in copies:
        copy.wait()


def pack(prefix_len, key_cache, value_cache, new_keys, new_values, heads_here):
    size = key_cache.shape[1] + new_keys.shape[0] + LEN_ROWS
    return pl.pallas_call(
        functools.partial(pack_kernel, HQ // KVH, heads_here),
        out_shape=jax.ShapeDtypeStruct((2, size, HD), BF16),
        in_specs=[SMEM, HBM, HBM, HBM, HBM],
        out_specs=VMEM,
        scratch_shapes=[pltpu.SemaphoreType.DMA((4,))],
        compiler_params=PARAMS_MOST,
        cost_estimate=cost(0, 4 * size * HD * 2),
        name="pack",
    )(prefix_len, key_cache, value_cache, new_keys, new_values)


def lane_max(x):
    parts = [x[:, i : i + HD] for i in range(0, x.shape[1], HD)]
    return functools.reduce(jnp.maximum, parts)


def lane_sum(x):
    parts = [x[:, i : i + HD] for i in range(0, x.shape[1], HD)]
    return functools.reduce(jnp.add, parts)


def attend_kernel(
    first, last, chunk, slots, shards_at, span, held, place_ref, q_ref, cos_ref, sin_ref, *refs
):
    n = len(shards_at)
    kv_refs = refs[:n]
    refs = refs[n:]
    rows = q_ref.shape[0]
    heads = q_ref.shape[1] // HD
    begin_row, n_rows = span
    at_rows = slice(begin_row, begin_row + n_rows)
    at_held = slice(held, held + n_rows)
    me = place_ref[0]
    if first:
        if chunk:
            w_ref, acc_out, stats_out, query_out, w_held, raw, sem, sems = refs
            columns = pl.ds(pl.multiple_of(place_ref[1] * chunk, chunk), chunk)
            depth = w_ref.shape[0] // W_COPIES
            copies = []
            for i in range(W_COPIES):
                at = pl.ds(i * depth, depth)
                copies.append(pltpu.make_async_copy(w_ref.at[at, columns], w_held.at[at], sems.at[i]))
        else:
            acc_out, stats_out, query_out, raw, sem = refs
            copies = []
        copy = pltpu.make_async_copy(q_ref, raw, sem)
        copy.start()
        for other in copies:
            other.start()
    else:
        acc_in, stats_in = refs[:2]
        refs = refs[2:]
        if chunk:
            w_held, attended_out, part_out = refs
        elif last:
            (attended_out,) = refs
        else:
            acc_out, stats_out = refs
    row = lax.broadcasted_iota(jnp.int32, (n_rows, rows), 0) + begin_row
    column = lax.broadcasted_iota(jnp.int32, (n_rows, rows), 1)
    slot = lax.broadcasted_iota(jnp.int32, (1, HD), 1).astype(F32)
    segments = []
    for ref, at in zip(kv_refs, shards_at):
        shard = place_ref[2 + at]
        high = ref[0, slots + rows :, :].astype(F32)
        live = (high * LOW + ref[1, slots + rows :, :].astype(F32))[:1, :]
        pieces = [jnp.where(slot + float(i) < live, 0.0, NEG) for i in range(0, slots, HD)]
        segments.append((ref, None, 0, slots, jnp.concatenate(pieces, axis=1)))
        table = pl.ds(pl.multiple_of(shard * rows, rows), rows)
        keys = rotated(ref[0, slots : slots + rows, :].astype(F32), cos_ref[table], sin_ref[table])
        mask = jnp.where(column <= row + (me - shard) * rows, 0.0, NEG)
        segments.append((ref, keys.astype(BF16), slots, rows, mask))
    if first:
        factor = math.log2(math.e) / math.sqrt(HD)
        table = pl.ds(pl.multiple_of(me * rows, rows), rows)
        cosine = cos_ref[table] * factor
        sine = sin_ref[table] * factor
        copy.wait()
        for head in range(heads):
            at = slice(head * HD, (head + 1) * HD)
            query_out[:, at] = rotated(raw[:, at].astype(F32), cosine, sine).astype(BF16)
        q_ref = query_out

    def score(head):
        query = q_ref[at_rows, head * HD : (head + 1) * HD]
        scores = []
        for ref, keys, begin, count, mask in segments:
            keys = ref[0, begin : begin + count, :] if keys is None else keys
            scores.append(lax.dot_general(query, keys, NT, preferred_element_type=F32) + mask)
        return scores

    lane = lax.broadcasted_iota(jnp.int32, (n_rows, HD), 1)
    stats = jnp.zeros((n_rows, HD), F32)
    following = score(0)
    for head in range(heads):
        scores = following
        if head + 1 < heads:
            following = score(head + 1)
        at = slice(head * HD, (head + 1) * HD)
        peak = functools.reduce(jnp.maximum, [lane_max(x) for x in scores])
        peak = jnp.max(peak, axis=1, keepdims=True)
        if not first:
            before = stats_in[at_held, head : head + 1]
            peak = jnp.maximum(before, peak)
            shrink = jnp.exp2(before - peak)
        total = None
        out = None
        for (ref, keys, begin, count, mask), part in zip(segments, scores):
            weights = jnp.exp2(part - peak)
            subtotal = lane_sum(weights)
            total = subtotal if total is None else total + subtotal
            values = ref[1, begin : begin + count, :]
            update = jnp.dot(weights.astype(BF16), values, preferred_element_type=F32)
            out = update if out is None else out + update
        total = jnp.sum(total, axis=1, keepdims=True)
        if not first:
            total = total + stats_in[at_held, HD // 2 + head : HD // 2 + head + 1] * shrink
            out = out + acc_in[at_held, at] * shrink
        if last:
            attended_out[:, at] = (out / total).astype(BF16)
        else:
            acc_out[:, at] = out
            stats = jnp.where(lane == head, peak, stats)
            stats = jnp.where(lane == HD // 2 + head, total, stats)
    if not last:
        stats_out[...] = stats
    if first:
        for other in copies:
            other.wait()
    elif chunk:
        tile = 512
        for i in range(0, chunk, tile):
            part = jnp.dot(attended_out[...], w_held[:, i : i + tile], preferred_element_type=F32)
            part_out[:, i : i + tile] = part.astype(BF16)


def attend(
    name, place, query, tables, arrays, shards_at, state, last, weight=None, chunk=0, span=None, held=0
):
    rows, width = query.shape
    slots = arrays[0].shape[1] - rows - LEN_ROWS
    span = (0, rows) if span is None else span
    first = state is None
    operands = [place, query, *tables, *arrays]
    in_specs = [SMEM, HBM if first else VMEM] + [VMEM] * (2 + len(arrays))
    scratch = []
    if first:
        scratch = [pltpu.VMEM((rows, width), BF16), pltpu.SemaphoreType.DMA]
    else:
        operands += state
        in_specs += [VMEM] * 2
    if chunk:
        operands.append(weight)
        in_specs.append(HBM if first else VMEM)
    if last:
        out_shape = [jax.ShapeDtypeStruct((span[1], width), BF16)]
        if chunk:
            out_shape.append(jax.ShapeDtypeStruct((span[1], chunk), BF16))
    else:
        out_shape = [
            jax.ShapeDtypeStruct((span[1], width), F32),
            jax.ShapeDtypeStruct((span[1], HD), F32),
        ]
        if first:
            out_shape.append(jax.ShapeDtypeStruct((rows, width), BF16))
            if chunk:
                out_shape.append(jax.ShapeDtypeStruct((width, chunk), BF16))
                scratch.append(pltpu.SemaphoreType.DMA((W_COPIES,)))
    keys = len(arrays) * (slots + rows)
    return pl.pallas_call(
        functools.partial(attend_kernel, first, last, chunk, slots, shards_at, span, held),
        out_shape=out_shape,
        in_specs=in_specs,
        out_specs=[VMEM] * len(out_shape),
        scratch_shapes=scratch,
        compiler_params=PARAMS if first else PARAMS_LESS,
        cost_estimate=cost(
            rows * width * keys // 2, rows * width, rows * (width // HD) * keys // 8
        ),
        name=name,
    )(*operands)


def project_kernel(pieces, order_ref, *refs):
    x = jnp.concatenate([ref[...] for ref in refs[:pieces]], axis=0)
    out = jnp.dot(x, refs[pieces][...], preferred_element_type=F32)
    cut = refs[0].shape[0]
    for i, ref in enumerate(refs[pieces + 1 :]):
        ref[...] = out[i * cut : (i + 1) * cut].astype(BF16)


def project(name, order, at, attended, out_weight, chunk, tile=512):
    cut, depth = attended[0].shape
    pieces = len(attended)
    tile = min(tile, chunk)
    per = chunk // tile
    return pl.pallas_call(
        functools.partial(project_kernel, pieces),
        out_shape=(jax.ShapeDtypeStruct((cut, chunk), BF16),) * pieces,
        grid_spec=pltpu.PrefetchScalarGridSpec(
            num_scalar_prefetch=1,
            grid=(per,),
            in_specs=[pl.BlockSpec((cut, depth), lambda j, order: (0, 0))] * pieces
            + [pl.BlockSpec((depth, tile), lambda j, order: (0, order[at] * per + j))],
            out_specs=(pl.BlockSpec((cut, tile), lambda j, order: (0, j)),) * pieces,
        ),
        compiler_params=PARAMS,
        cost_estimate=cost(2 * pieces * cut * depth * chunk, depth * chunk * 2),
        name=name,
    )(order, *attended, out_weight)


def add_kernel(a_ref, b_ref, out_ref):
    out_ref[...] = (a_ref[...].astype(F32) + b_ref[...].astype(F32)).astype(BF16)


def added(name, a, b):
    return pl.pallas_call(
        add_kernel,
        out_shape=jax.ShapeDtypeStruct(a.shape, BF16),
        in_specs=[VMEM, VMEM],
        out_specs=VMEM,
        compiler_params=PARAMS_LESS,
        cost_estimate=cost(a.size, a.size * 6),
        name=name,
    )(a, b)


def finish(name, flag, parts, begin, rows_all, into=None):
    rows, columns = parts[0].shape
    blocks = columns // BLOCK
    steps = 2 if blocks % 16 == 0 else 1
    per = blocks // steps
    count = len(parts)
    flags = () if flag is None else (flag,)

    def kernel(*refs):
        if flags:
            chosen = refs[0][0] == 1
            refs = refs[1:]
        out_ref, scale_ref = refs[-2:]
        lane = lax.broadcasted_iota(jnp.int32, (rows, HD), 1)
        scales = jnp.zeros((rows, HD), F32)
        for block in range(per):
            at = slice(block * BLOCK, (block + 1) * BLOCK)
            terms = [ref[:, at].astype(F32) for ref in refs[:count]]
            if flags:
                terms = [jnp.where(chosen, terms[0], terms[1])] + terms[2:]
            total = functools.reduce(jnp.add, terms)
            scale = jnp.max(jnp.abs(total), axis=1, keepdims=True) + 1e-06
            out_ref[:, at] = (total / scale).astype(BF16)
            scales = jnp.where(lane == block, scale, scales)
        scale_ref[...] = scales.T[:per]

    part_spec = pl.BlockSpec((rows, columns // steps), lambda i: (0, i))
    into = () if into is None else into
    return pl.pallas_call(
        kernel,
        out_shape=(
            jax.ShapeDtypeStruct((rows_all, columns), BF16),
            jax.ShapeDtypeStruct((blocks, rows_all), F32),
        ),
        grid=(steps,),
        in_specs=[SMEM] * len(flags) + [part_spec] * count + [pl.BlockSpec(memory_space=pl.ANY)] * len(into),
        out_specs=(
            pl.BlockSpec((rows, columns // steps), lambda i: (begin // rows, i)),
            pl.BlockSpec((per, rows), lambda i: (i, begin // rows)),
        ),
        input_output_aliases={len(flags) + count: 0, len(flags) + count + 1: 1} if into else {},
        compiler_params=PARAMS_LESS,
        cost_estimate=cost(rows * columns * 6, rows * columns * 2 * (count + 1)),
        name=name,
    )(*flags, *parts, *into)


def after(value, *others):
    return lax.optimization_barrier((value, *others))[0]


def local(
    queries, new_keys, new_values, key_cache, value_cache, prefix_len, stretch_start, out_weight
):
    rows = queries.shape[0]
    heads_here = queries.shape[1] // HD
    group = HQ // KVH
    tensor_pos = lax.axis_index("tensor")
    lanes = lax.axis_size("tensor")
    n_seq, n_pipe = lax.axis_size("seq"), lax.axis_size("pipe")
    shards = n_seq * n_pipe
    assert heads_here <= group
    me = lax.axis_index("seq") * n_pipe + lax.axis_index("pipe")
    own = pack(prefix_len, key_cache, value_cache, new_keys, new_values, heads_here)

    positions = stretch_start[0] + jnp.arange(shards * rows, dtype=jnp.int32)
    lane = jnp.arange(HD)
    freq = 500000.0 ** (-((lane % (HD // 2)).astype(F32) * 2.0 / HD))
    angle = positions.astype(F32)[:, None] * freq[None, :]
    tables = [jnp.cos(angle), jnp.sin(angle) * jnp.where(lane < HD // 2, -1.0, 1.0)[None, :]]

    columns = D // lanes
    step = jnp.arange(lanes, dtype=jnp.int32)
    if n_seq == 2 and n_pipe == 2 and lanes == 4:
        order = jnp.where(tensor_pos < 2, 3 - step, step)
        flag = ((tensor_pos == 0) | (tensor_pos == lanes - 1)).astype(jnp.int32).reshape(1)
        inward = [(0, 1), (3, 2)]
        middle = [(1, 2), (2, 1)]
        outward = [(1, 0), (2, 3)]
        swap = [(0, 1), (1, 0)]
        far = lax.ppermute(own, "seq", swap)
        near = lax.ppermute(own, "pipe", swap)
        place = jnp.stack([me, order[0], me, me ^ 1, me ^ 2, me ^ 3]).astype(jnp.int32)
        acc, stats, query, w_held = attend(
            "attend_near",
            place,
            queries,
            tables,
            [own, near],
            (0, 1),
            None,
            False,
            weight=out_weight,
            chunk=columns,
        )
        far = after(far, stats)
        cross = lax.ppermute(far, "pipe", swap)
        cut = rows // 2
        state = attend(
            "attend_far", place, query, tables, [far], (2,), (acc, stats), False, span=(0, cut)
        )
        attended, first_part = [None, None], [None, None]
        attended[0], first_part[0] = attend(
            "attend_cross",
            place,
            query,
            tables,
            [cross],
            (3,),
            tuple(state),
            True,
            weight=w_held,
            chunk=columns,
            span=(0, cut),
        )
        attended[1], first_part[1] = attend(
            "attend_rest",
            place,
            query,
            tables,
            [far, cross],
            (2, 3),
            (acc, after(stats, first_part[0])),
            True,
            weight=w_held,
            chunk=columns,
            span=(cut, cut),
            held=cut,
        )
        part = [first_part]
        for k in range(1, 4):
            part.append(project(f"project_{k}", order, k, attended, out_weight, columns))
        come = [[None, None] for k in range(3)]
        for i in range(2):
            come[0][i] = lax.ppermute(part[0][i], "tensor", inward)
        part[1] = [part[1][0], after(part[1][1], come[0][0])]
        for k in (1, 2):
            come[k] = [lax.ppermute(p, "tensor", inward) for p in part[k]]
        done = None
        previous = attended[1]
        for i in range(2):
            previous = added(f"add_0{i}", part[0][i], after(come[0][i], previous))
            across = lax.ppermute(previous, "tensor", middle)
            second = lax.ppermute(added(f"add_1{i}", part[1][i], come[1][i]), "tensor", middle)
            back = lax.ppermute(added(f"add_3{i}", part[3][i], across), "tensor", outward)
            parts = [part[3][i], part[2][i], come[2][i], second, back]
            done = finish(f"finish_{i}", flag, parts, i * cut, rows, done)
        return done[0], done[1].T
    every = lax.all_gather(own, ("seq", "pipe"), axis=0)
    place = jnp.concatenate([jnp.stack([me, me]), jnp.arange(shards)]).astype(jnp.int32)
    state = None
    query = queries
    for shard in range(shards):
        state = attend(
            "attend", place, query, tables, [every[shard]], (shard,), state, shard == shards - 1
        )
        if shard == 0:
            query = state[2]
            state = state[:2]
    partial = [
        project(f"project_{k}", step, k, state[:1], out_weight, columns)[0] for k in range(lanes)
    ]
    total = lax.psum_scatter(jnp.stack(partial), "tensor", scatter_dimension=0, tiled=True)[0]
    values, scales = finish("finish", None, [total], 0, rows)
    return values, scales.T


def solution(mesh):
    return jax.shard_map(
        local,
        mesh=mesh,
        in_specs=(
            P(("groups", "seq", "pipe"), "tensor"),
            P(("groups", "seq", "pipe"), None),
            P(("groups", "seq", "pipe"), None),
            P(None, ("groups", "seq", "pipe"), None),
            P(None, ("groups", "seq", "pipe"), None),
            P(("groups", "seq", "pipe")),
            P("groups"),
            P("tensor", None),
        ),
        out_specs=(P(("groups", "seq", "pipe"), "tensor"), P(("groups", "seq", "pipe"), "tensor")),
        check_vma=False,
    )
```

```python
import functools
import math

import jax
import jax.numpy as jnp
from jax import lax
from jax.experimental import pallas as pl
from jax.experimental.pallas import tpu as pltpu
from jax.sharding import PartitionSpec as P

D = 8192
HD = 128
HQ = 32
KVH = 4
BLOCK = 128
LEN_ROWS = 16
LOW = 32
W_COPIES = 8
HEADS_PER_STEP = 4
NEG = -1e30
VMEM_LIMIT = 44 * 1024 * 1024
VMEM_MOST = 60 * 1024 * 1024
F32 = jnp.float32
BF16 = jnp.bfloat16
NT = (((1,), (1,)), ((), ()))


SMEM = pl.BlockSpec(memory_space=pltpu.SMEM)
VMEM = pl.BlockSpec(memory_space=pltpu.VMEM)
HBM = pl.BlockSpec(memory_space=pltpu.HBM)
PARAMS = pltpu.CompilerParams(vmem_limit_bytes=VMEM_LIMIT)
PARAMS_LESS = pltpu.CompilerParams(vmem_limit_bytes=28 * 1024 * 1024)
PARAMS_MOST = pltpu.CompilerParams(vmem_limit_bytes=VMEM_MOST)


def cost(flops, nbytes, transcendentals=0):
    return pl.CostEstimate(
        flops=int(flops), bytes_accessed=int(nbytes), transcendentals=int(transcendentals)
    )


def rotated(x, cosine, sine):
    return x * cosine + pltpu.roll(x, HD // 2, 1) * sine


def pack_kernel(per_kv_head, heads_here, len_ref, k_ref, v_ref, nk_ref, nv_ref, out_ref, sems):
    slots, rows = k_ref.shape[1], nk_ref.shape[0]
    head = lax.axis_index("tensor") * heads_here // per_kv_head
    columns = pl.ds(pl.multiple_of(head * HD, HD), HD)
    copies = []
    for i, (cache, new) in enumerate(((k_ref, nk_ref), (v_ref, nv_ref))):
        copies.append((cache.at[head], out_ref.at[i, pl.ds(0, slots)]))
        copies.append((new.at[:, columns], out_ref.at[i, pl.ds(slots, rows)]))
    copies = [pltpu.make_async_copy(*pair, sems.at[i]) for i, pair in enumerate(copies)]
    for copy in copies:
        copy.start()
    live = len_ref[0]
    for i, part in enumerate((live // LOW, live % LOW)):
        part = jnp.full((LEN_ROWS, HD), part.astype(F32), F32).astype(BF16)
        out_ref[i, slots + rows :] = part
    for copy in copies:
        copy.wait()


def pack(prefix_len, key_cache, value_cache, new_keys, new_values, heads_here):
    size = key_cache.shape[1] + new_keys.shape[0] + LEN_ROWS
    return pl.pallas_call(
        functools.partial(pack_kernel, HQ // KVH, heads_here),
        out_shape=jax.ShapeDtypeStruct((2, size, HD), BF16),
        in_specs=[SMEM, HBM, HBM, HBM, HBM],
        out_specs=VMEM,
        scratch_shapes=[pltpu.SemaphoreType.DMA((4,))],
        compiler_params=PARAMS_MOST,
        cost_estimate=cost(0, 4 * size * HD * 2),
        name="pack",
    )(prefix_len, key_cache, value_cache, new_keys, new_values)


def lane_max(x):
    parts = [x[:, i : i + HD] for i in range(0, x.shape[1], HD)]
    return functools.reduce(jnp.maximum, parts)


def lane_sum(x):
    parts = [x[:, i : i + HD] for i in range(0, x.shape[1], HD)]
    return functools.reduce(jnp.add, parts)


def attend_kernel(
    first, last, chunk, slots, shards_at, span, held, place_ref, q_ref, cos_ref, sin_ref, *refs
):
    n = len(shards_at)
    kv_refs = refs[:n]
    refs = refs[n:]
    rows = q_ref.shape[0]
    heads = q_ref.shape[1] // HD
    begin_row, n_rows = span
    at_rows = slice(begin_row, begin_row + n_rows)
    at_held = slice(held, held + n_rows)
    me = place_ref[0]
    if first:
        if chunk:
            w_ref, acc_out, stats_out, query_out, w_held, raw, sem, sems = refs
            columns = pl.ds(pl.multiple_of(place_ref[1] * chunk, chunk), chunk)
            depth = w_ref.shape[0] // W_COPIES
            copies = []
            for i in range(W_COPIES):
                at = pl.ds(i * depth, depth)
                copies.append(pltpu.make_async_copy(w_ref.at[at, columns], w_held.at[at], sems.at[i]))
        else:
            acc_out, stats_out, query_out, raw, sem = refs
            copies = []
        copy = pltpu.make_async_copy(q_ref, raw, sem)
        copy.start()
        for other in copies:
            other.start()
    else:
        acc_in, stats_in = refs[:2]
        refs = refs[2:]
        if chunk:
            w_held, attended_out, part_out = refs
        elif last:
            (attended_out,) = refs
        else:
            acc_out, stats_out = refs
    row = lax.broadcasted_iota(jnp.int32, (n_rows, rows), 0) + begin_row
    column = lax.broadcasted_iota(jnp.int32, (n_rows, rows), 1)
    slot = lax.broadcasted_iota(jnp.int32, (1, HD), 1).astype(F32)
    segments = []
    for ref, at in zip(kv_refs, shards_at):
        shard = place_ref[2 + at]
        high = ref[0, slots + rows :, :].astype(F32)
        live = (high * LOW + ref[1, slots + rows :, :].astype(F32))[:1, :]
        pieces = [jnp.where(slot + float(i) < live, 0.0, NEG) for i in range(0, slots, HD)]
        segments.append((ref, None, 0, slots, jnp.concatenate(pieces, axis=1)))
        table = pl.ds(pl.multiple_of(shard * rows, rows), rows)
        keys = rotated(ref[0, slots : slots + rows, :].astype(F32), cos_ref[table], sin_ref[table])
        mask = jnp.where(column <= row + (me - shard) * rows, 0.0, NEG)
        segments.append((ref, keys.astype(BF16), slots, rows, mask))
    if first:
        factor = math.log2(math.e) / math.sqrt(HD)
        table = pl.ds(pl.multiple_of(me * rows, rows), rows)
        cosine = cos_ref[table] * factor
        sine = sin_ref[table] * factor
        copy.wait()
        for head in range(heads):
            at = slice(head * HD, (head + 1) * HD)
            query_out[:, at] = rotated(raw[:, at].astype(F32), cosine, sine).astype(BF16)
        q_ref = query_out

    lane = lax.broadcasted_iota(jnp.int32, (n_rows, HD), 1)
    per_step = heads if first else min(heads, HEADS_PER_STEP)

    def columns_of(head):
        return pl.ds(head * HD if first else pl.multiple_of(head * HD, HD), HD)

    def score(head):
        query = q_ref[at_rows, columns_of(head)]
        scores = []
        for ref, keys, begin, count, mask in segments:
            keys = ref[0, begin : begin + count, :] if keys is None else keys
            scores.append(lax.dot_general(query, keys, NT, preferred_element_type=F32) + mask)
        return scores

    def step(index, stats):
        head = index * per_step
        following = score(head)
        for i in range(per_step):
            scores = following
            if i + 1 < per_step:
                following = score(head + 1)
            at = columns_of(head)
            peak = functools.reduce(jnp.maximum, [lane_max(x) for x in scores])
            peak = jnp.max(peak, axis=1, keepdims=True)
            if not first:
                held_stats = stats_in[at_held, :]
                before = jnp.max(jnp.where(lane == head, held_stats, -jnp.inf), axis=1, keepdims=True)
                sums = jnp.where(lane == HD // 2 + head, held_stats, 0.0)
                sums = jnp.sum(sums, axis=1, keepdims=True)
                peak = jnp.maximum(before, peak)
                shrink = jnp.exp2(before - peak)
            total = None
            out = None
            for (ref, keys, begin, count, mask), part in zip(segments, scores):
                weights = jnp.exp2(part - peak)
                subtotal = lane_sum(weights)
                total = subtotal if total is None else total + subtotal
                values = ref[1, begin : begin + count, :]
                update = jnp.dot(weights.astype(BF16), values, preferred_element_type=F32)
                out = update if out is None else out + update
            total = jnp.sum(total, axis=1, keepdims=True)
            if not first:
                total = total + sums * shrink
                out = out + acc_in[at_held, at] * shrink
            if last:
                attended_out[:, at] = (out / total).astype(BF16)
            else:
                acc_out[:, at] = out
                stats = jnp.where(lane == head, peak, stats)
                stats = jnp.where(lane == HD // 2 + head, total, stats)
            head = head + 1
        return stats

    stats = jnp.zeros((n_rows, HD), F32)
    if per_step == heads:
        stats = step(0, stats)
    else:
        stats = lax.fori_loop(0, heads // per_step, step, stats)
    if not last:
        stats_out[...] = stats
    if first:
        for other in copies:
            other.wait()
    elif chunk:
        tile = 512
        for i in range(0, chunk, tile):
            part = jnp.dot(attended_out[...], w_held[:, i : i + tile], preferred_element_type=F32)
            part_out[:, i : i + tile] = part.astype(BF16)


def attend(
    name, place, query, tables, arrays, shards_at, state, last, weight=None, chunk=0, span=None, held=0
):
    rows, width = query.shape
    slots = arrays[0].shape[1] - rows - LEN_ROWS
    span = (0, rows) if span is None else span
    first = state is None
    operands = [place, query, *tables, *arrays]
    in_specs = [SMEM, HBM if first else VMEM] + [VMEM] * (2 + len(arrays))
    scratch = []
    if first:
        scratch = [pltpu.VMEM((rows, width), BF16), pltpu.SemaphoreType.DMA]
    else:
        operands += state
        in_specs += [VMEM] * 2
    if chunk:
        operands.append(weight)
        in_specs.append(HBM if first else VMEM)
    if last:
        out_shape = [jax.ShapeDtypeStruct((span[1], width), BF16)]
        if chunk:
            out_shape.append(jax.ShapeDtypeStruct((span[1], chunk), BF16))
    else:
        out_shape = [
            jax.ShapeDtypeStruct((span[1], width), F32),
            jax.ShapeDtypeStruct((span[1], HD), F32),
        ]
        if first:
            out_shape.append(jax.ShapeDtypeStruct((rows, width), BF16))
            if chunk:
                out_shape.append(jax.ShapeDtypeStruct((width, chunk), BF16))
                scratch.append(pltpu.SemaphoreType.DMA((W_COPIES,)))
    keys = len(arrays) * (slots + rows)
    return pl.pallas_call(
        functools.partial(attend_kernel, first, last, chunk, slots, shards_at, span, held),
        out_shape=out_shape,
        in_specs=in_specs,
        out_specs=[VMEM] * len(out_shape),
        scratch_shapes=scratch,
        compiler_params=PARAMS if first else PARAMS_LESS,
        cost_estimate=cost(
            rows * width * keys // 2, rows * width, rows * (width // HD) * keys // 8
        ),
        name=name,
    )(*operands)


def project_kernel(pieces, order_ref, *refs):
    x = jnp.concatenate([ref[...] for ref in refs[:pieces]], axis=0)
    out = jnp.dot(x, refs[pieces][...], preferred_element_type=F32)
    cut = refs[0].shape[0]
    for i, ref in enumerate(refs[pieces + 1 :]):
        ref[...] = out[i * cut : (i + 1) * cut].astype(BF16)


def project(name, order, at, attended, out_weight, chunk, tile=512):
    cut, depth = attended[0].shape
    pieces = len(attended)
    tile = min(tile, chunk)
    per = chunk // tile
    return pl.pallas_call(
        functools.partial(project_kernel, pieces),
        out_shape=(jax.ShapeDtypeStruct((cut, chunk), BF16),) * pieces,
        grid_spec=pltpu.PrefetchScalarGridSpec(
            num_scalar_prefetch=1,
            grid=(per,),
            in_specs=[pl.BlockSpec((cut, depth), lambda j, order: (0, 0))] * pieces
            + [pl.BlockSpec((depth, tile), lambda j, order: (0, order[at] * per + j))],
            out_specs=(pl.BlockSpec((cut, tile), lambda j, order: (0, j)),) * pieces,
        ),
        compiler_params=PARAMS,
        cost_estimate=cost(2 * pieces * cut * depth * chunk, depth * chunk * 2),
        name=name,
    )(order, *attended, out_weight)


def add_kernel(a_ref, b_ref, out_ref):
    out_ref[...] = (a_ref[...].astype(F32) + b_ref[...].astype(F32)).astype(BF16)


def added(name, a, b):
    return pl.pallas_call(
        add_kernel,
        out_shape=jax.ShapeDtypeStruct(a.shape, BF16),
        in_specs=[VMEM, VMEM],
        out_specs=VMEM,
        compiler_params=PARAMS_LESS,
        cost_estimate=cost(a.size, a.size * 6),
        name=name,
    )(a, b)


def finish(name, flag, parts, begin, rows_all, into=None):
    rows, columns = parts[0].shape
    blocks = columns // BLOCK
    steps = 2 if blocks % 16 == 0 else 1
    per = blocks // steps
    count = len(parts)
    flags = () if flag is None else (flag,)

    def kernel(*refs):
        if flags:
            chosen = refs[0][0] == 1
            refs = refs[1:]
        out_ref, scale_ref = refs[-2:]
        lane = lax.broadcasted_iota(jnp.int32, (rows, HD), 1)
        scales = jnp.zeros((rows, HD), F32)
        for block in range(per):
            at = slice(block * BLOCK, (block + 1) * BLOCK)
            terms = [ref[:, at].astype(F32) for ref in refs[:count]]
            if flags:
                terms = [jnp.where(chosen, terms[0], terms[1])] + terms[2:]
            total = functools.reduce(jnp.add, terms)
            scale = jnp.max(jnp.abs(total), axis=1, keepdims=True) + 1e-06
            out_ref[:, at] = (total / scale).astype(BF16)
            scales = jnp.where(lane == block, scale, scales)
        scale_ref[...] = scales.T[:per]

    part_spec = pl.BlockSpec((rows, columns // steps), lambda i: (0, i))
    into = () if into is None else into
    return pl.pallas_call(
        kernel,
        out_shape=(
            jax.ShapeDtypeStruct((rows_all, columns), BF16),
            jax.ShapeDtypeStruct((blocks, rows_all), F32),
        ),
        grid=(steps,),
        in_specs=[SMEM] * len(flags) + [part_spec] * count + [pl.BlockSpec(memory_space=pl.ANY)] * len(into),
        out_specs=(
            pl.BlockSpec((rows, columns // steps), lambda i: (begin // rows, i)),
            pl.BlockSpec((per, rows), lambda i: (i, begin // rows)),
        ),
        input_output_aliases={len(flags) + count: 0, len(flags) + count + 1: 1} if into else {},
        compiler_params=PARAMS_LESS,
        cost_estimate=cost(rows * columns * 6, rows * columns * 2 * (count + 1)),
        name=name,
    )(*flags, *parts, *into)


def after(value, *others):
    return lax.optimization_barrier((value, *others))[0]


def local(
    queries, new_keys, new_values, key_cache, value_cache, prefix_len, stretch_start, out_weight
):
    rows = queries.shape[0]
    heads_here = queries.shape[1] // HD
    group = HQ // KVH
    tensor_pos = lax.axis_index("tensor")
    lanes = lax.axis_size("tensor")
    n_seq, n_pipe = lax.axis_size("seq"), lax.axis_size("pipe")
    shards = n_seq * n_pipe
    assert heads_here <= group
    me = lax.axis_index("seq") * n_pipe + lax.axis_index("pipe")
    own = pack(prefix_len, key_cache, value_cache, new_keys, new_values, heads_here)

    positions = stretch_start[0] + jnp.arange(shards * rows, dtype=jnp.int32)
    lane = jnp.arange(HD)
    freq = 500000.0 ** (-((lane % (HD // 2)).astype(F32) * 2.0 / HD))
    angle = positions.astype(F32)[:, None] * freq[None, :]
    tables = [jnp.cos(angle), jnp.sin(angle) * jnp.where(lane < HD // 2, -1.0, 1.0)[None, :]]

    columns = D // lanes
    step = jnp.arange(lanes, dtype=jnp.int32)
    if n_seq == 2 and n_pipe == 2 and lanes == 4:
        order = jnp.where(tensor_pos < 2, 3 - step, step)
        flag = ((tensor_pos == 0) | (tensor_pos == lanes - 1)).astype(jnp.int32).reshape(1)
        inward = [(0, 1), (3, 2)]
        middle = [(1, 2), (2, 1)]
        outward = [(1, 0), (2, 3)]
        swap = [(0, 1), (1, 0)]
        far = lax.ppermute(own, "seq", swap)
        near = lax.ppermute(own, "pipe", swap)
        place = jnp.stack([me, order[0], me, me ^ 1, me ^ 2, me ^ 3]).astype(jnp.int32)
        acc, stats, query, w_held = attend(
            "attend_near",
            place,
            queries,
            tables,
            [own, near],
            (0, 1),
            None,
            False,
            weight=out_weight,
            chunk=columns,
        )
        far = after(far, stats)
        cross = lax.ppermute(far, "pipe", swap)
        cut = rows // 2
        state = attend(
            "attend_far", place, query, tables, [far], (2,), (acc, stats), False, span=(0, cut)
        )
        attended, first_part = [None, None], [None, None]
        attended[0], first_part[0] = attend(
            "attend_cross",
            place,
            query,
            tables,
            [cross],
            (3,),
            tuple(state),
            True,
            weight=w_held,
            chunk=columns,
            span=(0, cut),
        )
        attended[1], first_part[1] = attend(
            "attend_rest",
            place,
            query,
            tables,
            [far, cross],
            (2, 3),
            (acc, after(stats, first_part[0])),
            True,
            weight=w_held,
            chunk=columns,
            span=(cut, cut),
            held=cut,
        )
        part = [first_part]
        for k in range(1, 4):
            part.append(project(f"project_{k}", order, k, attended, out_weight, columns))
        come = [[None, None] for k in range(3)]
        for i in range(2):
            come[0][i] = lax.ppermute(part[0][i], "tensor", inward)
        part[1] = [part[1][0], after(part[1][1], come[0][0])]
        for k in (1, 2):
            come[k] = [lax.ppermute(p, "tensor", inward) for p in part[k]]
        done = None
        previous = attended[1]
        for i in range(2):
            previous = added(f"add_0{i}", part[0][i], after(come[0][i], previous))
            across = lax.ppermute(previous, "tensor", middle)
            second = lax.ppermute(added(f"add_1{i}", part[1][i], come[1][i]), "tensor", middle)
            back = lax.ppermute(added(f"add_3{i}", part[3][i], across), "tensor", outward)
            parts = [part[3][i], part[2][i], come[2][i], second, back]
            done = finish(f"finish_{i}", flag, parts, i * cut, rows, done)
        return done[0], done[1].T
    every = lax.all_gather(own, ("seq", "pipe"), axis=0)
    place = jnp.concatenate([jnp.stack([me, me]), jnp.arange(shards)]).astype(jnp.int32)
    state = None
    query = queries
    for shard in range(shards):
        state = attend(
            "attend", place, query, tables, [every[shard]], (shard,), state, shard == shards - 1
        )
        if shard == 0:
            query = state[2]
            state = state[:2]
    partial = [
        project(f"project_{k}", step, k, state[:1], out_weight, columns)[0] for k in range(lanes)
    ]
    total = lax.psum_scatter(jnp.stack(partial), "tensor", scatter_dimension=0, tiled=True)[0]
    values, scales = finish("finish", None, [total], 0, rows)
    return values, scales.T


def solution(mesh):
    return jax.shard_map(
        local,
        mesh=mesh,
        in_specs=(
            P(("groups", "seq", "pipe"), "tensor"),
            P(("groups", "seq", "pipe"), None),
            P(("groups", "seq", "pipe"), None),
            P(None, ("groups", "seq", "pipe"), None),
            P(None, ("groups", "seq", "pipe"), None),
            P(("groups", "seq", "pipe")),
            P("groups"),
            P("tensor", None),
        ),
        out_specs=(P(("groups", "seq", "pipe"), "tensor"), P(("groups", "seq", "pipe"), "tensor")),
        check_vma=False,
    )
```

```python
import functools
import math

import jax
import jax.numpy as jnp
from jax import lax
from jax.experimental import pallas as pl
from jax.experimental.pallas import tpu as pltpu
from jax.sharding import PartitionSpec as P

D = 8192
HD = 128
HQ = 32
KVH = 4
BLOCK = 128
LEN_ROWS = 16
LOW = 32
W_COPIES = 8
HEADS_PER_STEP = 4
NEG = -1e30
VMEM_LIMIT = 44 * 1024 * 1024
VMEM_MOST = 60 * 1024 * 1024
F32 = jnp.float32
BF16 = jnp.bfloat16
NT = (((1,), (1,)), ((), ()))


SMEM = pl.BlockSpec(memory_space=pltpu.SMEM)
VMEM = pl.BlockSpec(memory_space=pltpu.VMEM)
HBM = pl.BlockSpec(memory_space=pltpu.HBM)
PARAMS = pltpu.CompilerParams(vmem_limit_bytes=VMEM_LIMIT)
PARAMS_LESS = pltpu.CompilerParams(vmem_limit_bytes=28 * 1024 * 1024)
PARAMS_MOST = pltpu.CompilerParams(vmem_limit_bytes=VMEM_MOST)


def cost(flops, nbytes, transcendentals=0):
    return pl.CostEstimate(
        flops=int(flops), bytes_accessed=int(nbytes), transcendentals=int(transcendentals)
    )


def rotated(x, cosine, sine):
    return x * cosine + pltpu.roll(x, HD // 2, 1) * sine


def pack_kernel(per_kv_head, heads_here, len_ref, k_ref, v_ref, nk_ref, nv_ref, out_ref, sems):
    slots, rows = k_ref.shape[1], nk_ref.shape[0]
    head = lax.axis_index("tensor") * heads_here // per_kv_head
    columns = pl.ds(pl.multiple_of(head * HD, HD), HD)
    copies = []
    for i, (cache, new) in enumerate(((k_ref, nk_ref), (v_ref, nv_ref))):
        copies.append((cache.at[head], out_ref.at[i, pl.ds(0, slots)]))
        copies.append((new.at[:, columns], out_ref.at[i, pl.ds(slots, rows)]))
    copies = [pltpu.make_async_copy(*pair, sems.at[i]) for i, pair in enumerate(copies)]
    for copy in copies:
        copy.start()
    live = len_ref[0]
    for i, part in enumerate((live // LOW, live % LOW)):
        part = jnp.full((LEN_ROWS, HD), part.astype(F32), F32).astype(BF16)
        out_ref[i, slots + rows :] = part
    for copy in copies:
        copy.wait()


def pack(prefix_len, key_cache, value_cache, new_keys, new_values, heads_here):
    size = key_cache.shape[1] + new_keys.shape[0] + LEN_ROWS
    return pl.pallas_call(
        functools.partial(pack_kernel, HQ // KVH, heads_here),
        out_shape=jax.ShapeDtypeStruct((2, size, HD), BF16),
        in_specs=[SMEM, HBM, HBM, HBM, HBM],
        out_specs=VMEM,
        scratch_shapes=[pltpu.SemaphoreType.DMA((4,))],
        compiler_params=PARAMS_MOST,
        cost_estimate=cost(0, 4 * size * HD * 2),
        name="pack",
    )(prefix_len, key_cache, value_cache, new_keys, new_values)


def lane_max(x):
    parts = [x[:, i : i + HD] for i in range(0, x.shape[1], HD)]
    return functools.reduce(jnp.maximum, parts)


def lane_sum(x):
    parts = [x[:, i : i + HD] for i in range(0, x.shape[1], HD)]
    return functools.reduce(jnp.add, parts)


def attend_kernel(
    first, last, chunk, slots, shards_at, span, held, place_ref, q_ref, cos_ref, sin_ref, *refs
):
    n = len(shards_at)
    kv_refs = refs[:n]
    refs = refs[n:]
    rows = q_ref.shape[0]
    heads = q_ref.shape[1] // HD
    begin_row, n_rows = span
    at_rows = slice(begin_row, begin_row + n_rows)
    at_held = slice(held, held + n_rows)
    me = place_ref[0]
    if first:
        if chunk:
            w_ref, acc_out, stats_out, query_out, w_held, raw, sem, sems = refs
            columns = pl.ds(pl.multiple_of(place_ref[1] * chunk, chunk), chunk)
            depth = w_ref.shape[0] // W_COPIES
            copies = []
            for i in range(W_COPIES):
                at = pl.ds(i * depth, depth)
                copies.append(pltpu.make_async_copy(w_ref.at[at, columns], w_held.at[at], sems.at[i]))
        else:
            acc_out, stats_out, query_out, raw, sem = refs
            copies = []
        copy = pltpu.make_async_copy(q_ref, raw, sem)
        copy.start()
        for other in copies:
            other.start()
    else:
        acc_in, stats_in = refs[:2]
        refs = refs[2:]
        if chunk:
            w_held, attended_out, part_out = refs
        elif last:
            (attended_out,) = refs
        else:
            acc_out, stats_out = refs
    row = lax.broadcasted_iota(jnp.int32, (n_rows, rows), 0) + begin_row
    column = lax.broadcasted_iota(jnp.int32, (n_rows, rows), 1)
    slot = lax.broadcasted_iota(jnp.int32, (1, HD), 1).astype(F32)
    segments = []
    for ref, at in zip(kv_refs, shards_at):
        shard = place_ref[2 + at]
        high = ref[0, slots + rows :, :].astype(F32)
        live = (high * LOW + ref[1, slots + rows :, :].astype(F32))[:1, :]
        pieces = [jnp.where(slot + float(i) < live, 0.0, NEG) for i in range(0, slots, HD)]
        segments.append((ref, None, 0, slots, jnp.concatenate(pieces, axis=1)))
        table = pl.ds(pl.multiple_of(shard * rows, rows), rows)
        keys = rotated(ref[0, slots : slots + rows, :].astype(F32), cos_ref[table], sin_ref[table])
        mask = jnp.where(column <= row + (me - shard) * rows, 0.0, NEG)
        segments.append((ref, keys.astype(BF16), slots, rows, mask))
    if first:
        factor = math.log2(math.e) / math.sqrt(HD)
        table = pl.ds(pl.multiple_of(me * rows, rows), rows)
        cosine = cos_ref[table] * factor
        sine = sin_ref[table] * factor
        copy.wait()
        for head in range(heads):
            at = slice(head * HD, (head + 1) * HD)
            query_out[:, at] = rotated(raw[:, at].astype(F32), cosine, sine).astype(BF16)
        q_ref = query_out

    lane = lax.broadcasted_iota(jnp.int32, (n_rows, HD), 1)
    per_step = heads if first else min(heads, HEADS_PER_STEP)

    def columns_of(head):
        return pl.ds(head * HD if first else pl.multiple_of(head * HD, HD), HD)

    def score(head):
        query = q_ref[at_rows, columns_of(head)]
        scores = []
        for ref, keys, begin, count, mask in segments:
            keys = ref[0, begin : begin + count, :] if keys is None else keys
            scores.append(lax.dot_general(query, keys, NT, preferred_element_type=F32) + mask)
        return scores

    def step(index, stats):
        head = index * per_step
        following = score(head)
        for i in range(per_step):
            scores = following
            if i + 1 < per_step:
                following = score(head + 1)
            at = columns_of(head)
            peak = functools.reduce(jnp.maximum, [lane_max(x) for x in scores])
            peak = jnp.max(peak, axis=1, keepdims=True)
            if not first:
                held_stats = stats_in[at_held, :]
                before = jnp.max(jnp.where(lane == head, held_stats, -jnp.inf), axis=1, keepdims=True)
                sums = jnp.where(lane == HD // 2 + head, held_stats, 0.0)
                sums = jnp.sum(sums, axis=1, keepdims=True)
                peak = jnp.maximum(before, peak)
                shrink = jnp.exp2(before - peak)
            total = None
            out = None
            for (ref, keys, begin, count, mask), part in zip(segments, scores):
                weights = jnp.exp2(part - peak)
                subtotal = lane_sum(weights)
                total = subtotal if total is None else total + subtotal
                values = ref[1, begin : begin + count, :]
                update = jnp.dot(weights.astype(BF16), values, preferred_element_type=F32)
                out = update if out is None else out + update
            total = jnp.sum(total, axis=1, keepdims=True)
            if not first:
                total = total + sums * shrink
                out = out + acc_in[at_held, at] * shrink
            if last:
                attended_out[:, at] = (out / total).astype(BF16)
            else:
                acc_out[:, at] = out
                stats = jnp.where(lane == head, peak, stats)
                stats = jnp.where(lane == HD // 2 + head, total, stats)
            head = head + 1
        return stats

    stats = jnp.zeros((n_rows, HD), F32)
    if per_step == heads:
        stats = step(0, stats)
    else:
        stats = lax.fori_loop(0, heads // per_step, step, stats)
    if not last:
        stats_out[...] = stats
    if first:
        for other in copies:
            other.wait()
    elif chunk:
        tile = 512
        for i in range(0, chunk, tile):
            part = jnp.dot(attended_out[...], w_held[:, i : i + tile], preferred_element_type=F32)
            part_out[:, i : i + tile] = part.astype(BF16)


def attend(
    name, place, query, tables, arrays, shards_at, state, last, weight=None, chunk=0, span=None, held=0
):
    rows, width = query.shape
    slots = arrays[0].shape[1] - rows - LEN_ROWS
    span = (0, rows) if span is None else span
    first = state is None
    operands = [place, query, *tables, *arrays]
    in_specs = [SMEM, HBM if first else VMEM] + [VMEM] * (2 + len(arrays))
    scratch = []
    if first:
        scratch = [pltpu.VMEM((rows, width), BF16), pltpu.SemaphoreType.DMA]
    else:
        operands += state
        in_specs += [VMEM] * 2
    if chunk:
        operands.append(weight)
        in_specs.append(HBM if first else VMEM)
    if last:
        out_shape = [jax.ShapeDtypeStruct((span[1], width), BF16)]
        if chunk:
            out_shape.append(jax.ShapeDtypeStruct((span[1], chunk), BF16))
    else:
        out_shape = [
            jax.ShapeDtypeStruct((span[1], width), F32),
            jax.ShapeDtypeStruct((span[1], HD), F32),
        ]
        if first:
            out_shape.append(jax.ShapeDtypeStruct((rows, width), BF16))
            if chunk:
                out_shape.append(jax.ShapeDtypeStruct((width, chunk), BF16))
                scratch.append(pltpu.SemaphoreType.DMA((W_COPIES,)))
    keys = len(arrays) * (slots + rows)
    return pl.pallas_call(
        functools.partial(attend_kernel, first, last, chunk, slots, shards_at, span, held),
        out_shape=out_shape,
        in_specs=in_specs,
        out_specs=[VMEM] * len(out_shape),
        scratch_shapes=scratch,
        compiler_params=PARAMS if first else PARAMS_LESS,
        cost_estimate=cost(
            rows * width * keys // 2, rows * width, rows * (width // HD) * keys // 8
        ),
        name=name,
    )(*operands)


def project_kernel(pieces, order_ref, *refs):
    x = jnp.concatenate([ref[...] for ref in refs[:pieces]], axis=0)
    out = jnp.dot(x, refs[pieces][...], preferred_element_type=F32)
    cut = refs[0].shape[0]
    for i, ref in enumerate(refs[pieces + 1 :]):
        ref[...] = out[i * cut : (i + 1) * cut].astype(BF16)


def project(name, order, at, attended, out_weight, chunk, tile=512):
    cut, depth = attended[0].shape
    pieces = len(attended)
    tile = min(tile, chunk)
    per = chunk // tile
    return pl.pallas_call(
        functools.partial(project_kernel, pieces),
        out_shape=(jax.ShapeDtypeStruct((cut, chunk), BF16),) * pieces,
        grid_spec=pltpu.PrefetchScalarGridSpec(
            num_scalar_prefetch=1,
            grid=(per,),
            in_specs=[pl.BlockSpec((cut, depth), lambda j, order: (0, 0))] * pieces
            + [pl.BlockSpec((depth, tile), lambda j, order: (0, order[at] * per + j))],
            out_specs=(pl.BlockSpec((cut, tile), lambda j, order: (0, j)),) * pieces,
        ),
        compiler_params=PARAMS,
        cost_estimate=cost(2 * pieces * cut * depth * chunk, depth * chunk * 2),
        name=name,
    )(order, *attended, out_weight)


def add_kernel(a_ref, b_ref, out_ref):
    out_ref[...] = (a_ref[...].astype(F32) + b_ref[...].astype(F32)).astype(BF16)


def added(name, a, b):
    return pl.pallas_call(
        add_kernel,
        out_shape=jax.ShapeDtypeStruct(a.shape, BF16),
        in_specs=[VMEM, VMEM],
        out_specs=VMEM,
        compiler_params=PARAMS_LESS,
        cost_estimate=cost(a.size, a.size * 6),
        name=name,
    )(a, b)


def finish(name, flag, parts, begin, rows_all, into=None):
    rows, columns = parts[0].shape
    blocks = columns // BLOCK
    steps = 2 if blocks % 16 == 0 else 1
    per = blocks // steps
    count = len(parts)
    flags = () if flag is None else (flag,)

    def kernel(*refs):
        if flags:
            chosen = refs[0][0] == 1
            refs = refs[1:]
        out_ref, scale_ref = refs[-2:]
        lane = lax.broadcasted_iota(jnp.int32, (rows, HD), 1)
        scales = jnp.zeros((rows, HD), F32)
        for block in range(per):
            at = slice(block * BLOCK, (block + 1) * BLOCK)
            terms = [ref[:, at].astype(F32) for ref in refs[:count]]
            if flags:
                terms = [jnp.where(chosen, terms[0], terms[1])] + terms[2:]
            total = functools.reduce(jnp.add, terms)
            scale = jnp.max(jnp.abs(total), axis=1, keepdims=True) + 1e-06
            out_ref[:, at] = (total / scale).astype(BF16)
            scales = jnp.where(lane == block, scale, scales)
        scale_ref[...] = scales.T[:per]

    part_spec = pl.BlockSpec((rows, columns // steps), lambda i: (0, i))
    into = () if into is None else into
    return pl.pallas_call(
        kernel,
        out_shape=(
            jax.ShapeDtypeStruct((rows_all, columns), BF16),
            jax.ShapeDtypeStruct((blocks, rows_all), F32),
        ),
        grid=(steps,),
        in_specs=[SMEM] * len(flags) + [part_spec] * count + [pl.BlockSpec(memory_space=pl.ANY)] * len(into),
        out_specs=(
            pl.BlockSpec((rows, columns // steps), lambda i: (begin // rows, i)),
            pl.BlockSpec((per, rows), lambda i: (i, begin // rows)),
        ),
        input_output_aliases={len(flags) + count: 0, len(flags) + count + 1: 1} if into else {},
        compiler_params=PARAMS_LESS,
        cost_estimate=cost(rows * columns * 6, rows * columns * 2 * (count + 1)),
        name=name,
    )(*flags, *parts, *into)


def after(value, *others):
    return lax.optimization_barrier((value, *others))[0]


def local(
    queries, new_keys, new_values, key_cache, value_cache, prefix_len, stretch_start, out_weight
):
    rows = queries.shape[0]
    heads_here = queries.shape[1] // HD
    group = HQ // KVH
    tensor_pos = lax.axis_index("tensor")
    lanes = lax.axis_size("tensor")
    n_seq, n_pipe = lax.axis_size("seq"), lax.axis_size("pipe")
    shards = n_seq * n_pipe
    assert heads_here <= group
    me = lax.axis_index("seq") * n_pipe + lax.axis_index("pipe")
    own = pack(prefix_len, key_cache, value_cache, new_keys, new_values, heads_here)

    positions = stretch_start[0] + jnp.arange(shards * rows, dtype=jnp.int32)
    lane = jnp.arange(HD)
    freq = 500000.0 ** (-((lane % (HD // 2)).astype(F32) * 2.0 / HD))
    angle = positions.astype(F32)[:, None] * freq[None, :]
    tables = [jnp.cos(angle), jnp.sin(angle) * jnp.where(lane < HD // 2, -1.0, 1.0)[None, :]]

    columns = D // lanes
    step = jnp.arange(lanes, dtype=jnp.int32)
    if n_seq == 2 and n_pipe == 2 and lanes == 4:
        order = jnp.where(tensor_pos < 2, 3 - step, step)
        flag = ((tensor_pos == 0) | (tensor_pos == lanes - 1)).astype(jnp.int32).reshape(1)
        inward = [(0, 1), (3, 2)]
        middle = [(1, 2), (2, 1)]
        outward = [(1, 0), (2, 3)]
        swap = [(0, 1), (1, 0)]
        far = lax.ppermute(own, "seq", swap)
        near = lax.ppermute(own, "pipe", swap)
        place = jnp.stack([me, order[0], me, me ^ 1, me ^ 2, me ^ 3]).astype(jnp.int32)
        acc, stats, query, w_held = attend(
            "attend_near",
            place,
            queries,
            tables,
            [own, near],
            (0, 1),
            None,
            False,
            weight=out_weight,
            chunk=columns,
        )
        far = after(far, stats)
        cross = lax.ppermute(far, "pipe", swap)
        cut = rows // 2
        state = attend(
            "attend_far", place, query, tables, [far], (2,), (acc, stats), False, span=(0, cut)
        )
        attended, first_part = [None, None], [None, None]
        attended[0], first_part[0] = attend(
            "attend_cross",
            place,
            query,
            tables,
            [cross],
            (3,),
            tuple(state),
            True,
            weight=w_held,
            chunk=columns,
            span=(0, cut),
        )
        attended[1], first_part[1] = attend(
            "attend_rest",
            place,
            query,
            tables,
            [far, cross],
            (2, 3),
            (acc, after(stats, first_part[0])),
            True,
            weight=w_held,
            chunk=columns,
            span=(cut, cut),
            held=cut,
        )
        part = [first_part]
        part.append(project("project_1", order, 1, attended, out_weight, columns))
        third = project("project_3", order, 3, attended, out_weight, columns)
        rest = [attended[0], after(attended[1], third[0])]
        part += [project("project_2", order, 2, rest, out_weight, columns), third]
        come = [[None, None] for k in range(3)]
        for i in range(2):
            come[0][i] = lax.ppermute(part[0][i], "tensor", inward)
        part[1] = [part[1][0], after(part[1][1], come[0][0])]
        come[1] = [lax.ppermute(p, "tensor", inward) for p in part[1]]
        part[2] = [part[2][0], after(part[2][1], come[1][0])]
        come[2] = [lax.ppermute(p, "tensor", inward) for p in part[2]]
        done = None
        previous = part[1][0]
        for i in range(2):
            previous = added(f"add_0{i}", part[0][i], after(come[0][i], previous))
            across = lax.ppermute(previous, "tensor", middle)
            second = lax.ppermute(added(f"add_1{i}", part[1][i], come[1][i] if i == 0 else after(come[1][i], back)), "tensor", middle)
            back = lax.ppermute(added(f"add_3{i}", part[3][i], across), "tensor", outward)
            parts = [part[3][i], part[2][i], come[2][i], second, back]
            done = finish(f"finish_{i}", flag, parts, i * cut, rows, done)
        return done[0], done[1].T
    every = lax.all_gather(own, ("seq", "pipe"), axis=0)
    place = jnp.concatenate([jnp.stack([me, me]), jnp.arange(shards)]).astype(jnp.int32)
    state = None
    query = queries
    for shard in range(shards):
        state = attend(
            "attend", place, query, tables, [every[shard]], (shard,), state, shard == shards - 1
        )
        if shard == 0:
            query = state[2]
            state = state[:2]
    partial = [
        project(f"project_{k}", step, k, state[:1], out_weight, columns)[0] for k in range(lanes)
    ]
    total = lax.psum_scatter(jnp.stack(partial), "tensor", scatter_dimension=0, tiled=True)[0]
    values, scales = finish("finish", None, [total], 0, rows)
    return values, scales.T


def solution(mesh):
    return jax.shard_map(
        local,
        mesh=mesh,
        in_specs=(
            P(("groups", "seq", "pipe"), "tensor"),
            P(("groups", "seq", "pipe"), None),
            P(("groups", "seq", "pipe"), None),
            P(None, ("groups", "seq", "pipe"), None),
            P(None, ("groups", "seq", "pipe"), None),
            P(("groups", "seq", "pipe")),
            P("groups"),
            P("tensor", None),
        ),
        out_specs=(P(("groups", "seq", "pipe"), "tensor"), P(("groups", "seq", "pipe"), "tensor")),
        check_vma=False,
    )
```

```python
import functools
import math

import jax
import jax.numpy as jnp
from jax import lax
from jax.experimental import pallas as pl
from jax.experimental.pallas import tpu as pltpu
from jax.sharding import PartitionSpec as P

D = 8192
HD = 128
HQ = 32
KVH = 4
BLOCK = 128
LEN_ROWS = 16
LOW = 32
W_COPIES = 8
HEADS_PER_STEP = 4
NEG = -1e30
VMEM_LIMIT = 44 * 1024 * 1024
VMEM_MOST = 60 * 1024 * 1024
F32 = jnp.float32
BF16 = jnp.bfloat16
NT = (((1,), (1,)), ((), ()))


SMEM = pl.BlockSpec(memory_space=pltpu.SMEM)
VMEM = pl.BlockSpec(memory_space=pltpu.VMEM)
HBM = pl.BlockSpec(memory_space=pltpu.HBM)
PARAMS = pltpu.CompilerParams(vmem_limit_bytes=VMEM_LIMIT)
PARAMS_LESS = pltpu.CompilerParams(vmem_limit_bytes=28 * 1024 * 1024)
PARAMS_MOST = pltpu.CompilerParams(vmem_limit_bytes=VMEM_MOST)


def cost(flops, nbytes, transcendentals=0):
    return pl.CostEstimate(
        flops=int(flops), bytes_accessed=int(nbytes), transcendentals=int(transcendentals)
    )


def rotated(x, cosine, sine):
    return x * cosine + pltpu.roll(x, HD // 2, 1) * sine


def pack_kernel(per_kv_head, heads_here, len_ref, k_ref, v_ref, nk_ref, nv_ref, out_ref, sems):
    slots, rows = k_ref.shape[1], nk_ref.shape[0]
    head = lax.axis_index("tensor") * heads_here // per_kv_head
    columns = pl.ds(pl.multiple_of(head * HD, HD), HD)
    copies = []
    for i, (cache, new) in enumerate(((k_ref, nk_ref), (v_ref, nv_ref))):
        copies.append((cache.at[head], out_ref.at[i, pl.ds(0, slots)]))
        copies.append((new.at[:, columns], out_ref.at[i, pl.ds(slots, rows)]))
    copies = [pltpu.make_async_copy(*pair, sems.at[i]) for i, pair in enumerate(copies)]
    for copy in copies:
        copy.start()
    live = len_ref[0]
    for i, part in enumerate((live // LOW, live % LOW)):
        part = jnp.full((LEN_ROWS, HD), part.astype(F32), F32).astype(BF16)
        out_ref[i, slots + rows :] = part
    for copy in copies:
        copy.wait()


def pack(prefix_len, key_cache, value_cache, new_keys, new_values, heads_here):
    size = key_cache.shape[1] + new_keys.shape[0] + LEN_ROWS
    return pl.pallas_call(
        functools.partial(pack_kernel, HQ // KVH, heads_here),
        out_shape=jax.ShapeDtypeStruct((2, size, HD), BF16),
        in_specs=[SMEM, HBM, HBM, HBM, HBM],
        out_specs=VMEM,
        scratch_shapes=[pltpu.SemaphoreType.DMA((4,))],
        compiler_params=PARAMS_MOST,
        cost_estimate=cost(0, 4 * size * HD * 2),
        name="pack",
    )(prefix_len, key_cache, value_cache, new_keys, new_values)


def lane_max(x):
    parts = [x[:, i : i + HD] for i in range(0, x.shape[1], HD)]
    return functools.reduce(jnp.maximum, parts)


def lane_sum(x):
    parts = [x[:, i : i + HD] for i in range(0, x.shape[1], HD)]
    return functools.reduce(jnp.add, parts)


def attend_kernel(
    first, last, chunk, slots, shards_at, span, held, place_ref, q_ref, cos_ref, sin_ref, *refs
):
    n = len(shards_at)
    kv_refs = refs[:n]
    refs = refs[n:]
    rows = q_ref.shape[0]
    heads = q_ref.shape[1] // HD
    begin_row, n_rows = span
    at_rows = slice(begin_row, begin_row + n_rows)
    at_held = slice(held, held + n_rows)
    me = place_ref[0]
    if first:
        if chunk:
            w_ref, acc_out, stats_out, query_out, w_held, raw, sem, sems = refs
            columns = pl.ds(pl.multiple_of(place_ref[1] * chunk, chunk), chunk)
            depth = w_ref.shape[0] // W_COPIES
            copies = []
            for i in range(W_COPIES):
                at = pl.ds(i * depth, depth)
                copies.append(pltpu.make_async_copy(w_ref.at[at, columns], w_held.at[at], sems.at[i]))
        else:
            acc_out, stats_out, query_out, raw, sem = refs
            copies = []
        copy = pltpu.make_async_copy(q_ref, raw, sem)
        copy.start()
        for other in copies:
            other.start()
    else:
        acc_in, stats_in = refs[:2]
        refs = refs[2:]
        if chunk:
            w_held, attended_out, part_out = refs
        elif last:
            (attended_out,) = refs
        else:
            acc_out, stats_out = refs
    row = lax.broadcasted_iota(jnp.int32, (n_rows, rows), 0) + begin_row
    column = lax.broadcasted_iota(jnp.int32, (n_rows, rows), 1)
    slot = lax.broadcasted_iota(jnp.int32, (1, HD), 1).astype(F32)
    segments = []
    for ref, at in zip(kv_refs, shards_at):
        shard = place_ref[2 + at]
        high = ref[0, slots + rows :, :].astype(F32)
        live = (high * LOW + ref[1, slots + rows :, :].astype(F32))[:1, :]
        pieces = [jnp.where(slot + float(i) < live, 0.0, NEG) for i in range(0, slots, HD)]
        segments.append((ref, None, 0, slots, jnp.concatenate(pieces, axis=1)))
        table = pl.ds(pl.multiple_of(shard * rows, rows), rows)
        keys = rotated(ref[0, slots : slots + rows, :].astype(F32), cos_ref[table], sin_ref[table])
        mask = jnp.where(column <= row + (me - shard) * rows, 0.0, NEG)
        segments.append((ref, keys.astype(BF16), slots, rows, mask))
    if first:
        factor = math.log2(math.e) / math.sqrt(HD)
        table = pl.ds(pl.multiple_of(me * rows, rows), rows)
        cosine = cos_ref[table] * factor
        sine = sin_ref[table] * factor
        copy.wait()
        for head in range(heads):
            at = slice(head * HD, (head + 1) * HD)
            query_out[:, at] = rotated(raw[:, at].astype(F32), cosine, sine).astype(BF16)
        q_ref = query_out

    lane = lax.broadcasted_iota(jnp.int32, (n_rows, HD), 1)
    per_step = heads if first else min(heads, HEADS_PER_STEP)

    def columns_of(head):
        return pl.ds(head * HD if first else pl.multiple_of(head * HD, HD), HD)

    def score(head):
        query = q_ref[at_rows, columns_of(head)]
        scores = []
        for ref, keys, begin, count, mask in segments:
            keys = ref[0, begin : begin + count, :] if keys is None else keys
            scores.append(lax.dot_general(query, keys, NT, preferred_element_type=F32) + mask)
        return scores

    def step(index, stats):
        head = index * per_step
        following = score(head)
        for i in range(per_step):
            scores = following
            if i + 1 < per_step:
                following = score(head + 1)
            at = columns_of(head)
            peak = functools.reduce(jnp.maximum, [lane_max(x) for x in scores])
            peak = jnp.max(peak, axis=1, keepdims=True)
            if not first:
                held_stats = stats_in[at_held, :]
                before = jnp.max(jnp.where(lane == head, held_stats, -jnp.inf), axis=1, keepdims=True)
                sums = jnp.where(lane == HD // 2 + head, held_stats, 0.0)
                sums = jnp.sum(sums, axis=1, keepdims=True)
                peak = jnp.maximum(before, peak)
                shrink = jnp.exp2(before - peak)
            total = None
            out = None
            for (ref, keys, begin, count, mask), part in zip(segments, scores):
                weights = jnp.exp2(part - peak)
                subtotal = lane_sum(weights)
                total = subtotal if total is None else total + subtotal
                values = ref[1, begin : begin + count, :]
                update = jnp.dot(weights.astype(BF16), values, preferred_element_type=F32)
                out = update if out is None else out + update
            total = jnp.sum(total, axis=1, keepdims=True)
            if not first:
                total = total + sums * shrink
                out = out + acc_in[at_held, at] * shrink
            if last:
                attended_out[:, at] = (out / total).astype(BF16)
            else:
                acc_out[:, at] = out
                stats = jnp.where(lane == head, peak, stats)
                stats = jnp.where(lane == HD // 2 + head, total, stats)
            head = head + 1
        return stats

    stats = jnp.zeros((n_rows, HD), F32)
    if per_step == heads:
        stats = step(0, stats)
    else:
        stats = lax.fori_loop(0, heads // per_step, step, stats)
    if not last:
        stats_out[...] = stats
    if first:
        for other in copies:
            other.wait()
    elif chunk:
        tile = 512
        for i in range(0, chunk, tile):
            part = jnp.dot(attended_out[...], w_held[:, i : i + tile], preferred_element_type=F32)
            part_out[:, i : i + tile] = part.astype(BF16)


def attend(
    name, place, query, tables, arrays, shards_at, state, last, weight=None, chunk=0, span=None, held=0
):
    rows, width = query.shape
    slots = arrays[0].shape[1] - rows - LEN_ROWS
    span = (0, rows) if span is None else span
    first = state is None
    operands = [place, query, *tables, *arrays]
    in_specs = [SMEM, HBM if first else VMEM] + [VMEM] * (2 + len(arrays))
    scratch = []
    if first:
        scratch = [pltpu.VMEM((rows, width), BF16), pltpu.SemaphoreType.DMA]
    else:
        operands += state
        in_specs += [VMEM] * 2
    if chunk:
        operands.append(weight)
        in_specs.append(HBM if first else VMEM)
    if last:
        out_shape = [jax.ShapeDtypeStruct((span[1], width), BF16)]
        if chunk:
            out_shape.append(jax.ShapeDtypeStruct((span[1], chunk), BF16))
    else:
        out_shape = [
            jax.ShapeDtypeStruct((span[1], width), F32),
            jax.ShapeDtypeStruct((span[1], HD), F32),
        ]
        if first:
            out_shape.append(jax.ShapeDtypeStruct((rows, width), BF16))
            if chunk:
                out_shape.append(jax.ShapeDtypeStruct((width, chunk), BF16))
                scratch.append(pltpu.SemaphoreType.DMA((W_COPIES,)))
    keys = len(arrays) * (slots + rows)
    return pl.pallas_call(
        functools.partial(attend_kernel, first, last, chunk, slots, shards_at, span, held),
        out_shape=out_shape,
        in_specs=in_specs,
        out_specs=[VMEM] * len(out_shape),
        scratch_shapes=scratch,
        compiler_params=PARAMS if first else PARAMS_LESS,
        cost_estimate=cost(
            rows * width * keys // 2, rows * width, rows * (width // HD) * keys // 8
        ),
        name=name,
    )(*operands)


def project_kernel(pieces, order_ref, *refs):
    x = jnp.concatenate([ref[...] for ref in refs[:pieces]], axis=0)
    out = jnp.dot(x, refs[pieces][...], preferred_element_type=F32)
    cut = refs[0].shape[0]
    for i, ref in enumerate(refs[pieces + 1 :]):
        ref[...] = out[i * cut : (i + 1) * cut].astype(BF16)


def project(name, order, at, attended, out_weight, chunk, tile=512):
    cut, depth = attended[0].shape
    pieces = len(attended)
    tile = min(tile, chunk)
    per = chunk // tile
    return pl.pallas_call(
        functools.partial(project_kernel, pieces),
        out_shape=(jax.ShapeDtypeStruct((cut, chunk), BF16),) * pieces,
        grid_spec=pltpu.PrefetchScalarGridSpec(
            num_scalar_prefetch=1,
            grid=(per,),
            in_specs=[pl.BlockSpec((cut, depth), lambda j, order: (0, 0))] * pieces
            + [pl.BlockSpec((depth, tile), lambda j, order: (0, order[at] * per + j))],
            out_specs=(pl.BlockSpec((cut, tile), lambda j, order: (0, j)),) * pieces,
        ),
        compiler_params=PARAMS,
        cost_estimate=cost(2 * pieces * cut * depth * chunk, depth * chunk * 2),
        name=name,
    )(order, *attended, out_weight)


def add_kernel(a_ref, b_ref, out_ref):
    out_ref[...] = (a_ref[...].astype(F32) + b_ref[...].astype(F32)).astype(BF16)


def added(name, a, b):
    return pl.pallas_call(
        add_kernel,
        out_shape=jax.ShapeDtypeStruct(a.shape, BF16),
        in_specs=[VMEM, VMEM],
        out_specs=VMEM,
        compiler_params=PARAMS_LESS,
        cost_estimate=cost(a.size, a.size * 6),
        name=name,
    )(a, b)


def gather_kernel(flag_ref, first_ref, second_ref, a_ref, b_ref, out_ref):
    own = jnp.where(flag_ref[0] == 1, first_ref[...].astype(F32), second_ref[...].astype(F32))
    out_ref[...] = own + (a_ref[...].astype(F32) + b_ref[...].astype(F32))


def gathered(name, flag, first, second, a, b):
    return pl.pallas_call(
        gather_kernel,
        out_shape=jax.ShapeDtypeStruct(a.shape, F32),
        in_specs=[SMEM] + [VMEM] * 4,
        out_specs=VMEM,
        compiler_params=PARAMS_LESS,
        cost_estimate=cost(a.size * 3, a.size * 12),
        name=name,
    )(flag, first, second, a, b)


def finish(name, flag, parts, begin, rows_all, into=None):
    rows, columns = parts[0].shape
    blocks = columns // BLOCK
    steps = 2 if blocks % 16 == 0 else 1
    per = blocks // steps
    count = len(parts)
    flags = () if flag is None else (flag,)

    def kernel(*refs):
        if flags:
            chosen = refs[0][0] == 1
            refs = refs[1:]
        out_ref, scale_ref = refs[-2:]
        lane = lax.broadcasted_iota(jnp.int32, (rows, HD), 1)
        scales = jnp.zeros((rows, HD), F32)
        for block in range(per):
            at = slice(block * BLOCK, (block + 1) * BLOCK)
            terms = [ref[:, at].astype(F32) for ref in refs[:count]]
            if flags:
                terms = [jnp.where(chosen, terms[0], terms[1])] + terms[2:]
            total = functools.reduce(jnp.add, terms)
            scale = jnp.max(jnp.abs(total), axis=1, keepdims=True) + 1e-06
            out_ref[:, at] = (total / scale).astype(BF16)
            scales = jnp.where(lane == block, scale, scales)
        scale_ref[...] = scales.T[:per]

    part_spec = pl.BlockSpec((rows, columns // steps), lambda i: (0, i))
    into = () if into is None else into
    return pl.pallas_call(
        kernel,
        out_shape=(
            jax.ShapeDtypeStruct((rows_all, columns), BF16),
            jax.ShapeDtypeStruct((blocks, rows_all), F32),
        ),
        grid=(steps,),
        in_specs=[SMEM] * len(flags) + [part_spec] * count + [pl.BlockSpec(memory_space=pl.ANY)] * len(into),
        out_specs=(
            pl.BlockSpec((rows, columns // steps), lambda i: (begin // rows, i)),
            pl.BlockSpec((per, rows), lambda i: (i, begin // rows)),
        ),
        input_output_aliases={len(flags) + count: 0, len(flags) + count + 1: 1} if into else {},
        compiler_params=PARAMS_LESS,
        cost_estimate=cost(rows * columns * 6, rows * columns * 2 * (count + 1)),
        name=name,
    )(*flags, *parts, *into)


def after(value, *others):
    return lax.optimization_barrier((value, *others))[0]


def local(
    queries, new_keys, new_values, key_cache, value_cache, prefix_len, stretch_start, out_weight
):
    rows = queries.shape[0]
    heads_here = queries.shape[1] // HD
    group = HQ // KVH
    tensor_pos = lax.axis_index("tensor")
    lanes = lax.axis_size("tensor")
    n_seq, n_pipe = lax.axis_size("seq"), lax.axis_size("pipe")
    shards = n_seq * n_pipe
    assert heads_here <= group
    me = lax.axis_index("seq") * n_pipe + lax.axis_index("pipe")
    own = pack(prefix_len, key_cache, value_cache, new_keys, new_values, heads_here)

    positions = stretch_start[0] + jnp.arange(shards * rows, dtype=jnp.int32)
    lane = jnp.arange(HD)
    freq = 500000.0 ** (-((lane % (HD // 2)).astype(F32) * 2.0 / HD))
    angle = positions.astype(F32)[:, None] * freq[None, :]
    tables = [jnp.cos(angle), jnp.sin(angle) * jnp.where(lane < HD // 2, -1.0, 1.0)[None, :]]

    columns = D // lanes
    step = jnp.arange(lanes, dtype=jnp.int32)
    if n_seq == 2 and n_pipe == 2 and lanes == 4:
        order = jnp.where(tensor_pos < 2, 3 - step, step)
        flag = ((tensor_pos == 0) | (tensor_pos == lanes - 1)).astype(jnp.int32).reshape(1)
        inward = [(0, 1), (3, 2)]
        middle = [(1, 2), (2, 1)]
        outward = [(1, 0), (2, 3)]
        swap = [(0, 1), (1, 0)]
        far = lax.ppermute(own, "seq", swap)
        near = lax.ppermute(own, "pipe", swap)
        place = jnp.stack([me, order[0], me, me ^ 1, me ^ 2, me ^ 3]).astype(jnp.int32)
        acc, stats, query, w_held = attend(
            "attend_near",
            place,
            queries,
            tables,
            [own, near],
            (0, 1),
            None,
            False,
            weight=out_weight,
            chunk=columns,
        )
        far = after(far, stats)
        cross = lax.ppermute(far, "pipe", swap)
        cut = rows // 2
        state = attend(
            "attend_far", place, query, tables, [far], (2,), (acc, stats), False, span=(0, cut)
        )
        attended, first_part = [None, None], [None, None]
        attended[0], first_part[0] = attend(
            "attend_cross",
            place,
            query,
            tables,
            [cross],
            (3,),
            tuple(state),
            True,
            weight=w_held,
            chunk=columns,
            span=(0, cut),
        )
        attended[1], first_part[1] = attend(
            "attend_rest",
            place,
            query,
            tables,
            [far, cross],
            (2, 3),
            (acc, after(stats, first_part[0])),
            True,
            weight=w_held,
            chunk=columns,
            span=(cut, cut),
            held=cut,
        )
        part = [first_part]
        part.append(project("project_1", order, 1, attended, out_weight, columns))
        third = project("project_3", order, 3, attended, out_weight, columns)
        rest = [attended[0], after(attended[1], third[0])]
        part += [project("project_2", order, 2, rest, out_weight, columns), third]
        come = [[None, None] for k in range(3)]
        for i in range(2):
            come[0][i] = lax.ppermute(part[0][i], "tensor", inward)
        part[1] = [part[1][0], after(part[1][1], come[0][0])]
        come[1] = [lax.ppermute(p, "tensor", inward) for p in part[1]]
        part[2] = [part[2][0], after(part[2][1], come[1][0])]
        come[2] = [lax.ppermute(p, "tensor", inward) for p in part[2]]
        done = None
        previous = part[1][0]
        for i in range(2):
            previous = added(f"add_0{i}", part[0][i], after(come[0][i], previous))
            across = lax.ppermute(previous, "tensor", middle)
            second = lax.ppermute(added(f"add_1{i}", part[1][i], come[1][i] if i == 0 else after(come[1][i], back)), "tensor", middle)
            back = lax.ppermute(added(f"add_3{i}", part[3][i], across), "tensor", outward)
            parts = [part[3][i], part[2][i], come[2][i], second, back]
            if i == 1:
                most = gathered("gather", flag, *parts[:2], *parts[3:])
                done = finish("finish_1", None, [most, after(come[2][1], most)], cut, rows, done)
            else:
                done = finish("finish_0", flag, parts, 0, rows, done)
        return done[0], done[1].T
    every = lax.all_gather(own, ("seq", "pipe"), axis=0)
    place = jnp.concatenate([jnp.stack([me, me]), jnp.arange(shards)]).astype(jnp.int32)
    state = None
    query = queries
    for shard in range(shards):
        state = attend(
            "attend", place, query, tables, [every[shard]], (shard,), state, shard == shards - 1
        )
        if shard == 0:
            query = state[2]
            state = state[:2]
    partial = [
        project(f"project_{k}", step, k, state[:1], out_weight, columns)[0] for k in range(lanes)
    ]
    total = lax.psum_scatter(jnp.stack(partial), "tensor", scatter_dimension=0, tiled=True)[0]
    values, scales = finish("finish", None, [total], 0, rows)
    return values, scales.T


def solution(mesh):
    return jax.shard_map(
        local,
        mesh=mesh,
        in_specs=(
            P(("groups", "seq", "pipe"), "tensor"),
            P(("groups", "seq", "pipe"), None),
            P(("groups", "seq", "pipe"), None),
            P(None, ("groups", "seq", "pipe"), None),
            P(None, ("groups", "seq", "pipe"), None),
            P(("groups", "seq", "pipe")),
            P("groups"),
            P("tensor", None),
        ),
        out_specs=(P(("groups", "seq", "pipe"), "tensor"), P(("groups", "seq", "pipe"), "tensor")),
        check_vma=False,
    )
```

```python
import functools
import math

import jax
import jax.numpy as jnp
from jax import lax
from jax.experimental import pallas as pl
from jax.experimental.pallas import tpu as pltpu
from jax.sharding import PartitionSpec as P

D = 8192
HD = 128
HQ = 32
KVH = 4
BLOCK = 128
LEN_ROWS = 16
LOW = 32
W_COPIES = 8
HEADS_PER_STEP = 4
NEG = -1e30
VMEM_LIMIT = 44 * 1024 * 1024
VMEM_MOST = 60 * 1024 * 1024
F32 = jnp.float32
BF16 = jnp.bfloat16
NT = (((1,), (1,)), ((), ()))


SMEM = pl.BlockSpec(memory_space=pltpu.SMEM)
VMEM = pl.BlockSpec(memory_space=pltpu.VMEM)
HBM = pl.BlockSpec(memory_space=pltpu.HBM)
PARAMS = pltpu.CompilerParams(vmem_limit_bytes=VMEM_LIMIT)
PARAMS_LESS = pltpu.CompilerParams(vmem_limit_bytes=28 * 1024 * 1024)
PARAMS_MOST = pltpu.CompilerParams(vmem_limit_bytes=VMEM_MOST)


def cost(flops, nbytes, transcendentals=0):
    return pl.CostEstimate(
        flops=int(flops), bytes_accessed=int(nbytes), transcendentals=int(transcendentals)
    )


def rotated(x, cosine, sine):
    return x * cosine + pltpu.roll(x, HD // 2, 1) * sine


def pack_kernel(per_kv_head, heads_here, len_ref, k_ref, v_ref, nk_ref, nv_ref, out_ref, sems):
    slots, rows = k_ref.shape[1], nk_ref.shape[0]
    head = lax.axis_index("tensor") * heads_here // per_kv_head
    columns = pl.ds(pl.multiple_of(head * HD, HD), HD)
    copies = []
    for i, (cache, new) in enumerate(((k_ref, nk_ref), (v_ref, nv_ref))):
        copies.append((cache.at[head], out_ref.at[i, pl.ds(0, slots)]))
        copies.append((new.at[:, columns], out_ref.at[i, pl.ds(slots, rows)]))
    copies = [pltpu.make_async_copy(*pair, sems.at[i]) for i, pair in enumerate(copies)]
    for copy in copies:
        copy.start()
    live = len_ref[0]
    for i, part in enumerate((live // LOW, live % LOW)):
        part = jnp.full((LEN_ROWS, HD), part.astype(F32), F32).astype(BF16)
        out_ref[i, slots + rows :] = part
    for copy in copies:
        copy.wait()


def pack(prefix_len, key_cache, value_cache, new_keys, new_values, heads_here):
    size = key_cache.shape[1] + new_keys.shape[0] + LEN_ROWS
    return pl.pallas_call(
        functools.partial(pack_kernel, HQ // KVH, heads_here),
        out_shape=jax.ShapeDtypeStruct((2, size, HD), BF16),
        in_specs=[SMEM, HBM, HBM, HBM, HBM],
        out_specs=VMEM,
        scratch_shapes=[pltpu.SemaphoreType.DMA((4,))],
        compiler_params=PARAMS_MOST,
        cost_estimate=cost(0, 4 * size * HD * 2),
        name="pack",
    )(prefix_len, key_cache, value_cache, new_keys, new_values)


def lane_max(x):
    parts = [x[:, i : i + HD] for i in range(0, x.shape[1], HD)]
    return functools.reduce(jnp.maximum, parts)


def lane_sum(x):
    parts = [x[:, i : i + HD] for i in range(0, x.shape[1], HD)]
    return functools.reduce(jnp.add, parts)


def attend_kernel(
    first, last, chunk, slots, shards_at, span, held, place_ref, q_ref, cos_ref, sin_ref, *refs
):
    n = len(shards_at)
    kv_refs = refs[:n]
    refs = refs[n:]
    rows = q_ref.shape[0]
    heads = q_ref.shape[1] // HD
    begin_row, n_rows = span
    at_rows = slice(begin_row, begin_row + n_rows)
    at_held = slice(held, held + n_rows)
    me = place_ref[0]
    if first:
        if chunk:
            w_ref, acc_out, stats_out, query_out, w_held, raw, sem, sems = refs
            columns = pl.ds(pl.multiple_of(place_ref[1] * chunk, chunk), chunk)
            depth = w_ref.shape[0] // W_COPIES
            copies = []
            for i in range(W_COPIES):
                at = pl.ds(i * depth, depth)
                copies.append(pltpu.make_async_copy(w_ref.at[at, columns], w_held.at[at], sems.at[i]))
        else:
            acc_out, stats_out, query_out, raw, sem = refs
            copies = []
        copy = pltpu.make_async_copy(q_ref, raw, sem)
        copy.start()
        for other in copies:
            other.start()
    else:
        acc_in, stats_in = refs[:2]
        refs = refs[2:]
        if chunk:
            w_held, attended_out, part_out = refs
        elif last:
            (attended_out,) = refs
        else:
            acc_out, stats_out = refs
    row = lax.broadcasted_iota(jnp.int32, (n_rows, rows), 0) + begin_row
    column = lax.broadcasted_iota(jnp.int32, (n_rows, rows), 1)
    slot = lax.broadcasted_iota(jnp.int32, (1, HD), 1).astype(F32)
    segments = []
    for ref, at in zip(kv_refs, shards_at):
        shard = place_ref[2 + at]
        high = ref[0, slots + rows :, :].astype(F32)
        live = (high * LOW + ref[1, slots + rows :, :].astype(F32))[:1, :]
        pieces = [jnp.where(slot + float(i) < live, 0.0, NEG) for i in range(0, slots, HD)]
        segments.append((ref, None, 0, slots, jnp.concatenate(pieces, axis=1)))
        table = pl.ds(pl.multiple_of(shard * rows, rows), rows)
        keys = rotated(ref[0, slots : slots + rows, :].astype(F32), cos_ref[table], sin_ref[table])
        mask = jnp.where(column <= row + (me - shard) * rows, 0.0, NEG)
        segments.append((ref, keys.astype(BF16), slots, rows, mask))
    if first:
        factor = math.log2(math.e) / math.sqrt(HD)
        table = pl.ds(pl.multiple_of(me * rows, rows), rows)
        cosine = cos_ref[table] * factor
        sine = sin_ref[table] * factor
        copy.wait()
        for head in range(heads):
            at = slice(head * HD, (head + 1) * HD)
            query_out[:, at] = rotated(raw[:, at].astype(F32), cosine, sine).astype(BF16)
        q_ref = query_out

    lane = lax.broadcasted_iota(jnp.int32, (n_rows, HD), 1)
    per_step = heads if first else min(heads, HEADS_PER_STEP)

    def columns_of(head):
        return pl.ds(head * HD if first else pl.multiple_of(head * HD, HD), HD)

    def score(head):
        query = q_ref[at_rows, columns_of(head)]
        scores = []
        for ref, keys, begin, count, mask in segments:
            keys = ref[0, begin : begin + count, :] if keys is None else keys
            scores.append(lax.dot_general(query, keys, NT, preferred_element_type=F32) + mask)
        return scores

    def step(index, stats):
        head = index * per_step
        following = score(head)
        for i in range(per_step):
            scores = following
            if i + 1 < per_step:
                following = score(head + 1)
            at = columns_of(head)
            peak = functools.reduce(jnp.maximum, [lane_max(x) for x in scores])
            peak = jnp.max(peak, axis=1, keepdims=True)
            if not first:
                held_stats = stats_in[at_held, :]
                before = jnp.max(jnp.where(lane == head, held_stats, -jnp.inf), axis=1, keepdims=True)
                sums = jnp.where(lane == HD // 2 + head, held_stats, 0.0)
                sums = jnp.sum(sums, axis=1, keepdims=True)
                peak = jnp.maximum(before, peak)
                shrink = jnp.exp2(before - peak)
            total = None
            out = None
            for (ref, keys, begin, count, mask), part in zip(segments, scores):
                weights = jnp.exp2(part - peak)
                subtotal = lane_sum(weights)
                total = subtotal if total is None else total + subtotal
                values = ref[1, begin : begin + count, :]
                update = jnp.dot(weights.astype(BF16), values, preferred_element_type=F32)
                out = update if out is None else out + update
            total = jnp.sum(total, axis=1, keepdims=True)
            if not first:
                total = total + sums * shrink
                out = out + acc_in[at_held, at] * shrink
            if last:
                attended_out[:, at] = (out / total).astype(BF16)
            else:
                acc_out[:, at] = out
                stats = jnp.where(lane == head, peak, stats)
                stats = jnp.where(lane == HD // 2 + head, total, stats)
            head = head + 1
        return stats

    stats = jnp.zeros((n_rows, HD), F32)
    if per_step == heads:
        stats = step(0, stats)
    else:
        stats = lax.fori_loop(0, heads // per_step, step, stats)
    if not last:
        stats_out[...] = stats
    if first:
        for other in copies:
            other.wait()
    elif chunk:
        tile = 512
        for i in range(0, chunk, tile):
            part = jnp.dot(attended_out[...], w_held[:, i : i + tile], preferred_element_type=F32)
            part_out[:, i : i + tile] = part.astype(BF16)


def attend(
    name, place, query, tables, arrays, shards_at, state, last, weight=None, chunk=0, span=None, held=0
):
    rows, width = query.shape
    slots = arrays[0].shape[1] - rows - LEN_ROWS
    span = (0, rows) if span is None else span
    first = state is None
    operands = [place, query, *tables, *arrays]
    in_specs = [SMEM, HBM if first else VMEM] + [VMEM] * (2 + len(arrays))
    scratch = []
    if first:
        scratch = [pltpu.VMEM((rows, width), BF16), pltpu.SemaphoreType.DMA]
    else:
        operands += state
        in_specs += [VMEM] * 2
    if chunk:
        operands.append(weight)
        in_specs.append(HBM if first else VMEM)
    if last:
        out_shape = [jax.ShapeDtypeStruct((span[1], width), BF16)]
        if chunk:
            out_shape.append(jax.ShapeDtypeStruct((span[1], chunk), BF16))
    else:
        out_shape = [
            jax.ShapeDtypeStruct((span[1], width), F32),
            jax.ShapeDtypeStruct((span[1], HD), F32),
        ]
        if first:
            out_shape.append(jax.ShapeDtypeStruct((rows, width), BF16))
            if chunk:
                out_shape.append(jax.ShapeDtypeStruct((width, chunk), BF16))
                scratch.append(pltpu.SemaphoreType.DMA((W_COPIES,)))
    keys = len(arrays) * (slots + rows)
    return pl.pallas_call(
        functools.partial(attend_kernel, first, last, chunk, slots, shards_at, span, held),
        out_shape=out_shape,
        in_specs=in_specs,
        out_specs=[VMEM] * len(out_shape),
        scratch_shapes=scratch,
        compiler_params=PARAMS if first else PARAMS_LESS,
        cost_estimate=cost(
            rows * width * keys // 2, rows * width, rows * (width // HD) * keys // 8
        ),
        name=name,
    )(*operands)


def project_kernel(pieces, order_ref, *refs):
    x = jnp.concatenate([ref[...] for ref in refs[:pieces]], axis=0)
    out = jnp.dot(x, refs[pieces][...], preferred_element_type=F32)
    cut = refs[0].shape[0]
    for i, ref in enumerate(refs[pieces + 1 :]):
        ref[...] = out[i * cut : (i + 1) * cut].astype(BF16)


def project(name, order, at, attended, out_weight, chunk, tile=512):
    cut, depth = attended[0].shape
    pieces = len(attended)
    tile = min(tile, chunk)
    per = chunk // tile
    return pl.pallas_call(
        functools.partial(project_kernel, pieces),
        out_shape=(jax.ShapeDtypeStruct((cut, chunk), BF16),) * pieces,
        grid_spec=pltpu.PrefetchScalarGridSpec(
            num_scalar_prefetch=1,
            grid=(per,),
            in_specs=[pl.BlockSpec((cut, depth), lambda j, order: (0, 0))] * pieces
            + [pl.BlockSpec((depth, tile), lambda j, order: (0, order[at] * per + j))],
            out_specs=(pl.BlockSpec((cut, tile), lambda j, order: (0, j)),) * pieces,
        ),
        compiler_params=PARAMS,
        cost_estimate=cost(2 * pieces * cut * depth * chunk, depth * chunk * 2),
        name=name,
    )(order, *attended, out_weight)


def add_kernel(a_ref, b_ref, out_ref):
    out_ref[...] = (a_ref[...].astype(F32) + b_ref[...].astype(F32)).astype(BF16)


def added(name, a, b):
    return pl.pallas_call(
        add_kernel,
        out_shape=jax.ShapeDtypeStruct(a.shape, BF16),
        in_specs=[VMEM, VMEM],
        out_specs=VMEM,
        compiler_params=PARAMS_LESS,
        cost_estimate=cost(a.size, a.size * 6),
        name=name,
    )(a, b)


def gather_kernel(flag_ref, first_ref, second_ref, a_ref, b_ref, out_ref):
    own = jnp.where(flag_ref[0] == 1, first_ref[...].astype(F32), second_ref[...].astype(F32))
    out_ref[...] = own + (a_ref[...].astype(F32) + b_ref[...].astype(F32))


def gathered(name, flag, first, second, a, b):
    return pl.pallas_call(
        gather_kernel,
        out_shape=jax.ShapeDtypeStruct(a.shape, F32),
        in_specs=[SMEM] + [VMEM] * 4,
        out_specs=VMEM,
        compiler_params=PARAMS_LESS,
        cost_estimate=cost(a.size * 3, a.size * 12),
        name=name,
    )(flag, first, second, a, b)


def finish(name, flag, parts, begin, rows_all, into=None):
    rows, columns = parts[0].shape
    blocks = columns // BLOCK
    steps = 2 if blocks % 16 == 0 and flag is not None else 1
    per = blocks // steps
    count = len(parts)
    flags = () if flag is None else (flag,)

    def kernel(*refs):
        if flags:
            chosen = refs[0][0] == 1
            refs = refs[1:]
        out_ref, scale_ref = refs[-2:]
        lane = lax.broadcasted_iota(jnp.int32, (rows, HD), 1)
        scales = jnp.zeros((rows, HD), F32)
        for block in range(per):
            at = slice(block * BLOCK, (block + 1) * BLOCK)
            terms = [ref[:, at].astype(F32) for ref in refs[:count]]
            if flags:
                terms = [jnp.where(chosen, terms[0], terms[1])] + terms[2:]
            total = functools.reduce(jnp.add, terms)
            scale = jnp.max(jnp.abs(total), axis=1, keepdims=True) + 1e-06
            out_ref[:, at] = (total / scale).astype(BF16)
            scales = jnp.where(lane == block, scale, scales)
        scale_ref[...] = scales.T[:per]

    part_spec = pl.BlockSpec((rows, columns // steps), lambda i: (0, i))
    into = () if into is None else into
    return pl.pallas_call(
        kernel,
        out_shape=(
            jax.ShapeDtypeStruct((rows_all, columns), BF16),
            jax.ShapeDtypeStruct((blocks, rows_all), F32),
        ),
        grid=(steps,),
        in_specs=[SMEM] * len(flags) + [part_spec] * count + [pl.BlockSpec(memory_space=pl.ANY)] * len(into),
        out_specs=(
            pl.BlockSpec((rows, columns // steps), lambda i: (begin // rows, i)),
            pl.BlockSpec((per, rows), lambda i: (i, begin // rows)),
        ),
        input_output_aliases={len(flags) + count: 0, len(flags) + count + 1: 1} if into else {},
        compiler_params=PARAMS_LESS,
        cost_estimate=cost(rows * columns * 6, rows * columns * 2 * (count + 1)),
        name=name,
    )(*flags, *parts, *into)


def after(value, *others):
    return lax.optimization_barrier((value, *others))[0]


def local(
    queries, new_keys, new_values, key_cache, value_cache, prefix_len, stretch_start, out_weight
):
    rows = queries.shape[0]
    heads_here = queries.shape[1] // HD
    group = HQ // KVH
    tensor_pos = lax.axis_index("tensor")
    lanes = lax.axis_size("tensor")
    n_seq, n_pipe = lax.axis_size("seq"), lax.axis_size("pipe")
    shards = n_seq * n_pipe
    assert heads_here <= group
    me = lax.axis_index("seq") * n_pipe + lax.axis_index("pipe")
    own = pack(prefix_len, key_cache, value_cache, new_keys, new_values, heads_here)

    positions = stretch_start[0] + jnp.arange(shards * rows, dtype=jnp.int32)
    lane = jnp.arange(HD)
    freq = 500000.0 ** (-((lane % (HD // 2)).astype(F32) * 2.0 / HD))
    angle = positions.astype(F32)[:, None] * freq[None, :]
    tables = [jnp.cos(angle), jnp.sin(angle) * jnp.where(lane < HD // 2, -1.0, 1.0)[None, :]]

    columns = D // lanes
    step = jnp.arange(lanes, dtype=jnp.int32)
    if n_seq == 2 and n_pipe == 2 and lanes == 4:
        order = jnp.where(tensor_pos < 2, 3 - step, step)
        flag = ((tensor_pos == 0) | (tensor_pos == lanes - 1)).astype(jnp.int32).reshape(1)
        inward = [(0, 1), (3, 2)]
        middle = [(1, 2), (2, 1)]
        outward = [(1, 0), (2, 3)]
        swap = [(0, 1), (1, 0)]
        far = lax.ppermute(own, "seq", swap)
        near = lax.ppermute(own, "pipe", swap)
        place = jnp.stack([me, order[0], me, me ^ 1, me ^ 2, me ^ 3]).astype(jnp.int32)
        acc, stats, query, w_held = attend(
            "attend_near",
            place,
            queries,
            tables,
            [own, near],
            (0, 1),
            None,
            False,
            weight=out_weight,
            chunk=columns,
        )
        far = after(far, stats)
        cross = lax.ppermute(far, "pipe", swap)
        cut = rows // 2
        state = attend(
            "attend_far", place, query, tables, [far], (2,), (acc, stats), False, span=(0, cut)
        )
        attended, first_part = [None, None], [None, None]
        attended[0], first_part[0] = attend(
            "attend_cross",
            place,
            query,
            tables,
            [cross],
            (3,),
            tuple(state),
            True,
            weight=w_held,
            chunk=columns,
            span=(0, cut),
        )
        attended[1], first_part[1] = attend(
            "attend_rest",
            place,
            query,
            tables,
            [far, cross],
            (2, 3),
            (acc, after(stats, first_part[0])),
            True,
            weight=w_held,
            chunk=columns,
            span=(cut, cut),
            held=cut,
        )
        part = [first_part]
        part.append(project("project_1", order, 1, attended, out_weight, columns))
        third = project("project_3", order, 3, attended, out_weight, columns)
        rest = [attended[0], after(attended[1], third[0])]
        part += [project("project_2", order, 2, rest, out_weight, columns), third]
        come = [[None, None] for k in range(3)]
        for i in range(2):
            come[0][i] = lax.ppermute(part[0][i], "tensor", inward)
        part[1] = [part[1][0], after(part[1][1], come[0][0])]
        come[1] = [lax.ppermute(p, "tensor", inward) for p in part[1]]
        part[2] = [part[2][0], after(part[2][1], come[1][0])]
        come[2] = [lax.ppermute(p, "tensor", inward) for p in part[2]]
        done = None
        previous = part[1][0]
        for i in range(2):
            previous = added(f"add_0{i}", part[0][i], after(come[0][i], previous))
            across = lax.ppermute(previous, "tensor", middle)
            second = lax.ppermute(added(f"add_1{i}", part[1][i], come[1][i] if i == 0 else after(come[1][i], back)), "tensor", middle)
            back = lax.ppermute(added(f"add_3{i}", part[3][i], across), "tensor", outward)
            parts = [part[3][i], part[2][i], come[2][i], second, back]
            if i == 1:
                most = gathered("gather", flag, *parts[:2], *parts[3:])
                done = finish("finish_1", None, [most, after(come[2][1], most)], cut, rows, done)
            else:
                done = finish("finish_0", flag, parts, 0, rows, done)
        return done[0], done[1].T
    every = lax.all_gather(own, ("seq", "pipe"), axis=0)
    place = jnp.concatenate([jnp.stack([me, me]), jnp.arange(shards)]).astype(jnp.int32)
    state = None
    query = queries
    for shard in range(shards):
        state = attend(
            "attend", place, query, tables, [every[shard]], (shard,), state, shard == shards - 1
        )
        if shard == 0:
            query = state[2]
            state = state[:2]
    partial = [
        project(f"project_{k}", step, k, state[:1], out_weight, columns)[0] for k in range(lanes)
    ]
    total = lax.psum_scatter(jnp.stack(partial), "tensor", scatter_dimension=0, tiled=True)[0]
    values, scales = finish("finish", None, [total], 0, rows)
    return values, scales.T


def solution(mesh):
    return jax.shard_map(
        local,
        mesh=mesh,
        in_specs=(
            P(("groups", "seq", "pipe"), "tensor"),
            P(("groups", "seq", "pipe"), None),
            P(("groups", "seq", "pipe"), None),
            P(None, ("groups", "seq", "pipe"), None),
            P(None, ("groups", "seq", "pipe"), None),
            P(("groups", "seq", "pipe")),
            P("groups"),
            P("tensor", None),
        ),
        out_specs=(P(("groups", "seq", "pipe"), "tensor"), P(("groups", "seq", "pipe"), "tensor")),
        check_vma=False,
    )
```
